32 devices in a mesh: ctx: 8 (over z, x), hx: 4 (over y, core).
Axes of the slice: x: 2, y: 2, z: 4, core: 2. Of those that a mesh axis runs over, the one named last changes fastest.
Arguments:
- query_latent: bfloat16 [16, 128, 512], P(None, 'hx'), may hold values from -2 to 2
- query_rope: bfloat16 [16, 8192], P(None, 'hx'), may hold values from -80 to 80
- cache_latent: bfloat16 [4, 16384, 512], P(None, ('ctx', 'hx')), may hold values from -16 to 16
- cache_rope: bfloat16 [4, 64, 16384], P(None, None, ('ctx', 'hx')), may hold values from -8 to 8
- suffix_latent: bfloat16 [16, 4096, 512], P(None, ('ctx', 'hx')), may hold values from -16 to 16
- suffix_rope: bfloat16 [16, 64, 4096], P(None, None, ('ctx', 'hx')), may hold values from -6 to 6
- lengths: int32 [4], replicated, may hold values from 4096 to 16384, as said below
- parents: int32 [16], replicated, may hold values from 0 to 15, as said below
- w_uv: bfloat16 [512, 16384], P(None, ('ctx', 'hx')), may hold values from -1.25 to 1.25
- w_o: bfloat16 [16384, 7168], P(('ctx', 'hx')), may hold values from -0.046875 to 0.046875
- hidden: bfloat16 [16, 7168], replicated, may hold values from -6 to 6
- norm_gain: float32 [7168], replicated, may hold values from 0.1 to 1.9
- w_gate: bfloat16 [32768, 7168], P(('ctx', 'hx')), may hold values from -0.0625 to 0.0625
- w_up: bfloat16 [32768, 7168], P(('ctx', 'hx')), may hold values from -0.0625 to 0.0625
- w_down: bfloat16 [32768, 7168], P(('ctx', 'hx')), may hold values from -0.25 to 0.25
- expert_ids: int32 [16, 8], replicated, may hold values from 0 to 15, all different within a row
- gate_weights: float32 [16, 8], replicated, may hold values from 0.1 to 0.6
Outputs:
- attended: bfloat16 [16, 7168], replicated
- updated: bfloat16 [16, 7168], P(None, ('ctx', 'hx'))
The draws below stay inside these ranges and needn't reach their ends.
Inputs may be any that keep to these rules, and one draw needn't show every extreme that they name: `lengths`: one request has length 16384 and another 16384 // 4. parents[b] is a hypothesis of the same request as b. `expert_ids`: each row names 8 different experts.
All inputs are finite; a program needn't handle non-finite values.
Results may differ from the reference program's by a relative error of at most 0.012.
Values may be sent and summed in bfloat16 or wider, within the bound.
No kernel may reach another device: no remote copies, remote signals or barrier semaphores. Data moves between devices by JAX's collectives and lax.ppermute only.
A program may use at most 128 MiB of HBM per device.

```python
import math
import jax
import jax.numpy as jnp
from jax import lax

H = 128
DL = 512
DR = 64
DN = 128
DV = 128
D = 7168
EFF = 2048
TOP = 8
EXPERTS = 16
REQ = 4
BEAMS = 4
CTX_DEV = 512
SUF_DEV = 128
HYPS = 16
CTX = 16384
SUF = 4096
DEVICES = 32


def draw_cache_rope(key, part):
    key = jax.random.fold_in(key, 11)
    return jax.random.normal(key, (REQ, DR, CTX), jnp.float32).astype(jnp.bfloat16)


def draw_query_rope(key, part):
    key = jax.random.fold_in(key, 12)
    return jax.random.normal(key, (HYPS, H * DR), jnp.float32).astype(jnp.bfloat16)


def draw_query_latent(key, part):
    key = jax.random.fold_in(key, 13)
    return (0.18 * jax.random.normal(key, (HYPS, H, DL), jnp.float32)).astype(jnp.bfloat16)


def draw_lengths(key, part):
    key = jax.random.fold_in(key, 14)
    key_list = jax.random.split(key, 2)
    ranking = jax.random.permutation(key_list[0], REQ)
    middle = jax.random.randint(key_list[1], (REQ,), CTX // 4, CTX + 1)
    return jnp.where(ranking == 0, CTX, jnp.where(ranking == 1, CTX // 4, middle)).astype(jnp.int32)


def draw_parents(key, part):
    key = jax.random.fold_in(key, 15)
    key_list = jax.random.split(key, 2)
    offsets = jax.random.randint(key_list[0], (REQ, BEAMS), 0, BEAMS)
    slot_rank = jax.vmap(lambda single: jax.random.permutation(single, BEAMS))(jax.random.split(key_list[1], REQ))
    offsets = jnp.where(slot_rank == 0, 0, jnp.where(slot_rank == 1, BEAMS - 1, offsets))
    return (jnp.arange(REQ)[:, None] * BEAMS + offsets).reshape(HYPS).astype(jnp.int32)


def with_spikes(drawn, rng, source, target, shards_of, factor):
    owner, partner = [(jnp.arange(drawn.shape[dim]) // (drawn.shape[dim] // shards_of)).reshape([-1 if axis == dim else 1 for axis in range(drawn.ndim)]) for dim in (source, target)]
    chosen = jax.random.permutation(rng, shards_of)[partner]
    strong = (owner == chosen) | (owner == (partner + shards_of // 2) % shards_of)
    return jnp.where(strong, factor * drawn, drawn)


def block_levels(key, shape, shards, smallest, largest):
    level, own = 1.0, jax.random.fold_in(key, 6)
    for dim, blocks in shards:
        heights = jnp.exp(jax.random.uniform(jax.random.fold_in(own, dim), (blocks,), jnp.float32, smallest / len(shards), largest / len(shards)))
        level = level * jnp.repeat(heights, shape[dim] // blocks).reshape([-1 if axis == dim else 1 for axis in range(len(shape))])
    return level


def different_ones(stream_key, rows, count, top, lift):
    order = jax.random.permutation(jax.random.fold_in(stream_key, 1), count)
    favour = order
    for power in range(3):
        favour = favour * favour // count
    favour = favour * lift // count
    chance = jax.random.randint(jax.random.fold_in(stream_key, 2), (rows, count), 0, 4096) + favour
    fixed_rows = jax.random.permutation(jax.random.fold_in(stream_key, 3), rows)[jnp.arange(count) % rows]
    chance = jnp.where(jnp.arange(rows)[:, None] == fixed_rows[None, :], 1 << 14, chance)
    priority = chance * count + jnp.arange(count)
    return lax.top_k(priority.astype(jnp.int32), top)[1].astype(jnp.int32)


def bell_draw(key, dims, deviation, limit, cuts=(), kind=jnp.bfloat16):
    factor_of = block_levels(key, dims, cuts, -0.22, 0.18) if cuts else 1.0
    result = jax.random.normal(key, dims, jnp.float32) * deviation * factor_of
    return jnp.minimum(jnp.maximum(result, -limit), limit).astype(kind)


def bell_draw_with(rng, extent, spread, limit, cuts, heavy, kind=jnp.bfloat16):
    values = spread * jax.random.normal(rng, extent, jnp.float32)
    if cuts:
        values = values * block_levels(rng, extent, cuts, -0.22, 0.18)
    return jnp.clip(with_spikes(values, jax.random.fold_in(rng, 3), *heavy), -limit, limit).astype(kind)


def setup_inputs(seed: int = 0) -> dict:
    splits = jax.random.split(jax.random.key(seed), 18)
    return {
        "query_latent": draw_query_latent(jax.random.fold_in(splits[17], 71), 0),
        "query_rope": draw_query_rope(jax.random.fold_in(splits[17], 71), 0),
        "cache_latent": bell_draw(splits[2], (REQ, CTX, DL), 4.0, 16.0, ((1, 32),)),
        "cache_rope": draw_cache_rope(jax.random.fold_in(splits[17], 71), 0),
        "suffix_latent": bell_draw(splits[4], (HYPS, SUF, DL), 4.0, 16.0, ((1, 32),)),
        "suffix_rope": bell_draw(splits[5], (HYPS, DR, SUF), 1.0, 6.0, ((2, 32),)),
        "lengths": draw_lengths(jax.random.fold_in(splits[17], 71), 0),
        "parents": draw_parents(jax.random.fold_in(splits[17], 71), 0),
        "w_uv": bell_draw(splits[8], (DL, H * DV), 0.088, 1.25, ((1, 32),)),
        "w_o": bell_draw(splits[9], (H * DV, D), (H * DV) ** -0.5, 0.046875, ((0, 32),)),
        "hidden": bell_draw(splits[10], (HYPS, D), 1.0, 6.0),
        "norm_gain": jnp.clip(1.0 + 0.18 * jax.random.normal(splits[11], (D,), jnp.float32), 0.1, 1.9),
        "w_gate": bell_draw(splits[12], (EXPERTS * EFF, D), D ** -0.5, 0.0625, ((0, 32),)),
        "w_up": bell_draw(splits[13], (EXPERTS * EFF, D), D ** -0.5, 0.0625, ((0, 32),)),
        "w_down": bell_draw_with(splits[14], (EXPERTS * EFF, D), EFF ** -0.5, 0.25, ((0, 32),), (0, 1, 32, 2.75)),
        "expert_ids": different_ones(splits[15], HYPS, EXPERTS, TOP, 4096),
        "gate_weights": jnp.clip(jax.random.uniform(splits[16], (HYPS, TOP), jnp.float32, 0.1, 0.6), 0.1, 0.6),
    }


MSCALE = 1.0 + 0.1 * math.log(40.0)
NEG = -1e+30

def reference(query_latent, query_rope, cache_latent, cache_rope, suffix_latent, suffix_rope, lengths, parents, w_uv, w_o, hidden, norm_gain, w_gate, w_up, w_down, expert_ids, gate_weights):
    softmax_scale = MSCALE * MSCALE / math.sqrt(DN + DR)
    q_lat = query_latent.astype(jnp.float32)
    q_rope = query_rope.reshape(HYPS, H, DR).astype(jnp.float32)
    request_of = (jnp.arange(HYPS, dtype=jnp.int32) // BEAMS).astype(jnp.int32)
    hyp_length = lengths[request_of]

    def group_step(carry, group):
        run_max, run_sum, run_acc = carry
        pre_start = (group * CTX_DEV).astype(jnp.int32)
        suf_start = (group * SUF_DEV).astype(jnp.int32)
        pre_lat = lax.dynamic_slice_in_dim(cache_latent, pre_start, CTX_DEV, 1)[request_of].astype(jnp.float32)
        pre_rope = lax.dynamic_slice_in_dim(cache_rope, pre_start, CTX_DEV, 2)[request_of].astype(jnp.float32)
        suf_lat = lax.dynamic_slice_in_dim(suffix_latent, suf_start, SUF_DEV, 1)[parents].astype(jnp.float32)
        suf_rope = lax.dynamic_slice_in_dim(suffix_rope, suf_start, SUF_DEV, 2)[parents].astype(jnp.float32)
        keys_lat = jnp.concatenate([pre_lat, suf_lat], axis=1)
        keys_rope = jnp.concatenate([pre_rope, suf_rope], axis=2)
        scores = jnp.einsum('bhl,bsl->bhs', q_lat, keys_lat) + jnp.einsum('bhr,brs->bhs', q_rope, keys_rope)
        scores = scores * softmax_scale
        position = pre_start + jnp.arange(CTX_DEV, dtype=jnp.int32)
        pre_live = position[None, :] < hyp_length[:, None]
        is_live = jnp.concatenate([pre_live, jnp.ones((HYPS, SUF_DEV), dtype=bool)], axis=1)
        scores = jnp.where(is_live[:, None, :], scores, NEG)
        local_max = lax.optimization_barrier(jnp.max(scores, axis=2))
        weights = jnp.exp(scores - local_max[:, :, None]).astype(jnp.bfloat16).astype(jnp.float32)
        weight_sum = lax.optimization_barrier(jnp.sum(weights, axis=2))
        weighted = jnp.einsum('bhs,bsl->bhl', weights, keys_lat)
        new_max = jnp.maximum(run_max, local_max)
        old_factor = jnp.exp(run_max - new_max)
        new_factor = jnp.exp(local_max - new_max)
        run_sum = run_sum * old_factor + weight_sum * new_factor
        run_acc = run_acc * old_factor[:, :, None] + weighted * new_factor[:, :, None]
        return ((new_max, run_sum, run_acc), None)
    start_carry = (jnp.full((HYPS, H), NEG, jnp.float32), jnp.zeros((HYPS, H), jnp.float32), jnp.zeros((HYPS, H, DL), jnp.float32))
    (run_max, run_sum, run_acc), unused = lax.scan(group_step, start_carry, jnp.arange(DEVICES, dtype=jnp.int32))
    attention = (run_acc / run_sum[:, :, None]).astype(jnp.bfloat16)
    value_map = w_uv.astype(jnp.float32).reshape(DL, H, DV)
    values = jnp.einsum('bhl,lhd->bhd', attention.astype(jnp.float32), value_map)
    values = values.astype(jnp.bfloat16).reshape(HYPS, H * DV)
    attended = jnp.dot(values, w_o, preferred_element_type=jnp.float32).astype(jnp.bfloat16)
    residual = hidden.astype(jnp.float32) + attended.astype(jnp.float32)
    mean_square = lax.optimization_barrier(jnp.mean(residual * residual, axis=1, keepdims=True))
    normed = (residual * lax.rsqrt(mean_square + 1e-06) * norm_gain).astype(jnp.bfloat16)

    def expert_step(moe_sum, expert):
        first_row = (expert * EFF).astype(jnp.int32)
        gate_rows = lax.dynamic_slice_in_dim(w_gate, first_row, EFF, 0)
        up_rows = lax.dynamic_slice_in_dim(w_up, first_row, EFF, 0)
        down_rows = lax.dynamic_slice_in_dim(w_down, first_row, EFF, 0)
        routed = lax.optimization_barrier(jnp.sum(gate_weights * (expert_ids == expert).astype(jnp.float32), axis=1))
        gate_out = jnp.dot(normed, gate_rows.T, preferred_element_type=jnp.float32)
        up_out = jnp.dot(normed, up_rows.T, preferred_element_type=jnp.float32)
        activated = (jax.nn.silu(gate_out) * up_out * routed[:, None]).astype(jnp.bfloat16)
        return (moe_sum + jnp.dot(activated, down_rows, preferred_element_type=jnp.float32), None)
    moe_sum, unused = lax.scan(expert_step, jnp.zeros((HYPS, D), jnp.float32), jnp.arange(EXPERTS, dtype=jnp.int32))
    updated = (residual + moe_sum).astype(jnp.bfloat16)
    return (attended, updated)
```

```python
from functools import partial
import math

import jax
import jax.numpy as jnp
from jax import lax
from jax.experimental import pallas as pl
from jax.experimental.pallas import tpu as pltpu
from jax.sharding import PartitionSpec as P

DL = 512
DR = 64
DN = 128
DV = 128
EFF = 2048
REQ = 4
BEAMS = 4
HYPS = 16


MSCALE = 1.0 + 0.1 * math.log(40.0)
NEG = -1e30


def merged(value, axis, join):
    pieces = jax.tree.map(lambda part: lax.all_gather(part, axis), value)
    head = jax.tree.map(lambda part: part[0], pieces)
    tail = jax.tree.map(lambda part: part[1:], pieces)
    subtotal, _ = lax.scan(lambda subtotal, section: (join(subtotal, section), None), head, tail)
    return subtotal


def merge_pair(first_set, second_set):
    max_a, sum_a, acc_a = first_set
    max_b, sum_b, acc_b = second_set
    new_max = jnp.maximum(max_a, max_b)
    factor_a = jnp.exp(max_a - new_max)
    factor_b = jnp.exp(max_b - new_max)
    return (
        new_max,
        sum_a * factor_a + sum_b * factor_b,
        acc_a * factor_a[..., None] + acc_b * factor_b[..., None],
    )


def request_stats(
    q_lat, q_rope, pre_lat, pre_rope, suf_lat, suf_rope, is_live, softmax_scale, with_prefix
):
    suf_scores = jnp.einsum("bhl,bsl->bhs", q_lat, suf_lat, preferred_element_type=jnp.float32)
    suf_scores = (
        suf_scores
        + jnp.einsum("bhr,brs->bhs", q_rope, suf_rope, preferred_element_type=jnp.float32)
    ) * softmax_scale
    row_max = jnp.max(suf_scores, axis=2)
    beam_count, head_count, lat_width = q_lat.shape
    flat_lat = q_lat.reshape(beam_count * head_count, lat_width)
    flat_rope = q_rope.reshape(beam_count * head_count, q_rope.shape[2])
    pre_scores = lax.dot_general(
        flat_lat, pre_lat, (((1,), (1,)), ((), ())), preferred_element_type=jnp.float32
    )
    pre_scores = pre_scores + jnp.dot(flat_rope, pre_rope, preferred_element_type=jnp.float32)
    pre_scores = jnp.where(is_live[None, :], pre_scores * softmax_scale, NEG).reshape(
        beam_count, head_count, -1
    )
    row_max = jnp.maximum(row_max, jnp.max(pre_scores, axis=2))
    suf_weights = jnp.exp(suf_scores - row_max[..., None]).astype(jnp.bfloat16)
    weight_sum = jnp.sum(suf_weights.astype(jnp.float32), axis=2)
    weighted = jnp.einsum("bhs,bsl->bhl", suf_weights, suf_lat, preferred_element_type=jnp.float32)
    pre_weights = jnp.exp(pre_scores - row_max[..., None]).astype(jnp.bfloat16)
    weight_sum = weight_sum + jnp.sum(pre_weights.astype(jnp.float32), axis=2)
    prefix_part = jnp.dot(
        pre_weights.reshape(beam_count * head_count, -1),
        pre_lat,
        preferred_element_type=jnp.float32,
    )
    weighted = weighted + prefix_part.reshape(beam_count, head_count, lat_width)
    return (row_max, weight_sum, weighted)


def general_local(
    query_latent,
    query_rope,
    cache_latent,
    cache_rope,
    suffix_latent,
    suffix_rope,
    lengths,
    parents,
    w_uv,
    w_o,
    hidden,
    norm_gain,
    w_gate,
    w_up,
    w_down,
    expert_ids,
    gate_weights,
):
    q_lat, q_rope = (
        lax.all_gather(query_latent, "hx", axis=1, tiled=True),
        lax.all_gather(query_rope, "hx", axis=1, tiled=True),
    )
    head_count = q_lat.shape[1]
    q_rope = q_rope.reshape(HYPS, head_count, DR)
    softmax_scale = MSCALE * MSCALE / math.sqrt(DN + DR)
    n_hx = lax.axis_size("hx")
    linear = lax.axis_index("ctx") * n_hx + lax.axis_index("hx")
    ctx_block = cache_latent.shape[1]
    offsets = linear * ctx_block + jnp.arange(ctx_block, dtype=jnp.int32)
    suf_lat = jnp.take(suffix_latent, parents, axis=0)
    suf_rope = jnp.take(suffix_rope, parents, axis=0)
    maxima = []
    totals_list = []
    sums_list = []
    for request in range(REQ):
        hyp_rows = slice(request * BEAMS, (request + 1) * BEAMS)
        is_live = offsets < lengths[request]
        bound_stats = partial(
            request_stats,
            q_lat[hyp_rows],
            q_rope[hyp_rows],
            cache_latent[request],
            cache_rope[request],
            suf_lat[hyp_rows],
            suf_rope[hyp_rows],
            is_live,
            softmax_scale,
        )
        request_sums = bound_stats(True)
        maxima.append(request_sums[0])
        totals_list.append(request_sums[1])
        sums_list.append(request_sums[2])
    row_max = jnp.concatenate(maxima, axis=0)
    weight_sum = jnp.concatenate(totals_list, axis=0)
    weighted = jnp.concatenate(sums_list, axis=0)
    part_max, part_sum, part_acc = (
        lax.all_to_all(row_max[None], "ctx", split_axis=2, concat_axis=0, tiled=True),
        lax.all_to_all(weight_sum[None], "ctx", split_axis=2, concat_axis=0, tiled=True),
        lax.all_to_all(weighted[None], "ctx", split_axis=2, concat_axis=0, tiled=True),
    )
    group_max = jnp.max(part_max, axis=0)
    factor = jnp.exp(part_max - group_max[None])
    group_sum = jnp.sum(part_sum * factor, axis=0)
    group_acc = jnp.sum(part_acc * factor[..., None], axis=0)
    group_max, group_sum, group_acc = merged((group_max, group_sum, group_acc), "hx", merge_pair)
    attention = (group_acc / group_sum[..., None]).astype(jnp.bfloat16)
    columns = w_uv.shape[1]
    head_span = max(1, columns // DV)
    first_head = lax.axis_index("hx") * columns // DV
    chosen = lax.dynamic_slice_in_dim(attention, first_head, head_span, 1)
    value_map = w_uv.reshape(DL, head_span, columns // head_span)
    values = jnp.einsum("bnl,lnc->bnc", chosen, value_map, preferred_element_type=jnp.float32)
    values = values.astype(jnp.bfloat16).reshape(HYPS, columns)
    partial_out = jnp.dot(values, w_o, preferred_element_type=jnp.float32)
    attended = lax.psum(partial_out, ("ctx", "hx")).astype(jnp.bfloat16)
    residual = hidden.astype(jnp.float32) + attended.astype(jnp.float32)
    mean_square = jnp.mean(residual * residual, axis=1, keepdims=True)
    normed = (residual * lax.rsqrt(mean_square + 1e-06) * norm_gain).astype(jnp.bfloat16)
    unit_count = w_gate.shape[0]
    expert_here = linear * unit_count // EFF
    routed = jnp.sum(gate_weights * (expert_ids == expert_here).astype(jnp.float32), axis=1)
    gate_out = lax.dot_general(
        normed, w_gate, (((1,), (1,)), ((), ())), preferred_element_type=jnp.float32
    )
    up_out = lax.dot_general(
        normed, w_up, (((1,), (1,)), ((), ())), preferred_element_type=jnp.float32
    )
    activated = (jax.nn.silu(gate_out) * up_out * routed[:, None]).astype(jnp.bfloat16)
    expert_terms = jnp.dot(activated, w_down, preferred_element_type=jnp.float32)
    moe_share = lax.psum_scatter(expert_terms, ("ctx", "hx"), scatter_dimension=1, tiled=True)
    share_width = moe_share.shape[1]
    residual_share = lax.dynamic_slice_in_dim(residual, linear * share_width, share_width, 1)
    updated = (residual_share + moe_share).astype(jnp.bfloat16)
    return (attended, updated)


BF = jnp.bfloat16
F32 = jnp.float32
AXES = ("z", "x", "y", "core")
SHAPE = (4, 2, 2, 2)
HEADS_DEV = 4
UNITS = 256
STAT = 16
LANES = 128
LENGTHS = 2
PARENTS = LENGTHS + REQ
VMEM = pl.BlockSpec(memory_space=pltpu.VMEM)
SMEM = pl.BlockSpec(memory_space=pltpu.SMEM)
HBM = pl.BlockSpec(memory_space=pltpu.HBM)
ANY = pl.BlockSpec(memory_space=pl.ANY)
NT = (((1,), (1,)), ((), ()))


def swap(value, mask, count):
    return lax.ppermute(value, AXES, [(i, i ^ mask) for i in range(count)])


def swaps(values, masks, count):
    return [swap(value, mask, count) for value, mask in zip(values, masks)]


def in_hbm(value):
    return pltpu.with_memory_space_constraint(value, pltpu.HBM)


def column(lane_row):
    n = lane_row.shape[1]
    at = lax.broadcasted_iota(jnp.int32, (n, n), 0)
    to = lax.broadcasted_iota(jnp.int32, (n, n), 1)
    return jnp.sum(jnp.where(at == to, lane_row, 0.0), axis=1, keepdims=True)


def write_stat(stat, row, lse):
    k, n = lse.shape
    for i in range(3):
        part = lse.astype(BF).astype(F32)
        stat[row:row + k, i * LANES:i * LANES + n] = part
        lse = lse - part


def read_stat(block, n):
    block = block.astype(F32)
    return (block[:REQ, :n] + block[:REQ, LANES:LANES + n]) + block[:REQ, 2 * LANES:2 * LANES + n]


def joined(lses):
    top = lses[0]
    for lse in lses[1:]:
        top = jnp.maximum(top, lse)
    weights = [jnp.exp(lse - top) for lse in lses]
    total = sum(weights[1:], weights[0])
    return [w / total for w in weights], top + jnp.log(total)


def attend_kernel(scale, fetch, info, ql0, ql1, qr0, qr1, cl_hbm, cr_hbm, sl_hbm, sr_hbm,
                  keep, send, spread, qbuf, rbuf, pbuf, stat, cl, cr, sl, sr, own_q, sems):
    linear = info[0]
    core, y, x, z0 = (info[0] >> k & 1 for k in range(4))
    heads = ql1.shape[1]
    rows = 2 * heads
    total_rows = BEAMS * rows
    half = total_rows // 2
    targets = keep.shape[0]
    block = half // targets
    copies = []
    for r in range(REQ):
        beams = pl.ds(r * BEAMS, BEAMS)
        group = [
            pltpu.make_async_copy(cl_hbm.at[r], cl.at[r], sems.at[0, r]),
            pltpu.make_async_copy(cr_hbm.at[r], cr.at[r], sems.at[1, r]),
            pltpu.make_async_copy(sl_hbm.at[beams], sl.at[beams], sems.at[2, r]),
            pltpu.make_async_copy(sr_hbm.at[beams], sr.at[beams], sems.at[3, r]),
        ]
        if fetch:
            group.append(pltpu.make_async_copy(ql0.at[beams], own_q.at[beams], sems.at[4, r]))
        for copy in group:
            copy.start()
        copies.append(group)
    first_q = own_q if fetch else ql0

    out_row = lax.broadcasted_iota(jnp.int32, (total_rows, total_rows), 0)
    in_row = lax.broadcasted_iota(jnp.int32, (total_rows, total_rows), 1)

    def source_of(row):
        bit = lambda k: (row >> k) & 1
        beam, head = (row >> 2) & 3, row & 3
        target = (bit(6) ^ x) * 4 + (bit(5) ^ y) * 2 + (bit(7) ^ core)
        return beam * rows + (bit(4) ^ core ^ z0) * heads + target * HEADS_DEV + head

    spread[...] = jnp.where(source_of(out_row) == in_row, 1.0, 0.0).astype(BF)
    moves = source_of(in_row) == out_row
    stat[...] = jnp.zeros_like(stat)

    for r in range(REQ):
        for copy in copies[r]:
            copy.wait()
        for j in range(BEAMS):
            b = r * BEAMS + j
            qbuf[j * rows:j * rows + heads] = first_q[b]
            qbuf[j * rows + heads:(j + 1) * rows] = ql1[b]
            rbuf[j * rows:j * rows + heads] = qr0[b]
            rbuf[j * rows + heads:(j + 1) * rows] = qr1[b]
        keys = cl[r]
        ctx_block = keys.shape[0]
        pre = lax.dot_general(qbuf[...], keys, NT, preferred_element_type=F32)
        pre = pre + jnp.dot(rbuf[...], cr[r], preferred_element_type=F32)
        position = linear * ctx_block + lax.broadcasted_iota(jnp.int32, (1, ctx_block), 1)
        pre = jnp.where(position < info[LENGTHS + r], pre * scale, NEG)
        own = [info[PARENTS + r * BEAMS + j] for j in range(BEAMS)]
        suf = []
        for j in range(BEAMS):
            part = slice(j * rows, (j + 1) * rows)
            s = lax.dot_general(qbuf[part], sl[own[j]], NT, preferred_element_type=F32)
            s = s + jnp.dot(rbuf[part], sr[own[j]], preferred_element_type=F32)
            suf.append(s * scale)
        suf = jnp.concatenate(suf, axis=0)
        top = jnp.maximum(jnp.max(pre, axis=1, keepdims=True), jnp.max(suf, axis=1, keepdims=True))
        pre_w = jnp.exp(pre - top).astype(BF)
        suf_w = jnp.exp(suf - top).astype(BF)
        total = jnp.sum(pre_w.astype(F32), axis=1, keepdims=True)
        total = total + jnp.sum(suf_w.astype(F32), axis=1, keepdims=True)
        acc = jnp.dot(pre_w, keys, preferred_element_type=F32)
        inv = 1.0 / total
        for j in range(BEAMS):
            part = slice(j * rows, (j + 1) * rows)
            a = acc[part] + jnp.dot(suf_w[part], sl[own[j]], preferred_element_type=F32)
            pbuf[part] = (a * inv[part]).astype(BF)
        moved = jnp.dot(spread[...], pbuf[...], preferred_element_type=F32).astype(BF)
        lse = top + jnp.log(total)
        lane_lse = jnp.sum(jnp.where(moves, lse, 0.0), axis=0, keepdims=True)
        for t in range(targets):
            for i, out in enumerate((keep, send)):
                at = i * half + t * block
                out[t, r * block:(r + 1) * block] = moved[at:at + block]
                write_stat(stat.at[i * targets + t], r, lane_lse[:, at:at + block])
    for t in range(targets):
        keep[t, REQ * block:] = stat[t].astype(BF)
        send[t, REQ * block:] = stat[targets + t].astype(BF)


def attend(scale, fetch, info, q_lat, q_rope, caches):
    heads, width = q_lat[0].shape[1:]
    rope = q_rope[0].shape[2]
    total_rows = BEAMS * 2 * heads
    targets = SHAPE[1] * SHAPE[2]
    message = jax.ShapeDtypeStruct((targets, REQ * total_rows // (2 * targets) + STAT, width), BF)
    keys = caches[0].shape[1] + caches[2].shape[1]
    own_q = q_lat[0].shape if fetch else (8, LANES)
    return pl.pallas_call(
        partial(attend_kernel, scale, fetch),
        in_specs=[SMEM, HBM if fetch else VMEM] + [VMEM] * 3 + [HBM] * 4,
        out_specs=[VMEM] * 2,
        out_shape=[message] * 2,
        scratch_shapes=[
            pltpu.VMEM((total_rows, total_rows), BF),
            pltpu.VMEM((total_rows, width), BF),
            pltpu.VMEM((total_rows, rope), BF),
            pltpu.VMEM((total_rows, width), BF),
            pltpu.VMEM((2 * targets, STAT, width), F32),
        ] + [pltpu.VMEM(c.shape, BF) for c in caches]
        + [pltpu.VMEM(own_q, BF), pltpu.SemaphoreType.DMA((5, REQ))],
        compiler_params=pltpu.CompilerParams(vmem_limit_bytes=20 << 20),
        cost_estimate=pl.CostEstimate(
            flops=REQ * 2 * total_rows * keys * (2 * width + rope), bytes_accessed=8 << 20,
            transcendentals=REQ * total_rows * keys),
        name="attend",
    )(info, in_hbm(q_lat[0]) if fetch else q_lat[0], q_lat[1], *q_rope, *(in_hbm(c) for c in caches))


def pair_kernel(a, b, *rest):
    outs, stat = rest[:-1], rest[-1]
    targets, rows, _ = a.shape
    body = rows - STAT
    block = body // REQ
    for t, out in enumerate(outs):
        weights, lse = joined([read_stat(v[t, body:], block) for v in (a, b)])
        for r in range(REQ):
            part = slice(r * block, (r + 1) * block)
            out[part] = (a[t, part].astype(F32) * column(weights[0][r:r + 1])
                         + b[t, part].astype(F32) * column(weights[1][r:r + 1])).astype(BF)
        stat[...] = jnp.zeros_like(stat)
        write_stat(stat, 0, lse)
        out[body:] = stat[...].astype(BF)


def merge_pair_of(a, b):
    targets = a.shape[0]
    return pl.pallas_call(
        pair_kernel,
        in_specs=[VMEM] * 2,
        out_specs=[VMEM] * targets,
        out_shape=[jax.ShapeDtypeStruct(a.shape[1:], BF)] * targets,
        scratch_shapes=[pltpu.VMEM((STAT, a.shape[2]), F32)],
        compiler_params=pltpu.CompilerParams(vmem_limit_bytes=4 << 20),
        cost_estimate=pl.CostEstimate(flops=4 * a.size, bytes_accessed=6 * a.size, transcendentals=0),
        name="merge_pair",
    )(a, b)


def plane_kernel(count, info, *refs):
    near, far = refs[:4], refs[4:8]
    outs, (stat, held) = refs[8 + count:-2], refs[-2:]
    body = near[0].shape[0] - STAT
    block = body // REQ
    small = block // 2
    y, z1 = info[0] >> 1 & 1, info[0] >> 4 & 1
    for other in range(2):
        sources = [near[2 * x + other] for x in range(2)] + [far[2 * x + 1 - other] for x in range(2)]
        weights, lse = joined([read_stat(ref[body:], block) for ref in sources])
        for z0 in range(2):
            for r in range(REQ):
                part = slice(r * block + z0 * small, r * block + (z0 + 1) * small)
                total = None
                for ref, w in zip(sources, weights):
                    term = ref[part].astype(F32) * column(w[r:r + 1, z0 * small:(z0 + 1) * small])
                    total = term if total is None else total + term
                held[2 * other + z0, r * small:(r + 1) * small] = total.astype(BF)
            stat[...] = jnp.zeros_like(stat)
            write_stat(stat, 0, lse[:, z0 * small:(z0 + 1) * small])
            held[2 * other + z0, REQ * small:] = stat[...].astype(BF)
    for d, out in enumerate(outs):
        out[...] = held[2 * ((d >> 1) ^ y ^ z1) + (d & 1)]


def merge_plane(info, near, far, needs):
    rows, width = near[0].shape
    shape = ((rows - STAT) // 2 + STAT, width)
    return pl.pallas_call(
        partial(plane_kernel, len(needs)),
        in_specs=[SMEM] + [VMEM] * 8 + [ANY] * len(needs),
        out_specs=[VMEM] * SHAPE[0],
        out_shape=[jax.ShapeDtypeStruct(shape, BF)] * SHAPE[0],
        scratch_shapes=[pltpu.VMEM((STAT, width), F32), pltpu.VMEM((SHAPE[0], *shape), BF)],
        compiler_params=pltpu.CompilerParams(vmem_limit_bytes=4 << 20),
        cost_estimate=pl.CostEstimate(flops=16 * rows * width, bytes_accessed=24 * rows * width, transcendentals=0),
        name="merge_plane",
    )(info, *near, *far, *needs)


def sum_kernel(count, split, needs, dtype, *refs):
    ins, outs = refs[:count], refs[count + needs:]
    for t, out in enumerate(outs):
        terms = [(ref[t] if split else ref[...]).astype(F32) for ref in ins]
        while len(terms) > 1:
            terms = [terms[i] + terms[i + 1] for i in range(0, len(terms) - 1, 2)] + terms[len(terms) & ~1:]
        out[...] = terms[0].astype(dtype)


def sums(arrays, split=False, needs=()):
    count = len(arrays)
    shape = arrays[0].shape
    outs = shape[0] if split else 1
    shape = shape[1:] if split else shape
    return pl.pallas_call(
        partial(sum_kernel, count, split, len(needs), BF),
        in_specs=[VMEM] * count + [ANY] * len(needs),
        out_specs=[VMEM] * outs,
        out_shape=[jax.ShapeDtypeStruct(shape, BF)] * outs,
        compiler_params=pltpu.CompilerParams(vmem_limit_bytes=4 << 20),
        cost_estimate=pl.CostEstimate(flops=count * arrays[0].size, bytes_accessed=4 * count * arrays[0].size,
                                      transcendentals=0),
        name="sums",
    )(*arrays, *needs)


def load_kernel(count, parts, which, *refs):
    sources, dests, sems = refs[:count], refs[count + 1:-1], refs[-1]
    copies = []
    for i in range(count):
        rows = dests[i].shape[0]
        copies.append(pltpu.make_async_copy(sources[i].at[pl.ds(which * rows, rows)], dests[i], sems.at[i]))
    for copy in copies:
        copy.start()
    for copy in copies:
        copy.wait()


def load(after, *arrays, parts=1, which=0):
    count = len(arrays)
    return pl.pallas_call(
        partial(load_kernel, count, parts, which),
        in_specs=[HBM] * count + [ANY],
        out_specs=[VMEM] * count,
        out_shape=[pltpu.VMEM((a.shape[0] // parts, *a.shape[1:]), a.dtype) for a in arrays],
        scratch_shapes=[pltpu.SemaphoreType.DMA((count,))],
        compiler_params=pltpu.CompilerParams(vmem_limit_bytes=1 << 20),
        cost_estimate=pl.CostEstimate(
            flops=0, bytes_accessed=sum(2 * a.size for a in arrays) // parts, transcendentals=0),
        name="load",
    )(*(in_hbm(a) for a in arrays), after)


def project_kernel(info, p0, p1, p2, p3, w_uv, w_o, *rest):
    keep, send = rest[-2:]
    parts = (p0, p1, p2, p3)
    rows, _ = p0.shape
    body = rows - STAT
    block = body // REQ
    weights, _ = joined([read_stat(p[body:], block) for p in parts])
    sums = []
    for r in range(REQ):
        total = None
        for p, w in zip(parts, weights):
            term = p[r * block:(r + 1) * block].astype(F32) * column(w[r:r + 1])
            total = term if total is None else total + term
        sums.append(total)
    attention = jnp.concatenate(sums, axis=0).astype(BF)
    full = jnp.dot(attention, w_uv[...], preferred_element_type=F32)
    rows, columns = full.shape
    row = lax.broadcasted_iota(jnp.int32, (rows, columns), 0)
    lane = lax.broadcasted_iota(jnp.int32, (rows, columns), 1)
    own = jnp.where((row & (HEADS_DEV - 1)) == lane // DV, full, 0.0).astype(BF)
    pick_hyp = lax.broadcasted_iota(jnp.int32, (HYPS, rows), 0)
    pick_row = lax.broadcasted_iota(jnp.int32, (HYPS, rows), 1)
    pick = jnp.where(pick_row // HEADS_DEV == pick_hyp, 1.0, 0.0).astype(BF)
    values = jnp.dot(pick, own, preferred_element_type=F32).astype(BF)
    width = keep.shape[2]
    plane = info[0] & 7
    for there, out in enumerate((keep, send)):
        for t in range(out.shape[0]):
            at = pl.multiple_of((plane ^ (2 * t + there)) * width, LANES)
            piece = jnp.dot(values, w_o[:, pl.ds(at, width)], preferred_element_type=F32)
            out[t] = piece.astype(BF)


def project(info, parts, w_uv, w_o, needs):
    squares = SHAPE[1] * SHAPE[2]
    out = jax.ShapeDtypeStruct((squares, HYPS, w_o.shape[1] // (2 * squares)), BF)
    return pl.pallas_call(
        project_kernel,
        in_specs=[SMEM] + [VMEM] * 6 + [ANY] * len(needs),
        out_specs=[VMEM] * 2,
        out_shape=[out] * 2,
        compiler_params=pltpu.CompilerParams(vmem_limit_bytes=6 << 20),
        cost_estimate=pl.CostEstimate(flops=2 * HYPS * w_o.size, bytes_accessed=2 * w_o.size, transcendentals=0),
        name="project",
    )(info, *parts, w_uv, w_o, *needs)


def experts_kernel(info, *refs):
    shares = refs[:8]
    hidden, gain, ids, gates, w_gate, w_up = refs[8:14]
    w_down, outs = refs[14:-8], refs[-8:]
    attended, keep, send, residual, x_buf, acc, x_held, held = outs
    linear = info[0]
    plane, depth = linear & 7, linear >> 3
    units = w_gate.shape[0]
    share = shares[0].shape[1]
    for d, ref in enumerate(shares):
        at = pl.multiple_of((plane ^ d) * share, LANES)
        x_buf[:, pl.ds(at, share)] = ref[...].astype(F32)
        attended[:, pl.ds(at, share)] = ref[...]
    x = x_buf[...] + hidden[...].astype(F32)
    mean_square = jnp.mean(x * x, axis=1, keepdims=True)
    normed = (x * lax.rsqrt(mean_square + 1e-06) * gain[...]).astype(BF)
    routed = jnp.sum(jnp.where(ids[...] == info[1], gates[...], 0.0), axis=1, keepdims=True)
    for k in range(units // UNITS):
        part = slice(k * UNITS, (k + 1) * UNITS)
        gate = lax.dot_general(normed, w_gate[part], NT, preferred_element_type=F32)
        up = lax.dot_general(normed, w_up[part], NT, preferred_element_type=F32)
        act = (gate / (1.0 + jnp.exp(-gate)) * up * routed).astype(BF)
        piece, row = divmod(k * UNITS, w_down[0].shape[0])
        term = jnp.dot(act, w_down[piece][row:row + UNITS], preferred_element_type=F32)
        if k == 0:
            acc[...] = term
        else:
            acc[...] += term
    count, _, width = held.shape
    for d in range(count):
        x_held[d] = x[:, d * width:(d + 1) * width]
        held[d] = acc[:, d * width:(d + 1) * width].astype(BF)
    residual[...] = x_held[linear]
    for there, out in enumerate((keep, send)):
        for t in range(out.shape[0]):
            for z in range(out.shape[1]):
                out[t, z] = held[((depth ^ z) << 3) + (plane ^ (2 * t + there))]


def experts(info, shares, hidden, gain, ids, gates, w_gate, w_up, *w_down):
    units, width = w_gate.shape
    squares = SHAPE[1] * SHAPE[2]
    small = width // (2 * squares * SHAPE[0])
    terms = jax.ShapeDtypeStruct((squares, SHAPE[0], HYPS, small), BF)
    return pl.pallas_call(
        experts_kernel,
        in_specs=[SMEM] + [VMEM] * (14 + len(w_down)),
        out_specs=[VMEM] * 4,
        out_shape=[
            jax.ShapeDtypeStruct((HYPS, width), BF), terms, terms,
            jax.ShapeDtypeStruct((HYPS, small), F32),
        ],
        scratch_shapes=[pltpu.VMEM((HYPS, width), F32)] * 2 + [
            pltpu.VMEM((2 * squares * SHAPE[0], HYPS, small), F32),
            pltpu.VMEM((2 * squares * SHAPE[0], HYPS, small), BF),
        ],
        compiler_params=pltpu.CompilerParams(vmem_limit_bytes=6 << 20),
        cost_estimate=pl.CostEstimate(flops=6 * HYPS * units * width, bytes_accessed=6 * units * width,
                                      transcendentals=HYPS * units),
        name="experts",
    )(info, *shares, hidden, gain, ids, gates, w_gate, w_up, *w_down)


def local(
    query_latent,
    query_rope,
    cache_latent,
    cache_rope,
    suffix_latent,
    suffix_rope,
    lengths,
    parents,
    w_uv,
    w_o,
    hidden,
    norm_gain,
    w_gate,
    w_up,
    w_down,
    expert_ids,
    gate_weights,
):
    count = math.prod(SHAPE)
    linear = lax.axis_index(AXES)
    scale = MSCALE * MSCALE / math.sqrt(DN + DR)
    info = jnp.concatenate([jnp.stack([linear, linear * w_gate.shape[0] // EFF]).astype(jnp.int32), lengths, parents])
    caches = (cache_latent, cache_rope, suffix_latent, suffix_rope)
    square, line = (2, 4, 6), (8, 16, 24)

    rope = query_rope.reshape(HYPS, query_latent.shape[1], DR)
    far_lat, far_rope = swap(query_latent, 2, count), swap(rope, 2, count)
    near_lat, near_rope = swap(query_latent, 1, count), swap(rope, 1, count)
    near_keep, near_send = attend(scale, True, info, (query_latent, near_lat), (rope, near_rope), caches)
    far_lat, far_rope, near_send = lax.optimization_barrier((far_lat, far_rope, near_send))
    far_lat, far_rope = (far_lat, swap(far_lat, 1, count)), (far_rope, swap(far_rope, 1, count))
    near = merge_pair_of(near_keep, swap(near_send, 1, count))
    near = [near[0], *swaps(near[1:], square, count)]
    far_keep, far_send = attend(scale, False, info, far_lat, far_rope, caches)
    far = merge_pair_of(far_keep, swap(far_send, 1, count))
    w_gate, = load(far[0], w_gate)
    far = [far[0], *swaps(far[1:], square, count)]
    parts = merge_plane(info, near, far, (w_gate,))
    w_uv, w_o, w_up = load(parts[0], w_uv, w_o, w_up)
    parts = [parts[0], *swaps(parts[1:], line, count)]
    keep, send = project(info, parts, w_uv, w_o, (w_up,))

    pieces = sums([keep, swap(send, 1, count)], split=True)
    down0, = load(pieces[0], w_down, parts=2, which=0)
    part, = sums([pieces[0], *swaps(pieces[1:], square, count)], needs=(down0,))
    down1, = load(part, w_down, parts=2, which=1)
    share, = sums([part, *swaps([part] * 3, line, count)], needs=(down1,))
    same_core = [share, *swaps([share] * 3, square, count)]
    other_core = [swap(v, 1, count) for v in same_core]
    shares = [v for pair in zip(same_core, other_core) for v in pair]
    attended, keep, send, residual = experts(
        info, shares, hidden, norm_gain.reshape(1, -1), expert_ids, gate_weights, w_gate, w_up, down0, down1)

    pieces = sums([keep, swap(send, 1, count)], split=True)
    parts = sums([pieces[0], *swaps(pieces[1:], square, count)], split=True)
    total = sum(v.astype(F32) for v in (parts[0], *swaps(parts[1:], line, count)))
    updated = (residual + total).astype(BF)
    return (attended, updated)


def solution(mesh):
    if mesh.shape["ctx"] == SHAPE[0] * SHAPE[1] and mesh.shape["hx"] == SHAPE[2] * SHAPE[3]:
        chosen, names = local, AXES
        mesh = jax.sharding.Mesh(mesh.devices.reshape(SHAPE), AXES)
    else:
        chosen, names = general_local, ("ctx", "hx")
    all_axes, hx = names, names[len(names) // 2:]
    in_specs = (
        P(None, hx, None),
        P(None, hx),
        P(None, all_axes, None),
        P(None, None, all_axes),
        P(None, all_axes, None),
        P(None, None, all_axes),
        P(),
        P(),
        P(None, all_axes),
        P(all_axes, None),
        P(),
        P(),
        P(all_axes, None),
        P(all_axes, None),
        P(all_axes, None),
        P(),
        P(),
    )
    out_specs = (P(), P(None, all_axes))
    return jax.shard_map(chosen, mesh=mesh, in_specs=in_specs, out_specs=out_specs, check_vma=False)
```

```python
from functools import partial
import math

import jax
import jax.numpy as jnp
from jax import lax
from jax.experimental import pallas as pl
from jax.experimental.pallas import tpu as pltpu
from jax.sharding import PartitionSpec as P

DL = 512
DR = 64
DN = 128
DV = 128
EFF = 2048
REQ = 4
BEAMS = 4
HYPS = 16


MSCALE = 1.0 + 0.1 * math.log(40.0)
NEG = -1e30


def merged(value, axis, join):
    pieces = jax.tree.map(lambda part: lax.all_gather(part, axis), value)
    head = jax.tree.map(lambda part: part[0], pieces)
    tail = jax.tree.map(lambda part: part[1:], pieces)
    subtotal, _ = lax.scan(lambda subtotal, section: (join(subtotal, section), None), head, tail)
    return subtotal


def merge_pair(first_set, second_set):
    max_a, sum_a, acc_a = first_set
    max_b, sum_b, acc_b = second_set
    new_max = jnp.maximum(max_a, max_b)
    factor_a = jnp.exp(max_a - new_max)
    factor_b = jnp.exp(max_b - new_max)
    return (
        new_max,
        sum_a * factor_a + sum_b * factor_b,
        acc_a * factor_a[..., None] + acc_b * factor_b[..., None],
    )


def request_stats(
    q_lat, q_rope, pre_lat, pre_rope, suf_lat, suf_rope, is_live, softmax_scale, with_prefix
):
    suf_scores = jnp.einsum("bhl,bsl->bhs", q_lat, suf_lat, preferred_element_type=jnp.float32)
    suf_scores = (
        suf_scores
        + jnp.einsum("bhr,brs->bhs", q_rope, suf_rope, preferred_element_type=jnp.float32)
    ) * softmax_scale
    row_max = jnp.max(suf_scores, axis=2)
    beam_count, head_count, lat_width = q_lat.shape
    flat_lat = q_lat.reshape(beam_count * head_count, lat_width)
    flat_rope = q_rope.reshape(beam_count * head_count, q_rope.shape[2])
    pre_scores = lax.dot_general(
        flat_lat, pre_lat, (((1,), (1,)), ((), ())), preferred_element_type=jnp.float32
    )
    pre_scores = pre_scores + jnp.dot(flat_rope, pre_rope, preferred_element_type=jnp.float32)
    pre_scores = jnp.where(is_live[None, :], pre_scores * softmax_scale, NEG).reshape(
        beam_count, head_count, -1
    )
    row_max = jnp.maximum(row_max, jnp.max(pre_scores, axis=2))
    suf_weights = jnp.exp(suf_scores - row_max[..., None]).astype(jnp.bfloat16)
    weight_sum = jnp.sum(suf_weights.astype(jnp.float32), axis=2)
    weighted = jnp.einsum("bhs,bsl->bhl", suf_weights, suf_lat, preferred_element_type=jnp.float32)
    pre_weights = jnp.exp(pre_scores - row_max[..., None]).astype(jnp.bfloat16)
    weight_sum = weight_sum + jnp.sum(pre_weights.astype(jnp.float32), axis=2)
    prefix_part = jnp.dot(
        pre_weights.reshape(beam_count * head_count, -1),
        pre_lat,
        preferred_element_type=jnp.float32,
    )
    weighted = weighted + prefix_part.reshape(beam_count, head_count, lat_width)
    return (row_max, weight_sum, weighted)


def general_local(
    query_latent,
    query_rope,
    cache_latent,
    cache_rope,
    suffix_latent,
    suffix_rope,
    lengths,
    parents,
    w_uv,
    w_o,
    hidden,
    norm_gain,
    w_gate,
    w_up,
    w_down,
    expert_ids,
    gate_weights,
):
    q_lat, q_rope = (
        lax.all_gather(query_latent, "hx", axis=1, tiled=True),
        lax.all_gather(query_rope, "hx", axis=1, tiled=True),
    )
    head_count = q_lat.shape[1]
    q_rope = q_rope.reshape(HYPS, head_count, DR)
    softmax_scale = MSCALE * MSCALE / math.sqrt(DN + DR)
    n_hx = lax.axis_size("hx")
    linear = lax.axis_index("ctx") * n_hx + lax.axis_index("hx")
    ctx_block = cache_latent.shape[1]
    offsets = linear * ctx_block + jnp.arange(ctx_block, dtype=jnp.int32)
    suf_lat = jnp.take(suffix_latent, parents, axis=0)
    suf_rope = jnp.take(suffix_rope, parents, axis=0)
    maxima = []
    totals_list = []
    sums_list = []
    for request in range(REQ):
        hyp_rows = slice(request * BEAMS, (request + 1) * BEAMS)
        is_live = offsets < lengths[request]
        bound_stats = partial(
            request_stats,
            q_lat[hyp_rows],
            q_rope[hyp_rows],
            cache_latent[request],
            cache_rope[request],
            suf_lat[hyp_rows],
            suf_rope[hyp_rows],
            is_live,
            softmax_scale,
        )
        request_sums = bound_stats(True)
        maxima.append(request_sums[0])
        totals_list.append(request_sums[1])
        sums_list.append(request_sums[2])
    row_max = jnp.concatenate(maxima, axis=0)
    weight_sum = jnp.concatenate(totals_list, axis=0)
    weighted = jnp.concatenate(sums_list, axis=0)
    part_max, part_sum, part_acc = (
        lax.all_to_all(row_max[None], "ctx", split_axis=2, concat_axis=0, tiled=True),
        lax.all_to_all(weight_sum[None], "ctx", split_axis=2, concat_axis=0, tiled=True),
        lax.all_to_all(weighted[None], "ctx", split_axis=2, concat_axis=0, tiled=True),
    )
    group_max = jnp.max(part_max, axis=0)
    factor = jnp.exp(part_max - group_max[None])
    group_sum = jnp.sum(part_sum * factor, axis=0)
    group_acc = jnp.sum(part_acc * factor[..., None], axis=0)
    group_max, group_sum, group_acc = merged((group_max, group_sum, group_acc), "hx", merge_pair)
    attention = (group_acc / group_sum[..., None]).astype(jnp.bfloat16)
    columns = w_uv.shape[1]
    head_span = max(1, columns // DV)
    first_head = lax.axis_index("hx") * columns // DV
    chosen = lax.dynamic_slice_in_dim(attention, first_head, head_span, 1)
    value_map = w_uv.reshape(DL, head_span, columns // head_span)
    values = jnp.einsum("bnl,lnc->bnc", chosen, value_map, preferred_element_type=jnp.float32)
    values = values.astype(jnp.bfloat16).reshape(HYPS, columns)
    partial_out = jnp.dot(values, w_o, preferred_element_type=jnp.float32)
    attended = lax.psum(partial_out, ("ctx", "hx")).astype(jnp.bfloat16)
    residual = hidden.astype(jnp.float32) + attended.astype(jnp.float32)
    mean_square = jnp.mean(residual * residual, axis=1, keepdims=True)
    normed = (residual * lax.rsqrt(mean_square + 1e-06) * norm_gain).astype(jnp.bfloat16)
    unit_count = w_gate.shape[0]
    expert_here = linear * unit_count // EFF
    routed = jnp.sum(gate_weights * (expert_ids == expert_here).astype(jnp.float32), axis=1)
    gate_out = lax.dot_general(
        normed, w_gate, (((1,), (1,)), ((), ())), preferred_element_type=jnp.float32
    )
    up_out = lax.dot_general(
        normed, w_up, (((1,), (1,)), ((), ())), preferred_element_type=jnp.float32
    )
    activated = (jax.nn.silu(gate_out) * up_out * routed[:, None]).astype(jnp.bfloat16)
    expert_terms = jnp.dot(activated, w_down, preferred_element_type=jnp.float32)
    moe_share = lax.psum_scatter(expert_terms, ("ctx", "hx"), scatter_dimension=1, tiled=True)
    share_width = moe_share.shape[1]
    residual_share = lax.dynamic_slice_in_dim(residual, linear * share_width, share_width, 1)
    updated = (residual_share + moe_share).astype(jnp.bfloat16)
    return (attended, updated)


BF = jnp.bfloat16
F32 = jnp.float32
AXES = ("z", "x", "y", "core")
SHAPE = (4, 2, 2, 2)
CORE, Y, X, Z0, Z1 = 1, 2, 4, 8, 16
HEADS_DEV = 4
UNITS = 256
STAT = 16
LANES = 128
PARENTS = REQ
VMEM = pl.BlockSpec(memory_space=pltpu.VMEM)
SMEM = pl.BlockSpec(memory_space=pltpu.SMEM)
HBM = pl.BlockSpec(memory_space=pltpu.HBM)
NT = (((1,), (1,)), ((), ()))


def swap(value, mask):
    return lax.ppermute(value, AXES, [(i, i ^ mask) for i in range(math.prod(SHAPE))])


def in_hbm(value):
    return pltpu.with_memory_space_constraint(value, pltpu.HBM)


def bits(linear):
    return [linear >> k & 1 for k in range(5)]


def column(lane_row):
    n = lane_row.shape[1]
    at = lax.broadcasted_iota(jnp.int32, (n, n), 0)
    to = lax.broadcasted_iota(jnp.int32, (n, n), 1)
    return jnp.sum(jnp.where(at == to, lane_row, 0.0), axis=1, keepdims=True)


def stat_rows(lse):
    parts = []
    for _ in range(3):
        part = lse.astype(BF).astype(F32)
        parts.append(part)
        lse = lse - part
    return parts


def write_stat(out, body, parts, stat):
    stat[...] = jnp.zeros_like(stat)
    for i, part in enumerate(parts):
        stat[0:1, i * LANES:i * LANES + part.shape[1]] = part
    out[body:] = stat[...].astype(BF)


def read_stat(block, n):
    block = block.astype(F32)
    return (block[:1, :n] + block[:1, LANES:LANES + n]) + block[:1, 2 * LANES:2 * LANES + n]


def joined(lses):
    top = lses[0]
    for lse in lses[1:]:
        top = jnp.maximum(top, lse)
    weights = [jnp.exp(lse - top) for lse in lses]
    total = sum(weights[1:], weights[0])
    return [w / total for w in weights], top + jnp.log(total)


def attend_kernel(scale, first, count, fetch, later, info, ql0, ql1, qr0, qr1, cl_hbm, cr_hbm, sl_hbm, sr_hbm, *rest):
    earlier, rest = rest[:2 if later else 0], rest[-15:]
    keep, send, spread, qbuf, rbuf, pbuf, wide, lse_buf, stat, cl, cr, sl, sr, own_q, sems = rest
    linear = lax.axis_index(AXES)
    core, y, x, z0, _ = bits(linear)
    heads = ql1.shape[1]
    rows = 2 * heads
    total_rows = BEAMS * rows
    half = total_rows // 2
    targets = keep.shape[0]
    body = keep.shape[1] - STAT
    small = body // (2 * REQ)
    copies = []
    for k in range(count):
        beams = pl.ds((first + k) * BEAMS, BEAMS)
        here = pl.ds(k * BEAMS, BEAMS)
        group = [
            pltpu.make_async_copy(cl_hbm.at[first + k], cl.at[k], sems.at[0, k]),
            pltpu.make_async_copy(cr_hbm.at[first + k], cr.at[k], sems.at[1, k]),
            pltpu.make_async_copy(sl_hbm.at[beams], sl.at[here], sems.at[2, k]),
            pltpu.make_async_copy(sr_hbm.at[beams], sr.at[here], sems.at[3, k]),
        ]
        if fetch:
            group.append(pltpu.make_async_copy(ql0.at[here], own_q.at[here], sems.at[4, k]))
        for copy in group:
            copy.start()
        copies.append(group)
    first_q = own_q if fetch else ql0

    out_row = lax.broadcasted_iota(jnp.int32, (total_rows, total_rows), 0)
    in_row = lax.broadcasted_iota(jnp.int32, (total_rows, total_rows), 1)

    def source_of(row):
        bit = lambda k: (row >> k) & 1
        beam, head = (row >> 2) & 3, row & 3
        target = (bit(6) ^ x) * 4 + (bit(5) ^ y) * 2 + (bit(7) ^ core)
        return beam * rows + (bit(4) ^ core ^ z0) * heads + target * HEADS_DEV + head

    spread[...] = jnp.where(source_of(out_row) == in_row, 1.0, 0.0).astype(BF)
    moves = source_of(in_row) == out_row
    for i, out in enumerate((keep, send)):
        for t in range(targets):
            if later:
                out[t] = earlier[i][t]
                lse_buf[i * targets + t:i * targets + t + 1] = read_stat(earlier[i][t, body:], body)
            else:
                lse_buf[i * targets + t:i * targets + t + 1] = jnp.zeros((1, body), F32)
    wide[0] = qr0[...].astype(F32)
    wide[1] = qr1[...].astype(F32)
    per_group = LANES // DR
    head_row = lax.broadcasted_iota(jnp.int32, (heads, LANES), 0)
    own_lanes = lax.broadcasted_iota(jnp.int32, (heads, LANES), 1) // DR == head_row % per_group

    for k in range(count):
        r = first + k
        for copy in copies[k]:
            copy.wait()
        for j in range(BEAMS):
            for piece, q in enumerate((first_q, ql1)):
                part = slice(j * rows + piece * heads, j * rows + (piece + 1) * heads)
                qbuf[part] = q[k * BEAMS + j]
                b = r * BEAMS + j
                unfolded = jnp.zeros((heads, LANES), F32)
                for g in range(heads // per_group):
                    lanes = wide[piece, b:b + 1, g * LANES:(g + 1) * LANES]
                    unfolded = jnp.where(head_row // per_group == g, lanes, unfolded)
                rbuf[part] = jnp.where(own_lanes, unfolded, 0.0).astype(BF)
        keys = cl[k]
        ctx_block = keys.shape[0]
        pre = lax.dot_general(qbuf[...], keys, NT, preferred_element_type=F32)
        pre = pre + jnp.dot(rbuf[...], jnp.concatenate([cr[k]] * per_group, axis=0), preferred_element_type=F32)
        position = linear * ctx_block + lax.broadcasted_iota(jnp.int32, (1, ctx_block), 1)
        pre = jnp.where(position < info[r], pre * scale, NEG)
        own = [info[PARENTS + r * BEAMS + j] - first * BEAMS for j in range(BEAMS)]
        suf = []
        for j in range(BEAMS):
            part = slice(j * rows, (j + 1) * rows)
            s = lax.dot_general(qbuf[part], sl[own[j]], NT, preferred_element_type=F32)
            s = s + jnp.dot(rbuf[part], jnp.concatenate([sr[own[j]]] * per_group, axis=0),
                            preferred_element_type=F32)
            suf.append(s * scale)
        suf = jnp.concatenate(suf, axis=0)
        top = jnp.maximum(jnp.max(pre, axis=1, keepdims=True), jnp.max(suf, axis=1, keepdims=True))
        pre_w = jnp.exp(pre - top).astype(BF)
        suf_w = jnp.exp(suf - top).astype(BF)
        total = jnp.sum(pre_w.astype(F32), axis=1, keepdims=True)
        total = total + jnp.sum(suf_w.astype(F32), axis=1, keepdims=True)
        acc = jnp.dot(pre_w, keys, preferred_element_type=F32)
        inv = 1.0 / total
        for j in range(BEAMS):
            part = slice(j * rows, (j + 1) * rows)
            a = acc[part] + jnp.dot(suf_w[part], sl[own[j]], preferred_element_type=F32)
            pbuf[part] = (a * inv[part]).astype(BF)
        moved = jnp.dot(spread[...], pbuf[...], preferred_element_type=F32).astype(BF)
        lse = top + jnp.log(total)
        lane_lse = jnp.sum(jnp.where(moves, lse, 0.0), axis=0, keepdims=True)
        for i, out in enumerate((keep, send)):
            for t in range(targets):
                for zz in range(2):
                    at = i * half + (2 * t + zz) * small
                    to = (zz * REQ + r) * small
                    out[t, to:to + small] = moved[at:at + small]
                    lse_buf[i * targets + t:i * targets + t + 1, to:to + small] = lane_lse[:, at:at + small]
    parts = stat_rows(lse_buf[...])
    for i, out in enumerate((keep, send)):
        for t in range(targets):
            n = i * targets + t
            write_stat(out.at[t], body, [p[n:n + 1] for p in parts], stat)


def attend(scale, first, count, info, q_lat, q_rope, caches, earlier=()):
    fetch = first == 0 and count == REQ
    heads, width = q_lat[0].shape[1:]
    total_rows = BEAMS * 2 * heads
    targets = SHAPE[1] * SHAPE[2]
    body = REQ * total_rows // (2 * targets)
    message = jax.ShapeDtypeStruct((targets, body + STAT, width), BF)
    keys = caches[0].shape[1] + caches[2].shape[1]
    own_q = q_lat[0].shape if fetch else (8, LANES)
    return pl.pallas_call(
        partial(attend_kernel, scale, first, count, fetch, bool(earlier)),
        in_specs=[SMEM, HBM if fetch else VMEM] + [VMEM] * 3 + [HBM] * 4 + [VMEM] * len(earlier),
        out_specs=[VMEM] * 2,
        out_shape=[message] * 2,
        scratch_shapes=[
            pltpu.VMEM((total_rows, total_rows), BF),
            pltpu.VMEM((total_rows, width), BF),
            pltpu.VMEM((total_rows, LANES), BF),
            pltpu.VMEM((total_rows, width), BF),
            pltpu.VMEM((2, *q_rope[0].shape), F32),
            pltpu.VMEM((2 * targets, body), F32),
            pltpu.VMEM((STAT, width), F32),
        ] + [pltpu.VMEM((c.shape[0] * count // REQ, *c.shape[1:]), BF) for c in caches]
        + [pltpu.VMEM(own_q, BF), pltpu.SemaphoreType.DMA((5, count))],
        compiler_params=pltpu.CompilerParams(vmem_limit_bytes=14 << 20),
        cost_estimate=pl.CostEstimate(
            flops=count * 2 * total_rows * keys * (2 * width + DR), bytes_accessed=2 * count << 20,
            transcendentals=count * total_rows * keys),
        name="attend",
    )(info, in_hbm(q_lat[0]) if fetch else q_lat[0], q_lat[1], *q_rope, *(in_hbm(c) for c in caches), *earlier)


def pair_kernel(a, b, *rest):
    outs, stat = rest[:-1], rest[-1]
    targets, rows, _ = a.shape
    body = rows - STAT
    each = targets // len(outs)
    for t in range(targets):
        weights, lse = joined([read_stat(v[t, body:], body) for v in (a, b)])
        out = outs[t // each].at[t % each]
        out[:body] = (a[t, :body].astype(F32) * column(weights[0])
                      + b[t, :body].astype(F32) * column(weights[1])).astype(BF)
        write_stat(out, body, stat_rows(lse), stat)


def merge_pair_of(a, b, parts):
    return pl.pallas_call(
        pair_kernel,
        in_specs=[VMEM] * 2,
        out_specs=[VMEM] * parts,
        out_shape=[jax.ShapeDtypeStruct((a.shape[0] // parts, *a.shape[1:]), BF)] * parts,
        scratch_shapes=[pltpu.VMEM((STAT, a.shape[2]), F32)],
        compiler_params=pltpu.CompilerParams(vmem_limit_bytes=4 << 20),
        cost_estimate=pl.CostEstimate(flops=4 * a.size, bytes_accessed=6 * a.size, transcendentals=0),
        name="merge_pair",
    )(a, b)


def plane_kernel(count, *refs):
    groups = refs[:count], refs[count:2 * count]
    outs, (stat, held) = refs[2 * count:-2], refs[-2:]
    body = refs[0].shape[1] - STAT
    small = body // 2
    _, y, _, _, z1 = bits(lax.axis_index(AXES))
    for other, sources in enumerate(groups):
        weights, lse = joined([read_stat(ref[0, body:], body) for ref in sources])
        parts = stat_rows(lse)
        columns = [column(w) for w in weights]
        for z0 in range(2):
            part = slice(z0 * small, (z0 + 1) * small)
            total = None
            for ref, w in zip(sources, columns):
                term = ref[0, part].astype(F32) * w[part]
                total = term if total is None else total + term
            held[2 * other + z0, :small] = total.astype(BF)
            write_stat(held.at[2 * other + z0], small, [p[:, part] for p in parts], stat)
    for d, out in enumerate(outs):
        out[...] = held[2 * ((d >> 1) ^ y ^ z1) + (d & 1)]


def merge_plane(same, other):
    _, rows, width = same[0].shape
    shape = ((rows - STAT) // 2 + STAT, width)
    return pl.pallas_call(
        partial(plane_kernel, len(same)),
        in_specs=[VMEM] * 2 * len(same),
        out_specs=[VMEM] * SHAPE[0],
        out_shape=[jax.ShapeDtypeStruct(shape, BF)] * SHAPE[0],
        scratch_shapes=[pltpu.VMEM((STAT, width), F32), pltpu.VMEM((SHAPE[0], *shape), BF)],
        compiler_params=pltpu.CompilerParams(vmem_limit_bytes=4 << 20),
        cost_estimate=pl.CostEstimate(flops=16 * rows * width, bytes_accessed=24 * rows * width, transcendentals=0),
        name="merge_plane",
    )(*same, *other)


def sum_kernel(a, b, *outs):
    each = a.shape[0] // len(outs)
    for i, out in enumerate(outs):
        part = slice(i * each, (i + 1) * each)
        out[...] = (a[part].astype(F32) + b[part].astype(F32)).astype(out.dtype)


def stack_kernel(a, b, out):
    out[:a.shape[0]] = a[...]
    out[a.shape[0]:] = b[...]


def small_call(kernel, name, a, b, outs):
    return pl.pallas_call(
        kernel,
        in_specs=[VMEM] * 2,
        out_specs=[VMEM] * len(outs),
        out_shape=[jax.ShapeDtypeStruct(shape, BF) for shape in outs],
        compiler_params=pltpu.CompilerParams(vmem_limit_bytes=4 << 20),
        cost_estimate=pl.CostEstimate(flops=a.size, bytes_accessed=6 * a.size, transcendentals=0),
        name=name,
    )(a, b)


def halves(a, b):
    return small_call(sum_kernel, "halves", a, b, [(a.shape[0] // 2, *a.shape[1:])] * 2)


def plus(a, b):
    return small_call(sum_kernel, "plus", a, b, [a.shape])[0]


def cut_line(a, b):
    _, n, *tail = a.shape
    return halves(a.reshape(n, *tail), b.reshape(n, *tail))


def stacked(a, b):
    return small_call(stack_kernel, "stacked", a, b, [(2 * a.shape[0], *a.shape[1:])])[0]


def project_kernel(p0, p1, p2, p3, w_uv, w_o, keep, send):
    parts = (p0, p1, p2, p3)
    rows, _ = p0.shape
    body = rows - STAT
    weights, _ = joined([read_stat(p[body:], body) for p in parts])
    total = None
    for p, w in zip(parts, weights):
        term = p[:body].astype(F32) * column(w)
        total = term if total is None else total + term
    full = jnp.dot(total.astype(BF), w_uv[...], preferred_element_type=F32)
    rows, columns = full.shape
    row = lax.broadcasted_iota(jnp.int32, (rows, columns), 0)
    lane = lax.broadcasted_iota(jnp.int32, (rows, columns), 1)
    own = jnp.where((row & (HEADS_DEV - 1)) == lane // DV, full, 0.0).astype(BF)
    pick_hyp = lax.broadcasted_iota(jnp.int32, (HYPS, rows), 0)
    pick_row = lax.broadcasted_iota(jnp.int32, (HYPS, rows), 1)
    pick = jnp.where(pick_row // HEADS_DEV == pick_hyp, 1.0, 0.0).astype(BF)
    values = jnp.dot(pick, own, preferred_element_type=F32).astype(BF)
    width = keep.shape[2]
    plane = lax.axis_index(AXES) & 7
    for there, out in enumerate((keep, send)):
        for t in range(out.shape[0]):
            at = pl.multiple_of((plane ^ (2 * t + there)) * width, LANES)
            piece = jnp.dot(values, w_o[:, pl.ds(at, width)], preferred_element_type=F32)
            out[t] = piece.astype(BF)


def project(parts, w_uv, w_o):
    squares = SHAPE[1] * SHAPE[2]
    out = jax.ShapeDtypeStruct((squares, HYPS, w_o.shape[1] // (2 * squares)), BF)
    return pl.pallas_call(
        project_kernel,
        in_specs=[VMEM] * 6,
        out_specs=[VMEM] * 2,
        out_shape=[out] * 2,
        compiler_params=pltpu.CompilerParams(vmem_limit_bytes=4 << 20),
        cost_estimate=pl.CostEstimate(flops=2 * HYPS * w_o.size, bytes_accessed=2 * w_o.size, transcendentals=0),
        name="project",
    )(*parts, w_uv, w_o)


def experts_kernel(here, there, hidden, gain, ids, gates, w_gate, up_hbm, down_hbm,
                   attended, keep, send, residual, x_buf, acc, x_held, held, w_up, w_down, sems):
    units = w_gate.shape[0]
    chunks = units // UNITS
    copies = []
    for i, (source, dest) in enumerate(((up_hbm, w_up), (down_hbm, w_down))):
        for k in range(chunks):
            part = pl.ds(k * UNITS, UNITS)
            copy = pltpu.make_async_copy(source.at[part], dest.at[part], sems.at[i, k])
            copy.start()
            copies.append(copy)
    linear = lax.axis_index(AXES)
    plane, depth = linear & 7, linear >> 3
    share = here.shape[2]
    for core, shares in enumerate((here, there)):
        for t in range(shares.shape[0]):
            at = pl.multiple_of((plane ^ (2 * t + core)) * share, LANES)
            x_buf[:, pl.ds(at, share)] = shares[t].astype(F32)
            attended[:, pl.ds(at, share)] = shares[t]
    x = x_buf[...] + hidden[...].astype(F32)
    mean_square = jnp.mean(x * x, axis=1, keepdims=True)
    normed = (x * lax.rsqrt(mean_square + 1e-06) * gain[...]).astype(BF)
    expert = linear * units // EFF
    routed = column(jnp.sum(jnp.where(ids[...] == expert, gates[...], 0.0), axis=0, keepdims=True))
    parts = [slice(k * UNITS, (k + 1) * UNITS) for k in range(chunks)]
    gate = [lax.dot_general(normed, w_gate[part], NT, preferred_element_type=F32) for part in parts]
    gate = [g / (1.0 + jnp.exp(-g)) * routed for g in gate]
    act = []
    for k, part in enumerate(parts):
        copies[k].wait()
        up = lax.dot_general(normed, w_up[part], NT, preferred_element_type=F32)
        act.append((gate[k] * up).astype(BF))
    for k, part in enumerate(parts):
        copies[chunks + k].wait()
        term = jnp.dot(act[k], w_down[part], preferred_element_type=F32)
        if k == 0:
            acc[...] = term
        else:
            acc[...] += term
    count, _, width = held.shape
    for d in range(count):
        x_held[d] = x[:, d * width:(d + 1) * width]
        held[d] = acc[:, d * width:(d + 1) * width].astype(BF)
    residual[...] = x_held[linear]
    for core, out in enumerate((keep, send)):
        for t in range(out.shape[0]):
            for z in range(out.shape[1]):
                out[t, z] = held[((depth ^ z) << 3) + (plane ^ (2 * t + core))]


def experts(here, there, hidden, gain, ids, gates, w_gate, w_up, w_down):
    units, width = w_gate.shape
    squares = SHAPE[1] * SHAPE[2]
    small = width // (2 * squares * SHAPE[0])
    terms = jax.ShapeDtypeStruct((squares, SHAPE[0], HYPS, small), BF)
    return pl.pallas_call(
        experts_kernel,
        in_specs=[VMEM] * 7 + [HBM] * 2,
        out_specs=[VMEM] * 4,
        out_shape=[
            jax.ShapeDtypeStruct((HYPS, width), BF), terms, terms,
            jax.ShapeDtypeStruct((HYPS, small), F32),
        ],
        scratch_shapes=[pltpu.VMEM((HYPS, width), F32)] * 2 + [
            pltpu.VMEM((2 * squares * SHAPE[0], HYPS, small), F32),
            pltpu.VMEM((2 * squares * SHAPE[0], HYPS, small), BF),
        ] + [pltpu.VMEM((units, width), BF)] * 2 + [pltpu.SemaphoreType.DMA((2, units // UNITS))],
        compiler_params=pltpu.CompilerParams(vmem_limit_bytes=36 << 20),
        cost_estimate=pl.CostEstimate(flops=6 * HYPS * units * width, bytes_accessed=6 * units * width,
                                      transcendentals=HYPS * units),
        name="experts",
    )(here, there, hidden, gain, ids, gates, w_gate, in_hbm(w_up), in_hbm(w_down))


def local(
    query_latent,
    query_rope,
    cache_latent,
    cache_rope,
    suffix_latent,
    suffix_rope,
    lengths,
    parents,
    w_uv,
    w_o,
    hidden,
    norm_gain,
    w_gate,
    w_up,
    w_down,
    expert_ids,
    gate_weights,
):
    scale = MSCALE * MSCALE / math.sqrt(DN + DR)
    info = jnp.concatenate([lengths, parents])
    caches = (cache_latent, cache_rope, suffix_latent, suffix_rope)
    cut = HYPS // 2
    tied = lax.optimization_barrier

    near_lat, near_rope = swap(query_latent, CORE), swap(query_rope, CORE)
    lat_a = swap(query_latent[:cut], Y)
    far_rope = swap(query_rope, Y)
    lat_b = swap(query_latent[cut:], Y)
    keep, send = attend(scale, 0, REQ, info, (query_latent, near_lat), (query_rope, near_rope), caches)
    lat_a, far_rope, send = tied((lat_a, far_rope, send))
    far_rope = far_rope, swap(far_rope, CORE)
    near = merge_pair_of(keep, swap(send, CORE), 2)
    keep, send = attend(scale, 0, REQ // 2, info, (lat_a, swap(lat_a, CORE)), far_rope, caches)
    lat_b, send = tied((lat_b, send))
    near = merge_pair_of(near[0], swap(near[1], X), 2)
    keep, send = attend(scale, REQ // 2, REQ // 2, info, (lat_b, swap(lat_b, CORE)), far_rope, caches, (keep, send))
    far = merge_pair_of(keep, swap(send, CORE), SHAPE[1] * SHAPE[2])
    far_y, far_x, far_xy = (swap(v, mask) for v, mask in zip(far[1:], (Y, X, X ^ Y)))
    parts = merge_plane((near[0], far_y, far_xy), (swap(near[1], Y), far[0], far_x))
    parts = [parts[0], *(swap(v, mask) for v, mask in zip(parts[1:], (Z0, Z1, Z0 ^ Z1)))]
    keep, send = project(parts, w_uv, w_o)

    keep, send = halves(keep, swap(send, CORE))
    keep, send = halves(keep, swap(send, X))
    share = plus(keep, swap(send, Y))
    share = plus(share, swap(share, Z0))
    share = plus(share, swap(share, Z1))
    shares = stacked(share, swap(share, Y))
    shares = stacked(shares, swap(shares, X))
    attended, keep, send, residual = experts(
        shares, swap(shares, CORE), hidden, norm_gain.reshape(1, -1), expert_ids.T, gate_weights.T, w_gate, w_up, w_down)

    keep, send = halves(keep, swap(send, CORE))
    keep, send = halves(keep, swap(send, X))
    keep, send = cut_line(keep, swap(send, Y))
    keep, send = halves(keep, swap(send, Z1))
    total = keep.astype(F32) + swap(send, Z0).astype(F32)
    updated = (residual + total[0]).astype(BF)
    return (attended, updated)


def solution(mesh):
    if mesh.shape["ctx"] == SHAPE[0] * SHAPE[1] and mesh.shape["hx"] == SHAPE[2] * SHAPE[3]:
        chosen, names = local, AXES
        mesh = jax.sharding.Mesh(mesh.devices.reshape(SHAPE), AXES)
    else:
        chosen, names = general_local, ("ctx", "hx")
    all_axes, hx = names, names[len(names) // 2:]
    in_specs = (
        P(None, hx, None),
        P(None, hx),
        P(None, all_axes, None),
        P(None, None, all_axes),
        P(None, all_axes, None),
        P(None, None, all_axes),
        P(),
        P(),
        P(None, all_axes),
        P(all_axes, None),
        P(),
        P(),
        P(all_axes, None),
        P(all_axes, None),
        P(all_axes, None),
        P(),
        P(),
    )
    out_specs = (P(), P(None, all_axes))
    return jax.shard_map(chosen, mesh=mesh, in_specs=in_specs, out_specs=out_specs, check_vma=False)
```

```python
from functools import partial
import math

import jax
import jax.numpy as jnp
from jax import lax
from jax.experimental import pallas as pl
from jax.experimental.pallas import tpu as pltpu
from jax.sharding import PartitionSpec as P

DL = 512
DR = 64
DN = 128
DV = 128
EFF = 2048
REQ = 4
BEAMS = 4
HYPS = 16


MSCALE = 1.0 + 0.1 * math.log(40.0)
NEG = -1e30


def merged(value, axis, join):
    pieces = jax.tree.map(lambda part: lax.all_gather(part, axis), value)
    head = jax.tree.map(lambda part: part[0], pieces)
    tail = jax.tree.map(lambda part: part[1:], pieces)
    subtotal, _ = lax.scan(lambda subtotal, section: (join(subtotal, section), None), head, tail)
    return subtotal


def merge_pair(first_set, second_set):
    max_a, sum_a, acc_a = first_set
    max_b, sum_b, acc_b = second_set
    new_max = jnp.maximum(max_a, max_b)
    factor_a = jnp.exp(max_a - new_max)
    factor_b = jnp.exp(max_b - new_max)
    return (
        new_max,
        sum_a * factor_a + sum_b * factor_b,
        acc_a * factor_a[..., None] + acc_b * factor_b[..., None],
    )


def request_stats(
    q_lat, q_rope, pre_lat, pre_rope, suf_lat, suf_rope, is_live, softmax_scale, with_prefix
):
    suf_scores = jnp.einsum("bhl,bsl->bhs", q_lat, suf_lat, preferred_element_type=jnp.float32)
    suf_scores = (
        suf_scores
        + jnp.einsum("bhr,brs->bhs", q_rope, suf_rope, preferred_element_type=jnp.float32)
    ) * softmax_scale
    row_max = jnp.max(suf_scores, axis=2)
    beam_count, head_count, lat_width = q_lat.shape
    flat_lat = q_lat.reshape(beam_count * head_count, lat_width)
    flat_rope = q_rope.reshape(beam_count * head_count, q_rope.shape[2])
    pre_scores = lax.dot_general(
        flat_lat, pre_lat, (((1,), (1,)), ((), ())), preferred_element_type=jnp.float32
    )
    pre_scores = pre_scores + jnp.dot(flat_rope, pre_rope, preferred_element_type=jnp.float32)
    pre_scores = jnp.where(is_live[None, :], pre_scores * softmax_scale, NEG).reshape(
        beam_count, head_count, -1
    )
    row_max = jnp.maximum(row_max, jnp.max(pre_scores, axis=2))
    suf_weights = jnp.exp(suf_scores - row_max[..., None]).astype(jnp.bfloat16)
    weight_sum = jnp.sum(suf_weights.astype(jnp.float32), axis=2)
    weighted = jnp.einsum("bhs,bsl->bhl", suf_weights, suf_lat, preferred_element_type=jnp.float32)
    pre_weights = jnp.exp(pre_scores - row_max[..., None]).astype(jnp.bfloat16)
    weight_sum = weight_sum + jnp.sum(pre_weights.astype(jnp.float32), axis=2)
    prefix_part = jnp.dot(
        pre_weights.reshape(beam_count * head_count, -1),
        pre_lat,
        preferred_element_type=jnp.float32,
    )
    weighted = weighted + prefix_part.reshape(beam_count, head_count, lat_width)
    return (row_max, weight_sum, weighted)


def general_local(
    query_latent,
    query_rope,
    cache_latent,
    cache_rope,
    suffix_latent,
    suffix_rope,
    lengths,
    parents,
    w_uv,
    w_o,
    hidden,
    norm_gain,
    w_gate,
    w_up,
    w_down,
    expert_ids,
    gate_weights,
):
    q_lat, q_rope = (
        lax.all_gather(query_latent, "hx", axis=1, tiled=True),
        lax.all_gather(query_rope, "hx", axis=1, tiled=True),
    )
    head_count = q_lat.shape[1]
    q_rope = q_rope.reshape(HYPS, head_count, DR)
    softmax_scale = MSCALE * MSCALE / math.sqrt(DN + DR)
    n_hx = lax.axis_size("hx")
    linear = lax.axis_index("ctx") * n_hx + lax.axis_index("hx")
    ctx_block = cache_latent.shape[1]
    offsets = linear * ctx_block + jnp.arange(ctx_block, dtype=jnp.int32)
    suf_lat = jnp.take(suffix_latent, parents, axis=0)
    suf_rope = jnp.take(suffix_rope, parents, axis=0)
    maxima = []
    totals_list = []
    sums_list = []
    for request in range(REQ):
        hyp_rows = slice(request * BEAMS, (request + 1) * BEAMS)
        is_live = offsets < lengths[request]
        bound_stats = partial(
            request_stats,
            q_lat[hyp_rows],
            q_rope[hyp_rows],
            cache_latent[request],
            cache_rope[request],
            suf_lat[hyp_rows],
            suf_rope[hyp_rows],
            is_live,
            softmax_scale,
        )
        request_sums = bound_stats(True)
        maxima.append(request_sums[0])
        totals_list.append(request_sums[1])
        sums_list.append(request_sums[2])
    row_max = jnp.concatenate(maxima, axis=0)
    weight_sum = jnp.concatenate(totals_list, axis=0)
    weighted = jnp.concatenate(sums_list, axis=0)
    part_max, part_sum, part_acc = (
        lax.all_to_all(row_max[None], "ctx", split_axis=2, concat_axis=0, tiled=True),
        lax.all_to_all(weight_sum[None], "ctx", split_axis=2, concat_axis=0, tiled=True),
        lax.all_to_all(weighted[None], "ctx", split_axis=2, concat_axis=0, tiled=True),
    )
    group_max = jnp.max(part_max, axis=0)
    factor = jnp.exp(part_max - group_max[None])
    group_sum = jnp.sum(part_sum * factor, axis=0)
    group_acc = jnp.sum(part_acc * factor[..., None], axis=0)
    group_max, group_sum, group_acc = merged((group_max, group_sum, group_acc), "hx", merge_pair)
    attention = (group_acc / group_sum[..., None]).astype(jnp.bfloat16)
    columns = w_uv.shape[1]
    head_span = max(1, columns // DV)
    first_head = lax.axis_index("hx") * columns // DV
    chosen = lax.dynamic_slice_in_dim(attention, first_head, head_span, 1)
    value_map = w_uv.reshape(DL, head_span, columns // head_span)
    values = jnp.einsum("bnl,lnc->bnc", chosen, value_map, preferred_element_type=jnp.float32)
    values = values.astype(jnp.bfloat16).reshape(HYPS, columns)
    partial_out = jnp.dot(values, w_o, preferred_element_type=jnp.float32)
    attended = lax.psum(partial_out, ("ctx", "hx")).astype(jnp.bfloat16)
    residual = hidden.astype(jnp.float32) + attended.astype(jnp.float32)
    mean_square = jnp.mean(residual * residual, axis=1, keepdims=True)
    normed = (residual * lax.rsqrt(mean_square + 1e-06) * norm_gain).astype(jnp.bfloat16)
    unit_count = w_gate.shape[0]
    expert_here = linear * unit_count // EFF
    routed = jnp.sum(gate_weights * (expert_ids == expert_here).astype(jnp.float32), axis=1)
    gate_out = lax.dot_general(
        normed, w_gate, (((1,), (1,)), ((), ())), preferred_element_type=jnp.float32
    )
    up_out = lax.dot_general(
        normed, w_up, (((1,), (1,)), ((), ())), preferred_element_type=jnp.float32
    )
    activated = (jax.nn.silu(gate_out) * up_out * routed[:, None]).astype(jnp.bfloat16)
    expert_terms = jnp.dot(activated, w_down, preferred_element_type=jnp.float32)
    moe_share = lax.psum_scatter(expert_terms, ("ctx", "hx"), scatter_dimension=1, tiled=True)
    share_width = moe_share.shape[1]
    residual_share = lax.dynamic_slice_in_dim(residual, linear * share_width, share_width, 1)
    updated = (residual_share + moe_share).astype(jnp.bfloat16)
    return (attended, updated)


BF = jnp.bfloat16
F32 = jnp.float32
AXES = ("z", "x", "y", "core")
SHAPE = (4, 2, 2, 2)
CORE, Y, X, Z0, Z1 = 1, 2, 4, 8, 16
HEADS_DEV = 4
UNITS = 256
STAT = 16
LANES = 128
PARENTS = REQ
LOG2E = math.log2(math.e)
VMEM = pl.BlockSpec(memory_space=pltpu.VMEM)
SMEM = pl.BlockSpec(memory_space=pltpu.SMEM)
HBM = pl.BlockSpec(memory_space=pltpu.HBM)
NT = (((1,), (1,)), ((), ()))
EXCHANGE = pl.CostEstimate(flops=0, bytes_accessed=12 << 20, transcendentals=0)


def swap(value, mask):
    return lax.ppermute(value, AXES, [(i, i ^ mask) for i in range(math.prod(SHAPE))])


def in_hbm(value):
    return pltpu.with_memory_space_constraint(value, pltpu.HBM)


def bits(linear):
    return [linear >> k & 1 for k in range(5)]


def column(lane_row):
    n = lane_row.shape[1]
    at = lax.broadcasted_iota(jnp.int32, (n, n), 0)
    to = lax.broadcasted_iota(jnp.int32, (n, n), 1)
    return jnp.sum(jnp.where(at == to, lane_row, 0.0), axis=1, keepdims=True)


def stat_rows(lse):
    parts = []
    for _ in range(3):
        part = lse.astype(BF).astype(F32)
        parts.append(part)
        lse = lse - part
    return parts


def write_stat(out, body, parts, stat):
    stat[...] = jnp.zeros_like(stat)
    for i, part in enumerate(parts):
        stat[0:1, i * LANES:i * LANES + part.shape[1]] = part
    out[body:] = stat[...].astype(BF)


def read_stat(block, n):
    block = block.astype(F32)
    return (block[:1, :n] + block[:1, LANES:LANES + n]) + block[:1, 2 * LANES:2 * LANES + n]


def joined(lses):
    top = lses[0]
    for lse in lses[1:]:
        top = jnp.maximum(top, lse)
    weights = [jnp.exp(lse - top) for lse in lses]
    total = sum(weights[1:], weights[0])
    return [w / total for w in weights], top + jnp.log(total)


def attend_kernel(scale, fetch, info, ql0, ql1, qr0, qr1, cl_hbm, cr_hbm, sl_hbm, sr_hbm, keep, send0, send1,
                  spread, qbuf, rbuf, pbuf, wide, lse_buf, stat, cl, cr, sl, sr, own_q, own_r, sems):
    linear = lax.axis_index(AXES)
    core, y, x, z0, _ = bits(linear)
    heads = ql1.shape[1]
    rows = 2 * heads
    total_rows = BEAMS * rows
    targets = keep.shape[0]
    body = keep.shape[1] - STAT
    small = body // (2 * REQ)
    query_copies = []
    if fetch:
        query_copies = [pltpu.make_async_copy(qr0, own_r, sems.at[4, 0]),
                        pltpu.make_async_copy(ql0, own_q, sems.at[4, 1])]
        for copy in query_copies:
            copy.start()
    copies = []
    for r in range(REQ):
        beams = pl.ds(r * BEAMS, BEAMS)
        group = [
            pltpu.make_async_copy(cl_hbm.at[r], cl.at[r], sems.at[0, r]),
            pltpu.make_async_copy(cr_hbm.at[r], cr.at[r], sems.at[1, r]),
            pltpu.make_async_copy(sl_hbm.at[beams], sl.at[beams], sems.at[2, r]),
            pltpu.make_async_copy(sr_hbm.at[beams], sr.at[beams], sems.at[3, r]),
        ]
        for copy in group:
            copy.start()
        copies.append(group)
    first_q, first_r = (own_q, own_r) if fetch else (ql0, qr0)

    out_row = lax.broadcasted_iota(jnp.int32, (total_rows, total_rows), 0)
    in_row = lax.broadcasted_iota(jnp.int32, (total_rows, total_rows), 1)

    def source_of(row):
        bit = lambda k: (row >> k) & 1
        beam, head = (row >> 2) & 3, row & 3
        target = (bit(6) ^ x) * 4 + (bit(5) ^ y) * 2 + (bit(7) ^ core)
        return beam * rows + (bit(4) ^ core ^ z0) * heads + target * HEADS_DEV + head

    spread[...] = jnp.where(source_of(out_row) == in_row, 1.0, 0.0).astype(BF)
    moves = source_of(in_row) == out_row
    messages = [keep.at[t] for t in range(targets)]
    messages += [send.at[t] for send in (send0, send1) for t in range(targets // 2)]
    lse_buf[...] = jnp.zeros_like(lse_buf)
    for copy in query_copies:
        copy.wait()
    wide[0] = first_r[...].astype(F32)
    wide[1] = qr1[...].astype(F32)
    per_group = LANES // DR
    head_row = lax.broadcasted_iota(jnp.int32, (heads, LANES), 0)
    own_lanes = lax.broadcasted_iota(jnp.int32, (heads, LANES), 1) // DR == head_row % per_group

    for r in range(REQ):
        for j in range(BEAMS):
            for piece, q in enumerate((first_q, ql1)):
                part = slice(j * rows + piece * heads, j * rows + (piece + 1) * heads)
                b = r * BEAMS + j
                qbuf[r, part] = q[b]
                unfolded = jnp.zeros((heads, LANES), F32)
                for g in range(heads // per_group):
                    lanes = wide[piece, b:b + 1, g * LANES:(g + 1) * LANES]
                    unfolded = jnp.where(head_row // per_group == g, lanes, unfolded)
                rbuf[r, part] = jnp.where(own_lanes, unfolded, 0.0).astype(BF)

    def scores(r):
        for copy in copies[r]:
            copy.wait()
        keys = cl[r]
        ctx_block = keys.shape[0]
        pre = lax.dot_general(qbuf[r], keys, NT, preferred_element_type=F32)
        pre = pre + jnp.dot(rbuf[r], jnp.concatenate([cr[r]] * per_group, axis=0), preferred_element_type=F32)
        position = linear * ctx_block + lax.broadcasted_iota(jnp.int32, (1, ctx_block), 1)
        pre = jnp.where(position < info[r], pre, NEG)
        own = [info[PARENTS + r * BEAMS + j] for j in range(BEAMS)]
        suf = []
        suf_keys = []
        for j in range(0, BEAMS, 2):
            part = slice(j * rows, (j + 2) * rows)
            pair_keys = jnp.concatenate([sl[own[j]], sl[own[j + 1]]], axis=0)
            pair_rope = jnp.concatenate([sr[own[j]], sr[own[j + 1]]], axis=1)
            s = lax.dot_general(qbuf[r, part], pair_keys, NT, preferred_element_type=F32)
            s = s + jnp.dot(rbuf[r, part], jnp.concatenate([pair_rope] * per_group, axis=0),
                            preferred_element_type=F32)
            n = s.shape[1] // 2
            suf += [s[:rows, :n], s[rows:, n:]]
            suf_keys.append(pair_keys)
        return pre, jnp.concatenate(suf, axis=0), suf_keys

    def finish(r, pre, suf, suf_keys):
        top = jnp.maximum(jnp.max(pre, axis=1, keepdims=True), jnp.max(suf, axis=1, keepdims=True))
        pre_w = jnp.exp2((pre - top) * (scale * LOG2E))
        suf_w = jnp.exp2((suf - top) * (scale * LOG2E))
        total = jnp.sum(pre_w, axis=1, keepdims=True) + jnp.sum(suf_w, axis=1, keepdims=True)
        pre_w, suf_w = pre_w.astype(BF), suf_w.astype(BF)
        acc = jnp.dot(pre_w, cl[r], preferred_element_type=F32)
        inv = 1.0 / total
        for j in range(0, BEAMS, 2):
            part = slice(j * rows, (j + 2) * rows)
            first, second = suf_w[j * rows:(j + 1) * rows], suf_w[(j + 1) * rows:(j + 2) * rows]
            none = jnp.zeros_like(first)
            spread_w = jnp.concatenate([jnp.concatenate([first, none], axis=1),
                                        jnp.concatenate([none, second], axis=1)], axis=0)
            a = acc[part] + jnp.dot(spread_w, suf_keys[j // 2], preferred_element_type=F32)
            pbuf[r, part] = (a * inv[part]).astype(BF)
        moved = jnp.dot(spread[...], pbuf[r], preferred_element_type=F32).astype(BF)
        lse = scale * top + jnp.log(total)
        lane_lse = jnp.sum(jnp.where(moves, lse, 0.0), axis=0, keepdims=True)
        for n, message in enumerate(messages):
            for zz in range(2):
                at = (2 * n + zz) * small
                to = (zz * REQ + r) * small
                message[to:to + small] = moved[at:at + small]
                lse_buf[n:n + 1, to:to + small] = lane_lse[:, at:at + small]

    now = scores(0)
    for r in range(REQ):
        later = scores(r + 1) if r + 1 < REQ else None
        finish(r, *now)
        now = later
    parts = stat_rows(lse_buf[...])
    for n, message in enumerate(messages):
        write_stat(message, body, [p[n:n + 1] for p in parts], stat)


def attend(scale, fetch, info, q_lat, q_rope, caches):
    heads, width = q_lat[0].shape[1:]
    total_rows = BEAMS * 2 * heads
    targets = SHAPE[1] * SHAPE[2]
    body = REQ * total_rows // (2 * targets)
    message = lambda n: jax.ShapeDtypeStruct((n, body + STAT, width), BF)
    keys = caches[0].shape[1] + caches[2].shape[1]
    own = [v.shape if fetch else (STAT, LANES) for v in (q_lat[0], q_rope[0])]
    first = [in_hbm(v) if fetch else v for v in (q_lat[0], q_rope[0])]
    spec = HBM if fetch else VMEM
    return pl.pallas_call(
        partial(attend_kernel, scale, fetch),
        in_specs=[SMEM, spec, VMEM, spec, VMEM] + [HBM] * 4,
        out_specs=[VMEM] * 3,
        out_shape=[message(targets), message(targets // 2), message(targets // 2)],
        scratch_shapes=[
            pltpu.VMEM((total_rows, total_rows), BF),
            pltpu.VMEM((REQ, total_rows, width), BF),
            pltpu.VMEM((REQ, total_rows, LANES), BF),
            pltpu.VMEM((REQ, total_rows, width), BF),
            pltpu.VMEM((2, *q_rope[0].shape), F32),
            pltpu.VMEM((2 * targets, body), F32),
            pltpu.VMEM((STAT, width), F32),
        ] + [pltpu.VMEM(c.shape, BF) for c in caches]
        + [pltpu.VMEM(shape, BF) for shape in own] + [pltpu.SemaphoreType.DMA((5, REQ))],
        compiler_params=pltpu.CompilerParams(vmem_limit_bytes=14 << 20),
        cost_estimate=pl.CostEstimate(
            flops=REQ * 2 * total_rows * keys * (2 * width + DR), bytes_accessed=8 << 20,
            transcendentals=REQ * total_rows * keys),
        name="attend",
    )(info, first[0], q_lat[1], first[1], q_rope[1], *(in_hbm(c) for c in caches))


def pair_kernel(count, a, *refs):
    got, outs, stat = refs[:count], refs[count:-1], refs[-1]
    targets, rows, _ = a.shape
    body = rows - STAT
    for t in range(targets):
        ours, theirs = a.at[t], got[t // (targets // count)].at[t % (targets // count)]
        out = outs[t // (targets // len(outs))].at[t % (targets // len(outs))]
        weights, lse = joined([read_stat(v[body:], body) for v in (ours, theirs)])
        out[:body] = (ours[:body].astype(F32) * column(weights[0])
                      + theirs[:body].astype(F32) * column(weights[1])).astype(BF)
        write_stat(out, body, stat_rows(lse), stat)


def merge_pairs(a, got, parts):
    return pl.pallas_call(
        partial(pair_kernel, len(got)),
        in_specs=[VMEM] * (1 + len(got)),
        out_specs=[VMEM] * parts,
        out_shape=[jax.ShapeDtypeStruct((a.shape[0] // parts, *a.shape[1:]), BF)] * parts,
        scratch_shapes=[pltpu.VMEM((STAT, a.shape[2]), F32)],
        compiler_params=pltpu.CompilerParams(vmem_limit_bytes=4 << 20),
        cost_estimate=pl.CostEstimate(flops=4 * a.size, bytes_accessed=6 * a.size, transcendentals=0),
        name="merge_pairs",
    )(a, *got)


def plane_kernel(count, *refs):
    groups = refs[:count], refs[count:2 * count]
    outs, (stat, held) = refs[2 * count:-2], refs[-2:]
    body = refs[0].shape[1] - STAT
    small = body // 2
    _, y, _, _, z1 = bits(lax.axis_index(AXES))
    for other, sources in enumerate(groups):
        weights, lse = joined([read_stat(ref[0, body:], body) for ref in sources])
        parts = stat_rows(lse)
        columns = [column(w) for w in weights]
        for z0 in range(2):
            part = slice(z0 * small, (z0 + 1) * small)
            total = None
            for ref, w in zip(sources, columns):
                term = ref[0, part].astype(F32) * w[part]
                total = term if total is None else total + term
            held[2 * other + z0, :small] = total.astype(BF)
            write_stat(held.at[2 * other + z0], small, [p[:, part] for p in parts], stat)
    for d, out in enumerate(outs):
        out[...] = held[2 * ((d >> 1) ^ y ^ z1) + (d & 1)]


def merge_plane(same, other):
    _, rows, width = same[0].shape
    shape = ((rows - STAT) // 2 + STAT, width)
    return pl.pallas_call(
        partial(plane_kernel, len(same)),
        in_specs=[VMEM] * 2 * len(same),
        out_specs=[VMEM] * SHAPE[0],
        out_shape=[jax.ShapeDtypeStruct(shape, BF)] * SHAPE[0],
        scratch_shapes=[pltpu.VMEM((STAT, width), F32), pltpu.VMEM((SHAPE[0], *shape), BF)],
        compiler_params=pltpu.CompilerParams(vmem_limit_bytes=4 << 20),
        cost_estimate=pl.CostEstimate(flops=16 * rows * width, bytes_accessed=24 * rows * width, transcendentals=0),
        name="merge_plane",
    )(*same, *other)


def sum_kernel(count, *refs):
    ins, outs = refs[:count], refs[count:]
    for i, out in enumerate(outs):
        terms = [(ref[...] if len(outs) == 1 else ref[i]).astype(F32) for ref in ins]
        while len(terms) > 1:
            terms = [a + b for a, b in zip(terms[::2], terms[1::2])]
        out[...] = terms[0].astype(BF)


def sums(arrays, split):
    count, shape = len(arrays), arrays[0].shape
    outs = [shape[1:]] * shape[0] if split else [shape]
    return pl.pallas_call(
        partial(sum_kernel, count),
        in_specs=[VMEM] * count,
        out_specs=[VMEM] * len(outs),
        out_shape=[jax.ShapeDtypeStruct(out, BF) for out in outs],
        compiler_params=pltpu.CompilerParams(vmem_limit_bytes=4 << 20),
        cost_estimate=EXCHANGE,
        name="sums",
    )(*arrays)


def project_kernel(p0, p1, p2, p3, w_uv, w_o, keep, send):
    parts = (p0, p1, p2, p3)
    rows, _ = p0.shape
    body = rows - STAT
    weights, _ = joined([read_stat(p[body:], body) for p in parts])
    total = None
    for p, w in zip(parts, weights):
        term = p[:body].astype(F32) * column(w)
        total = term if total is None else total + term
    full = jnp.dot(total.astype(BF), w_uv[...], preferred_element_type=F32)
    rows, columns = full.shape
    row = lax.broadcasted_iota(jnp.int32, (rows, columns), 0)
    lane = lax.broadcasted_iota(jnp.int32, (rows, columns), 1)
    own = jnp.where((row & (HEADS_DEV - 1)) == lane // DV, full, 0.0).astype(BF)
    pick_hyp = lax.broadcasted_iota(jnp.int32, (HYPS, rows), 0)
    pick_row = lax.broadcasted_iota(jnp.int32, (HYPS, rows), 1)
    pick = jnp.where(pick_row // HEADS_DEV == pick_hyp, 1.0, 0.0).astype(BF)
    values = jnp.dot(pick, own, preferred_element_type=F32).astype(BF)
    width = keep.shape[2]
    plane = lax.axis_index(AXES) & 7
    for there, out in enumerate((keep, send)):
        for t in range(out.shape[0]):
            at = pl.multiple_of((plane ^ (2 * t + there)) * width, LANES)
            piece = jnp.dot(values, w_o[:, pl.ds(at, width)], preferred_element_type=F32)
            out[t] = piece.astype(BF)


def project(parts, w_uv, w_o):
    squares = SHAPE[1] * SHAPE[2]
    out = jax.ShapeDtypeStruct((squares, HYPS, w_o.shape[1] // (2 * squares)), BF)
    return pl.pallas_call(
        project_kernel,
        in_specs=[VMEM] * 6,
        out_specs=[VMEM] * 2,
        out_shape=[out] * 2,
        compiler_params=pltpu.CompilerParams(vmem_limit_bytes=4 << 20),
        cost_estimate=pl.CostEstimate(flops=2 * HYPS * w_o.size, bytes_accessed=2 * w_o.size, transcendentals=0),
        name="project",
    )(*parts, w_uv, w_o)


def core_sum_kernel(a, b, out):
    chip = lax.axis_index(AXES) >> 1
    square, depth = chip & 3, chip >> 2
    for t in range(a.shape[0]):
        for z in range(a.shape[1]):
            out[(depth ^ z) * a.shape[0] + (square ^ t)] = (a[t, z].astype(F32) + b[t, z].astype(F32)).astype(BF)


def core_sum(a, b):
    squares, depth, *tail = a.shape
    return pl.pallas_call(
        core_sum_kernel,
        in_specs=[VMEM] * 2,
        out_specs=VMEM,
        out_shape=jax.ShapeDtypeStruct((squares * depth, *tail), BF),
        compiler_params=pltpu.CompilerParams(vmem_limit_bytes=4 << 20),
        cost_estimate=EXCHANGE,
        name="core_sum",
    )(a, b)


def load_kernel(count, *refs):
    sources, dests, sems = refs[:count], refs[count + 1:-1], refs[-1]
    copies = [pltpu.make_async_copy(sources[i], dests[i], sems.at[i]) for i in range(count)]
    for copy in copies:
        copy.start()
    for copy in copies:
        copy.wait()


def load(after, *arrays):
    count = len(arrays)
    return pl.pallas_call(
        partial(load_kernel, count),
        in_specs=[HBM] * count + [pl.BlockSpec(memory_space=pl.ANY)],
        out_specs=[VMEM] * count,
        out_shape=[pltpu.VMEM(a.shape, a.dtype) for a in arrays],
        scratch_shapes=[pltpu.SemaphoreType.DMA((count,))],
        compiler_params=pltpu.CompilerParams(vmem_limit_bytes=1 << 20),
        cost_estimate=pl.CostEstimate(
            flops=0, bytes_accessed=sum(2 * a.size for a in arrays), transcendentals=0),
        name="load",
    )(*(in_hbm(a) for a in arrays), after)


def experts_kernel(*refs):
    shares, (hidden, gain, ids, gates, w_gate, w_up, down_hbm) = refs[:8], refs[8:15]
    attended, keep, send, residual, x_buf, acc, x_held, w_down, sems = refs[15:]
    units = w_gate.shape[0]
    chunks = units // UNITS
    parts = [slice(k * UNITS, (k + 1) * UNITS) for k in range(chunks)]
    downs = [pltpu.make_async_copy(down_hbm.at[pl.ds(k * UNITS, UNITS)], w_down.at[pl.ds(k * UNITS, UNITS)],
                                   sems.at[k]) for k in range(chunks)]
    for copy in downs:
        copy.start()
    linear = lax.axis_index(AXES)
    plane, depth = linear & 7, linear >> 3
    share = shares[0].shape[1]
    for d, ref in enumerate(shares):
        at = pl.multiple_of((plane ^ d) * share, LANES)
        x_buf[:, pl.ds(at, share)] = ref[...].astype(F32)
        attended[:, pl.ds(at, share)] = ref[...]
    x = x_buf[...] + hidden[...].astype(F32)
    mean_square = jnp.mean(x * x, axis=1, keepdims=True)
    normed = (x * lax.rsqrt(mean_square + 1e-06) * gain[...]).astype(BF)
    expert = linear * units // EFF
    routed = column(jnp.sum(jnp.where(ids[...] == expert, gates[...], 0.0), axis=0, keepdims=True))
    count, _, width = x_held.shape
    for d in range(count):
        x_held[d] = x[:, d * width:(d + 1) * width]
    residual[...] = x_held[linear]
    gate = [lax.dot_general(normed, w_gate[part], NT, preferred_element_type=F32) for part in parts]
    gate = [g / (1.0 + jnp.exp(-g)) * routed for g in gate]
    act = []
    for k, part in enumerate(parts):
        up = lax.dot_general(normed, w_up[part], NT, preferred_element_type=F32)
        act.append((gate[k] * up).astype(BF))
    for k, part in enumerate(parts):
        downs[k].wait()
        term = jnp.dot(act[k], w_down[part], preferred_element_type=F32)
        if k == 0:
            acc[...] = term
        else:
            acc[...] += term
    core = linear & CORE
    for d in range(0, count, 2):
        pair = [acc[:, (d + i) * width:(d + i + 1) * width].astype(BF) for i in range(2)]
        at = ((d >> 1) ^ (linear >> 1)) & 3, depth ^ (d >> 3)
        keep[at] = jnp.where(core == 1, pair[1], pair[0])
        send[at] = jnp.where(core == 1, pair[0], pair[1])


def experts(shares, hidden, gain, ids, gates, w_gate, w_up, w_down):
    units, width = w_gate.shape
    count = math.prod(SHAPE)
    small = width // count
    terms = jax.ShapeDtypeStruct((SHAPE[1] * SHAPE[2], SHAPE[0], HYPS, small), BF)
    return pl.pallas_call(
        experts_kernel,
        in_specs=[VMEM] * 14 + [HBM],
        out_specs=[VMEM] * 4,
        out_shape=[
            jax.ShapeDtypeStruct((HYPS, width), BF), terms, terms,
            jax.ShapeDtypeStruct((HYPS, small), F32),
        ],
        scratch_shapes=[pltpu.VMEM((HYPS, width), F32)] * 2 + [
            pltpu.VMEM((count, HYPS, small), F32),
            pltpu.VMEM((units, width), BF),
            pltpu.SemaphoreType.DMA((units // UNITS,)),
        ],
        compiler_params=pltpu.CompilerParams(vmem_limit_bytes=18 << 20),
        cost_estimate=pl.CostEstimate(flops=6 * HYPS * units * width, bytes_accessed=6 * units * width,
                                      transcendentals=HYPS * units),
        name="experts",
    )(*shares, hidden, gain, ids, gates, w_gate, w_up, in_hbm(w_down))


def local(
    query_latent,
    query_rope,
    cache_latent,
    cache_rope,
    suffix_latent,
    suffix_rope,
    lengths,
    parents,
    w_uv,
    w_o,
    hidden,
    norm_gain,
    w_gate,
    w_up,
    w_down,
    expert_ids,
    gate_weights,
):
    scale = MSCALE * MSCALE / math.sqrt(DN + DR)
    info = jnp.concatenate([lengths, parents])
    caches = (cache_latent, cache_rope, suffix_latent, suffix_rope)
    tied = lax.optimization_barrier
    square, line = (Y, X, X ^ Y), (Z0 ^ Z1, Z1, Z0)

    near_lat, near_rope = swap(query_latent, CORE), swap(query_rope, CORE)
    far_lat, far_rope = swap(query_latent, Y), swap(query_rope, Y)
    keep, *send = attend(scale, True, info, (query_latent, near_lat), (query_rope, near_rope), caches)
    near = merge_pairs(keep, [swap(v, CORE) for v in send], 2)
    far_lat, far_rope, near = tied((far_lat, far_rope, near))
    near_x = swap(near[1], X)
    far_lat, far_rope = (far_lat, swap(far_lat, CORE)), (far_rope, swap(far_rope, CORE))
    keep, *send = attend(scale, False, info, far_lat, far_rope, caches)
    keep, send, near_x = tied((keep, send, near_x))
    near = merge_pairs(near[0], [near_x], 2)
    near_y = swap(near[1], Y)
    far = merge_pairs(keep, [swap(v, CORE) for v in send], len(square) + 1)
    far_xy, far_x, far_y = swap(far[3], X ^ Y), swap(far[2], X), swap(far[1], Y)
    parts = merge_plane((near[0], far_y, far_xy), (near_y, far[0], far_x))
    w_uv, w_o = load(parts[0], w_uv, w_o)
    parts = [parts[0], *(swap(v, mask) for v, mask in zip(parts[:0:-1], line))]
    keep, send = project(parts, w_uv, w_o)

    pieces = sums([keep, swap(send, CORE)], True)
    share, = sums([pieces[0], *(swap(v, mask) for v, mask in zip(pieces[1:], square))], False)
    share, = sums([share, *(swap(share, mask) for mask in line[::-1])], False)
    shares = [share, *(swap(share, mask) for mask in square)]
    shares = [v for pair in zip(shares, [swap(v, CORE) for v in shares]) for v in pair]
    attended, keep, send, residual = experts(
        shares, hidden, norm_gain.reshape(1, -1), expert_ids.T, gate_weights.T, w_gate, w_up, w_down)

    total = core_sum(keep, swap(send, CORE))
    total = lax.all_to_all(total, AXES[:3], split_axis=0, concat_axis=0, tiled=True)
    updated = (residual + jnp.sum(total.astype(F32), axis=0)).astype(BF)
    return (attended, updated)


def solution(mesh):
    if mesh.shape["ctx"] == SHAPE[0] * SHAPE[1] and mesh.shape["hx"] == SHAPE[2] * SHAPE[3]:
        chosen, names = local, AXES
        mesh = jax.sharding.Mesh(mesh.devices.reshape(SHAPE), AXES)
    else:
        chosen, names = general_local, ("ctx", "hx")
    all_axes, hx = names, names[len(names) // 2:]
    in_specs = (
        P(None, hx, None),
        P(None, hx),
        P(None, all_axes, None),
        P(None, None, all_axes),
        P(None, all_axes, None),
        P(None, None, all_axes),
        P(),
        P(),
        P(None, all_axes),
        P(all_axes, None),
        P(),
        P(),
        P(all_axes, None),
        P(all_axes, None),
        P(all_axes, None),
        P(),
        P(),
    )
    out_specs = (P(), P(None, all_axes))
    return jax.shard_map(chosen, mesh=mesh, in_specs=in_specs, out_specs=out_specs, check_vma=False)
```

```python
from functools import partial
import math

import jax
import jax.numpy as jnp
from jax import lax
from jax.experimental import pallas as pl
from jax.experimental.pallas import tpu as pltpu
from jax.sharding import PartitionSpec as P

DL = 512
DR = 64
DN = 128
DV = 128
EFF = 2048
REQ = 4
BEAMS = 4
HYPS = 16


MSCALE = 1.0 + 0.1 * math.log(40.0)
NEG = -1e30


def merged(value, axis, join):
    pieces = jax.tree.map(lambda part: lax.all_gather(part, axis), value)
    head = jax.tree.map(lambda part: part[0], pieces)
    tail = jax.tree.map(lambda part: part[1:], pieces)
    subtotal, _ = lax.scan(lambda subtotal, section: (join(subtotal, section), None), head, tail)
    return subtotal


def merge_pair(first_set, second_set):
    max_a, sum_a, acc_a = first_set
    max_b, sum_b, acc_b = second_set
    new_max = jnp.maximum(max_a, max_b)
    factor_a = jnp.exp(max_a - new_max)
    factor_b = jnp.exp(max_b - new_max)
    return (
        new_max,
        sum_a * factor_a + sum_b * factor_b,
        acc_a * factor_a[..., None] + acc_b * factor_b[..., None],
    )


def request_stats(
    q_lat, q_rope, pre_lat, pre_rope, suf_lat, suf_rope, is_live, softmax_scale, with_prefix
):
    suf_scores = jnp.einsum("bhl,bsl->bhs", q_lat, suf_lat, preferred_element_type=jnp.float32)
    suf_scores = (
        suf_scores
        + jnp.einsum("bhr,brs->bhs", q_rope, suf_rope, preferred_element_type=jnp.float32)
    ) * softmax_scale
    row_max = jnp.max(suf_scores, axis=2)
    beam_count, head_count, lat_width = q_lat.shape
    flat_lat = q_lat.reshape(beam_count * head_count, lat_width)
    flat_rope = q_rope.reshape(beam_count * head_count, q_rope.shape[2])
    pre_scores = lax.dot_general(
        flat_lat, pre_lat, (((1,), (1,)), ((), ())), preferred_element_type=jnp.float32
    )
    pre_scores = pre_scores + jnp.dot(flat_rope, pre_rope, preferred_element_type=jnp.float32)
    pre_scores = jnp.where(is_live[None, :], pre_scores * softmax_scale, NEG).reshape(
        beam_count, head_count, -1
    )
    row_max = jnp.maximum(row_max, jnp.max(pre_scores, axis=2))
    suf_weights = jnp.exp(suf_scores - row_max[..., None]).astype(jnp.bfloat16)
    weight_sum = jnp.sum(suf_weights.astype(jnp.float32), axis=2)
    weighted = jnp.einsum("bhs,bsl->bhl", suf_weights, suf_lat, preferred_element_type=jnp.float32)
    pre_weights = jnp.exp(pre_scores - row_max[..., None]).astype(jnp.bfloat16)
    weight_sum = weight_sum + jnp.sum(pre_weights.astype(jnp.float32), axis=2)
    prefix_part = jnp.dot(
        pre_weights.reshape(beam_count * head_count, -1),
        pre_lat,
        preferred_element_type=jnp.float32,
    )
    weighted = weighted + prefix_part.reshape(beam_count, head_count, lat_width)
    return (row_max, weight_sum, weighted)


def general_local(
    query_latent,
    query_rope,
    cache_latent,
    cache_rope,
    suffix_latent,
    suffix_rope,
    lengths,
    parents,
    w_uv,
    w_o,
    hidden,
    norm_gain,
    w_gate,
    w_up,
    w_down,
    expert_ids,
    gate_weights,
):
    q_lat, q_rope = (
        lax.all_gather(query_latent, "hx", axis=1, tiled=True),
        lax.all_gather(query_rope, "hx", axis=1, tiled=True),
    )
    head_count = q_lat.shape[1]
    q_rope = q_rope.reshape(HYPS, head_count, DR)
    softmax_scale = MSCALE * MSCALE / math.sqrt(DN + DR)
    n_hx = lax.axis_size("hx")
    linear = lax.axis_index("ctx") * n_hx + lax.axis_index("hx")
    ctx_block = cache_latent.shape[1]
    offsets = linear * ctx_block + jnp.arange(ctx_block, dtype=jnp.int32)
    suf_lat = jnp.take(suffix_latent, parents, axis=0)
    suf_rope = jnp.take(suffix_rope, parents, axis=0)
    maxima = []
    totals_list = []
    sums_list = []
    for request in range(REQ):
        hyp_rows = slice(request * BEAMS, (request + 1) * BEAMS)
        is_live = offsets < lengths[request]
        bound_stats = partial(
            request_stats,
            q_lat[hyp_rows],
            q_rope[hyp_rows],
            cache_latent[request],
            cache_rope[request],
            suf_lat[hyp_rows],
            suf_rope[hyp_rows],
            is_live,
            softmax_scale,
        )
        request_sums = bound_stats(True)
        maxima.append(request_sums[0])
        totals_list.append(request_sums[1])
        sums_list.append(request_sums[2])
    row_max = jnp.concatenate(maxima, axis=0)
    weight_sum = jnp.concatenate(totals_list, axis=0)
    weighted = jnp.concatenate(sums_list, axis=0)
    part_max, part_sum, part_acc = (
        lax.all_to_all(row_max[None], "ctx", split_axis=2, concat_axis=0, tiled=True),
        lax.all_to_all(weight_sum[None], "ctx", split_axis=2, concat_axis=0, tiled=True),
        lax.all_to_all(weighted[None], "ctx", split_axis=2, concat_axis=0, tiled=True),
    )
    group_max = jnp.max(part_max, axis=0)
    factor = jnp.exp(part_max - group_max[None])
    group_sum = jnp.sum(part_sum * factor, axis=0)
    group_acc = jnp.sum(part_acc * factor[..., None], axis=0)
    group_max, group_sum, group_acc = merged((group_max, group_sum, group_acc), "hx", merge_pair)
    attention = (group_acc / group_sum[..., None]).astype(jnp.bfloat16)
    columns = w_uv.shape[1]
    head_span = max(1, columns // DV)
    first_head = lax.axis_index("hx") * columns // DV
    chosen = lax.dynamic_slice_in_dim(attention, first_head, head_span, 1)
    value_map = w_uv.reshape(DL, head_span, columns // head_span)
    values = jnp.einsum("bnl,lnc->bnc", chosen, value_map, preferred_element_type=jnp.float32)
    values = values.astype(jnp.bfloat16).reshape(HYPS, columns)
    partial_out = jnp.dot(values, w_o, preferred_element_type=jnp.float32)
    attended = lax.psum(partial_out, ("ctx", "hx")).astype(jnp.bfloat16)
    residual = hidden.astype(jnp.float32) + attended.astype(jnp.float32)
    mean_square = jnp.mean(residual * residual, axis=1, keepdims=True)
    normed = (residual * lax.rsqrt(mean_square + 1e-06) * norm_gain).astype(jnp.bfloat16)
    unit_count = w_gate.shape[0]
    expert_here = linear * unit_count // EFF
    routed = jnp.sum(gate_weights * (expert_ids == expert_here).astype(jnp.float32), axis=1)
    gate_out = lax.dot_general(
        normed, w_gate, (((1,), (1,)), ((), ())), preferred_element_type=jnp.float32
    )
    up_out = lax.dot_general(
        normed, w_up, (((1,), (1,)), ((), ())), preferred_element_type=jnp.float32
    )
    activated = (jax.nn.silu(gate_out) * up_out * routed[:, None]).astype(jnp.bfloat16)
    expert_terms = jnp.dot(activated, w_down, preferred_element_type=jnp.float32)
    moe_share = lax.psum_scatter(expert_terms, ("ctx", "hx"), scatter_dimension=1, tiled=True)
    share_width = moe_share.shape[1]
    residual_share = lax.dynamic_slice_in_dim(residual, linear * share_width, share_width, 1)
    updated = (residual_share + moe_share).astype(jnp.bfloat16)
    return (attended, updated)


BF = jnp.bfloat16
F32 = jnp.float32
AXES = ("z", "x", "y", "core")
SHAPE = (4, 2, 2, 2)
CORE, Y, X, Z0, Z1 = 1, 2, 4, 8, 16
HEADS_DEV = 4
UNITS = 256
STAT = 8
LANES = 128
PARENTS = REQ
AHEAD = 2
LOG2E = math.log2(math.e)
VMEM = pl.BlockSpec(memory_space=pltpu.VMEM)
SMEM = pl.BlockSpec(memory_space=pltpu.SMEM)
HBM = pl.BlockSpec(memory_space=pltpu.HBM)
NT = (((1,), (1,)), ((), ()))
EXCHANGE = pl.CostEstimate(flops=0, bytes_accessed=12 << 20, transcendentals=0)


def swap(value, mask):
    return lax.ppermute(value, AXES, [(i, i ^ mask) for i in range(math.prod(SHAPE))])


def in_hbm(value):
    return pltpu.with_memory_space_constraint(value, pltpu.HBM)


def bits(linear):
    return [linear >> k & 1 for k in range(5)]


def column(lane_row):
    n = lane_row.shape[1]
    at = lax.broadcasted_iota(jnp.int32, (n, n), 0)
    to = lax.broadcasted_iota(jnp.int32, (n, n), 1)
    return jnp.sum(jnp.where(at == to, lane_row, 0.0), axis=1, keepdims=True)


def stat_rows(lse):
    parts = []
    for _ in range(3):
        part = lse.astype(BF).astype(F32)
        parts.append(part)
        lse = lse - part
    return parts


def write_stat(out, body, parts, stat):
    stat[...] = jnp.zeros_like(stat)
    for i, part in enumerate(parts):
        stat[0:1, i * LANES:i * LANES + part.shape[1]] = part
    out[body:] = stat[...].astype(BF)


def read_stat(block, n):
    block = block.astype(F32)
    return (block[:1, :n] + block[:1, LANES:LANES + n]) + block[:1, 2 * LANES:2 * LANES + n]


def joined(lses):
    top = lses[0]
    for lse in lses[1:]:
        top = jnp.maximum(top, lse)
    weights = [jnp.exp(lse - top) for lse in lses]
    total = sum(weights[1:], weights[0])
    return [w / total for w in weights], top + jnp.log(total)


def attend_kernel(scale, fetch, info, ql0, ql1, qr0, qr1, cl_hbm, cr_hbm, sl_hbm, sr_hbm, keep, send0, send1,
                  spread, qbuf, rbuf, pbuf, wide, lse_buf, stat, cl, cr, sl, sr, own_q, own_r, sems):
    linear = lax.axis_index(AXES)
    core, y, x, z0, _ = bits(linear)
    heads = ql1.shape[1]
    rows = 2 * heads
    total_rows = BEAMS * rows
    targets = keep.shape[0]
    body = keep.shape[1] - STAT
    small = body // (2 * REQ)
    query_copies = []
    if fetch:
        query_copies = [pltpu.make_async_copy(qr0, own_r, sems.at[4, 0]),
                        pltpu.make_async_copy(ql0, own_q, sems.at[4, 1])]
        for copy in query_copies:
            copy.start()
    copies = []
    for r in range(REQ):
        beams = pl.ds(r * BEAMS, BEAMS)
        group = [
            pltpu.make_async_copy(cl_hbm.at[r], cl.at[r], sems.at[0, r]),
            pltpu.make_async_copy(cr_hbm.at[r], cr.at[r], sems.at[1, r]),
            pltpu.make_async_copy(sl_hbm.at[beams], sl.at[beams], sems.at[2, r]),
            pltpu.make_async_copy(sr_hbm.at[beams], sr.at[beams], sems.at[3, r]),
        ]
        copies.append(group)
        if r < AHEAD:
            for copy in group:
                copy.start()
    first_q, first_r = (own_q, own_r) if fetch else (ql0, qr0)

    out_row = lax.broadcasted_iota(jnp.int32, (total_rows, total_rows), 0)
    in_row = lax.broadcasted_iota(jnp.int32, (total_rows, total_rows), 1)

    def source_of(row):
        bit = lambda k: (row >> k) & 1
        beam, head = (row >> 2) & 3, row & 3
        target = (bit(6) ^ x) * 4 + (bit(5) ^ y) * 2 + (bit(7) ^ core)
        return beam * rows + (bit(4) ^ core ^ z0) * heads + target * HEADS_DEV + head

    spread[...] = jnp.where(source_of(out_row) == in_row, 1.0, 0.0).astype(BF)
    moves = source_of(in_row) == out_row
    messages = [keep.at[t] for t in range(targets)]
    messages += [send.at[t] for send in (send0, send1) for t in range(targets // 2)]
    lse_buf[...] = jnp.zeros_like(lse_buf)
    for copy in query_copies:
        copy.wait()
    wide[0] = first_r[...].astype(F32)
    wide[1] = qr1[...].astype(F32)
    per_group = LANES // DR
    head_row = lax.broadcasted_iota(jnp.int32, (heads, LANES), 0)
    own_lanes = lax.broadcasted_iota(jnp.int32, (heads, LANES), 1) // DR == head_row % per_group

    for r in range(REQ):
        for j in range(BEAMS):
            for piece, q in enumerate((first_q, ql1)):
                part = slice(j * rows + piece * heads, j * rows + (piece + 1) * heads)
                b = r * BEAMS + j
                qbuf[r, part] = q[b]
                unfolded = jnp.zeros((heads, LANES), F32)
                for g in range(heads // per_group):
                    lanes = wide[piece, b:b + 1, g * LANES:(g + 1) * LANES]
                    unfolded = jnp.where(head_row // per_group == g, lanes, unfolded)
                rbuf[r, part] = jnp.where(own_lanes, unfolded, 0.0).astype(BF)

    def scores(r):
        for copy in copies[r]:
            copy.wait()
        if r + AHEAD < REQ:
            for copy in copies[r + AHEAD]:
                copy.start()
        keys = cl[r]
        ctx_block = keys.shape[0]
        pre = lax.dot_general(qbuf[r], keys, NT, preferred_element_type=F32)
        pre = pre + jnp.dot(rbuf[r], jnp.concatenate([cr[r]] * per_group, axis=0), preferred_element_type=F32)
        position = linear * ctx_block + lax.broadcasted_iota(jnp.int32, (1, ctx_block), 1)
        pre = jnp.where(position < info[r], pre, NEG)
        own = [info[PARENTS + r * BEAMS + j] for j in range(BEAMS)]
        suf = []
        suf_keys = []
        for j in range(0, BEAMS, 2):
            part = slice(j * rows, (j + 2) * rows)
            pair_keys = jnp.concatenate([sl[own[j]], sl[own[j + 1]]], axis=0)
            pair_rope = jnp.concatenate([sr[own[j]], sr[own[j + 1]]], axis=1)
            s = lax.dot_general(qbuf[r, part], pair_keys, NT, preferred_element_type=F32)
            s = s + jnp.dot(rbuf[r, part], jnp.concatenate([pair_rope] * per_group, axis=0),
                            preferred_element_type=F32)
            n = s.shape[1] // 2
            suf += [s[:rows, :n], s[rows:, n:]]
            suf_keys.append(pair_keys)
        return pre, jnp.concatenate(suf, axis=0), suf_keys

    def finish(r, pre, suf, suf_keys):
        top = jnp.maximum(jnp.max(pre, axis=1, keepdims=True), jnp.max(suf, axis=1, keepdims=True))
        pre_w = jnp.exp2((pre - top) * (scale * LOG2E))
        suf_w = jnp.exp2((suf - top) * (scale * LOG2E))
        total = jnp.sum(pre_w, axis=1, keepdims=True) + jnp.sum(suf_w, axis=1, keepdims=True)
        pre_w, suf_w = pre_w.astype(BF), suf_w.astype(BF)
        acc = jnp.dot(pre_w, cl[r], preferred_element_type=F32)
        inv = 1.0 / total
        for j in range(0, BEAMS, 2):
            part = slice(j * rows, (j + 2) * rows)
            first, second = suf_w[j * rows:(j + 1) * rows], suf_w[(j + 1) * rows:(j + 2) * rows]
            none = jnp.zeros_like(first)
            spread_w = jnp.concatenate([jnp.concatenate([first, none], axis=1),
                                        jnp.concatenate([none, second], axis=1)], axis=0)
            a = acc[part] + jnp.dot(spread_w, suf_keys[j // 2], preferred_element_type=F32)
            pbuf[r, part] = (a * inv[part]).astype(BF)
        moved = jnp.dot(spread[...], pbuf[r], preferred_element_type=F32).astype(BF)
        lse = scale * top + jnp.log(total)
        lane_lse = jnp.sum(jnp.where(moves, lse, 0.0), axis=0, keepdims=True)
        for n, message in enumerate(messages):
            for zz in range(2):
                at = (2 * n + zz) * small
                to = (zz * REQ + r) * small
                message[to:to + small] = moved[at:at + small]
                lse_buf[n:n + 1, to:to + small] = lane_lse[:, at:at + small]

    now = scores(0)
    for r in range(REQ):
        later = scores(r + 1) if r + 1 < REQ else None
        finish(r, *now)
        now = later
    parts = stat_rows(lse_buf[...])
    for n, message in enumerate(messages):
        write_stat(message, body, [p[n:n + 1] for p in parts], stat)


def attend(scale, fetch, info, q_lat, q_rope, caches):
    heads, width = q_lat[0].shape[1:]
    total_rows = BEAMS * 2 * heads
    targets = SHAPE[1] * SHAPE[2]
    body = REQ * total_rows // (2 * targets)
    message = lambda n: jax.ShapeDtypeStruct((n, body + STAT, width), BF)
    keys = caches[0].shape[1] + caches[2].shape[1]
    own = [v.shape if fetch else (16, LANES) for v in (q_lat[0], q_rope[0])]
    first = [in_hbm(v) if fetch else v for v in (q_lat[0], q_rope[0])]
    spec = HBM if fetch else VMEM
    return pl.pallas_call(
        partial(attend_kernel, scale, fetch),
        in_specs=[SMEM, spec, VMEM, spec, VMEM] + [HBM] * 4,
        out_specs=[VMEM] * 3,
        out_shape=[message(targets), message(targets // 2), message(targets // 2)],
        scratch_shapes=[
            pltpu.VMEM((total_rows, total_rows), BF),
            pltpu.VMEM((REQ, total_rows, width), BF),
            pltpu.VMEM((REQ, total_rows, LANES), BF),
            pltpu.VMEM((REQ, total_rows, width), BF),
            pltpu.VMEM((2, *q_rope[0].shape), F32),
            pltpu.VMEM((2 * targets, body), F32),
            pltpu.VMEM((STAT, width), F32),
        ] + [pltpu.VMEM(c.shape, BF) for c in caches]
        + [pltpu.VMEM(shape, BF) for shape in own] + [pltpu.SemaphoreType.DMA((5, REQ))],
        compiler_params=pltpu.CompilerParams(vmem_limit_bytes=14 << 20),
        cost_estimate=pl.CostEstimate(
            flops=REQ * 2 * total_rows * keys * (2 * width + DR), bytes_accessed=8 << 20,
            transcendentals=REQ * total_rows * keys),
        name="attend",
    )(info, first[0], q_lat[1], first[1], q_rope[1], *(in_hbm(c) for c in caches))


def pair_kernel(count, a, *refs):
    got, outs, stat = refs[:count], refs[count:-1], refs[-1]
    targets, rows, _ = a.shape
    body = rows - STAT
    for t in range(targets):
        ours, theirs = a.at[t], got[t // (targets // count)].at[t % (targets // count)]
        out = outs[t // (targets // len(outs))].at[t % (targets // len(outs))]
        weights, lse = joined([read_stat(v[body:], body) for v in (ours, theirs)])
        out[:body] = (ours[:body].astype(F32) * column(weights[0])
                      + theirs[:body].astype(F32) * column(weights[1])).astype(BF)
        write_stat(out, body, stat_rows(lse), stat)


def merge_pairs(a, got, parts):
    return pl.pallas_call(
        partial(pair_kernel, len(got)),
        in_specs=[VMEM] * (1 + len(got)),
        out_specs=[VMEM] * parts,
        out_shape=[jax.ShapeDtypeStruct((a.shape[0] // parts, *a.shape[1:]), BF)] * parts,
        scratch_shapes=[pltpu.VMEM((STAT, a.shape[2]), F32)],
        compiler_params=pltpu.CompilerParams(vmem_limit_bytes=4 << 20),
        cost_estimate=pl.CostEstimate(flops=4 * a.size, bytes_accessed=6 * a.size, transcendentals=0),
        name="merge_pairs",
    )(a, *got)


def plane_kernel(count, *refs):
    groups = refs[:count], refs[count:2 * count]
    outs, (stat, held) = refs[2 * count:-2], refs[-2:]
    body = refs[0].shape[1] - STAT
    small = body // 2
    _, y, _, _, z1 = bits(lax.axis_index(AXES))
    for other, sources in enumerate(groups):
        weights, lse = joined([read_stat(ref[0, body:], body) for ref in sources])
        parts = stat_rows(lse)
        columns = [column(w) for w in weights]
        for z0 in range(2):
            part = slice(z0 * small, (z0 + 1) * small)
            total = None
            for ref, w in zip(sources, columns):
                term = ref[0, part].astype(F32) * w[part]
                total = term if total is None else total + term
            held[2 * other + z0, :small] = total.astype(BF)
            write_stat(held.at[2 * other + z0], small, [p[:, part] for p in parts], stat)
    for d, out in enumerate(outs):
        out[...] = held[2 * ((d >> 1) ^ y ^ z1) + (d & 1)]


def merge_plane(same, other):
    _, rows, width = same[0].shape
    shape = ((rows - STAT) // 2 + STAT, width)
    return pl.pallas_call(
        partial(plane_kernel, len(same)),
        in_specs=[VMEM] * 2 * len(same),
        out_specs=[VMEM] * SHAPE[0],
        out_shape=[jax.ShapeDtypeStruct(shape, BF)] * SHAPE[0],
        scratch_shapes=[pltpu.VMEM((STAT, width), F32), pltpu.VMEM((SHAPE[0], *shape), BF)],
        compiler_params=pltpu.CompilerParams(vmem_limit_bytes=4 << 20),
        cost_estimate=pl.CostEstimate(flops=16 * rows * width, bytes_accessed=24 * rows * width, transcendentals=0),
        name="merge_plane",
    )(*same, *other)


def sum_kernel(count, *refs):
    ins, outs = refs[:count], refs[count:]
    for i, out in enumerate(outs):
        terms = [(ref[...] if len(outs) == 1 else ref[i]).astype(F32) for ref in ins]
        while len(terms) > 1:
            terms = [a + b for a, b in zip(terms[::2], terms[1::2])]
        out[...] = terms[0].astype(BF)


def sums(arrays, split):
    count, shape = len(arrays), arrays[0].shape
    outs = [shape[1:]] * shape[0] if split else [shape]
    return pl.pallas_call(
        partial(sum_kernel, count),
        in_specs=[VMEM] * count,
        out_specs=[VMEM] * len(outs),
        out_shape=[jax.ShapeDtypeStruct(out, BF) for out in outs],
        compiler_params=pltpu.CompilerParams(vmem_limit_bytes=4 << 20),
        cost_estimate=EXCHANGE,
        name="sums",
    )(*arrays)


def project_kernel(p0, p1, p2, p3, w_uv, w_o, keep, send):
    parts = (p0, p1, p2, p3)
    rows, _ = p0.shape
    body = rows - STAT
    weights, _ = joined([read_stat(p[body:], body) for p in parts])
    total = None
    for p, w in zip(parts, weights):
        term = p[:body].astype(F32) * column(w)
        total = term if total is None else total + term
    full = jnp.dot(total.astype(BF), w_uv[...], preferred_element_type=F32)
    rows, columns = full.shape
    row = lax.broadcasted_iota(jnp.int32, (rows, columns), 0)
    lane = lax.broadcasted_iota(jnp.int32, (rows, columns), 1)
    own = jnp.where((row & (HEADS_DEV - 1)) == lane // DV, full, 0.0).astype(BF)
    pick_hyp = lax.broadcasted_iota(jnp.int32, (HYPS, rows), 0)
    pick_row = lax.broadcasted_iota(jnp.int32, (HYPS, rows), 1)
    pick = jnp.where(pick_row // HEADS_DEV == pick_hyp, 1.0, 0.0).astype(BF)
    values = jnp.dot(pick, own, preferred_element_type=F32).astype(BF)
    width = keep.shape[2]
    plane = lax.axis_index(AXES) & 7
    for there, out in enumerate((keep, send)):
        for t in range(out.shape[0]):
            at = pl.multiple_of((plane ^ (2 * t + there)) * width, LANES)
            piece = jnp.dot(values, w_o[:, pl.ds(at, width)], preferred_element_type=F32)
            out[t] = piece.astype(BF)


def project(parts, w_uv, w_o):
    squares = SHAPE[1] * SHAPE[2]
    out = jax.ShapeDtypeStruct((squares, HYPS, w_o.shape[1] // (2 * squares)), BF)
    return pl.pallas_call(
        project_kernel,
        in_specs=[VMEM] * 6,
        out_specs=[VMEM] * 2,
        out_shape=[out] * 2,
        compiler_params=pltpu.CompilerParams(vmem_limit_bytes=4 << 20),
        cost_estimate=pl.CostEstimate(flops=2 * HYPS * w_o.size, bytes_accessed=2 * w_o.size, transcendentals=0),
        name="project",
    )(*parts, w_uv, w_o)


def core_sum_kernel(a, b, out):
    chip = lax.axis_index(AXES) >> 1
    square, depth = chip & 3, chip >> 2
    for t in range(a.shape[0]):
        for z in range(a.shape[1]):
            out[(depth ^ z) * a.shape[0] + (square ^ t)] = (a[t, z].astype(F32) + b[t, z].astype(F32)).astype(BF)


def core_sum(a, b):
    squares, depth, *tail = a.shape
    return pl.pallas_call(
        core_sum_kernel,
        in_specs=[VMEM] * 2,
        out_specs=VMEM,
        out_shape=jax.ShapeDtypeStruct((squares * depth, *tail), BF),
        compiler_params=pltpu.CompilerParams(vmem_limit_bytes=4 << 20),
        cost_estimate=EXCHANGE,
        name="core_sum",
    )(a, b)


def load_kernel(count, *refs):
    sources, dests, sems = refs[:count], refs[count + 1:-1], refs[-1]
    copies = [pltpu.make_async_copy(sources[i], dests[i], sems.at[i]) for i in range(count)]
    for copy in copies:
        copy.start()
    for copy in copies:
        copy.wait()


def load(after, *arrays):
    count = len(arrays)
    return pl.pallas_call(
        partial(load_kernel, count),
        in_specs=[HBM] * count + [pl.BlockSpec(memory_space=pl.ANY)],
        out_specs=[VMEM] * count,
        out_shape=[pltpu.VMEM(a.shape, a.dtype) for a in arrays],
        scratch_shapes=[pltpu.SemaphoreType.DMA((count,))],
        compiler_params=pltpu.CompilerParams(vmem_limit_bytes=1 << 20),
        cost_estimate=pl.CostEstimate(
            flops=0, bytes_accessed=sum(2 * a.size for a in arrays), transcendentals=0),
        name="load",
    )(*(in_hbm(a) for a in arrays), after)


def experts_kernel(*refs):
    shares, (hidden, gain, ids, gates, w_gate, w_up, down_hbm) = refs[:8], refs[8:15]
    attended, keep, send, residual, x_buf, acc, x_held, w_down, sems = refs[15:]
    units = w_gate.shape[0]
    chunks = units // UNITS
    parts = [slice(k * UNITS, (k + 1) * UNITS) for k in range(chunks)]
    downs = [pltpu.make_async_copy(down_hbm.at[pl.ds(k * UNITS, UNITS)], w_down.at[pl.ds(k * UNITS, UNITS)],
                                   sems.at[k]) for k in range(chunks)]
    for copy in downs:
        copy.start()
    linear = lax.axis_index(AXES)
    plane, depth = linear & 7, linear >> 3
    share = shares[0].shape[1]
    for d, ref in enumerate(shares):
        at = pl.multiple_of((plane ^ d) * share, LANES)
        x_buf[:, pl.ds(at, share)] = ref[...].astype(F32)
        attended[:, pl.ds(at, share)] = ref[...]
    x = x_buf[...] + hidden[...].astype(F32)
    mean_square = jnp.mean(x * x, axis=1, keepdims=True)
    normed = (x * lax.rsqrt(mean_square + 1e-06) * gain[...]).astype(BF)
    expert = linear * units // EFF
    routed = column(jnp.sum(jnp.where(ids[...] == expert, gates[...], 0.0), axis=0, keepdims=True))
    count, _, width = x_held.shape
    for d in range(count):
        x_held[d] = x[:, d * width:(d + 1) * width]
    residual[...] = x_held[linear]
    gate = [lax.dot_general(normed, w_gate[part], NT, preferred_element_type=F32) for part in parts]
    gate = [g / (1.0 + jnp.exp(-g)) * routed for g in gate]
    act = []
    for k, part in enumerate(parts):
        up = lax.dot_general(normed, w_up[part], NT, preferred_element_type=F32)
        act.append((gate[k] * up).astype(BF))
    for k, part in enumerate(parts):
        downs[k].wait()
        term = jnp.dot(act[k], w_down[part], preferred_element_type=F32)
        if k == 0:
            acc[...] = term
        else:
            acc[...] += term
    core = linear & CORE
    for d in range(0, count, 2):
        pair = [acc[:, (d + i) * width:(d + i + 1) * width].astype(BF) for i in range(2)]
        at = ((d >> 1) ^ (linear >> 1)) & 3, depth ^ (d >> 3)
        keep[at] = jnp.where(core == 1, pair[1], pair[0])
        send[at] = jnp.where(core == 1, pair[0], pair[1])


def experts(shares, hidden, gain, ids, gates, w_gate, w_up, w_down):
    units, width = w_gate.shape
    count = math.prod(SHAPE)
    small = width // count
    terms = jax.ShapeDtypeStruct((SHAPE[1] * SHAPE[2], SHAPE[0], HYPS, small), BF)
    return pl.pallas_call(
        experts_kernel,
        in_specs=[VMEM] * 14 + [HBM],
        out_specs=[VMEM] * 4,
        out_shape=[
            jax.ShapeDtypeStruct((HYPS, width), BF), terms, terms,
            jax.ShapeDtypeStruct((HYPS, small), F32),
        ],
        scratch_shapes=[pltpu.VMEM((HYPS, width), F32)] * 2 + [
            pltpu.VMEM((count, HYPS, small), F32),
            pltpu.VMEM((units, width), BF),
            pltpu.SemaphoreType.DMA((units // UNITS,)),
        ],
        compiler_params=pltpu.CompilerParams(vmem_limit_bytes=18 << 20),
        cost_estimate=pl.CostEstimate(flops=6 * HYPS * units * width, bytes_accessed=6 * units * width,
                                      transcendentals=HYPS * units),
        name="experts",
    )(*shares, hidden, gain, ids, gates, w_gate, w_up, in_hbm(w_down))


def local(
    query_latent,
    query_rope,
    cache_latent,
    cache_rope,
    suffix_latent,
    suffix_rope,
    lengths,
    parents,
    w_uv,
    w_o,
    hidden,
    norm_gain,
    w_gate,
    w_up,
    w_down,
    expert_ids,
    gate_weights,
):
    scale = MSCALE * MSCALE / math.sqrt(DN + DR)
    info = jnp.concatenate([lengths, parents])
    caches = (cache_latent, cache_rope, suffix_latent, suffix_rope)
    tied = lax.optimization_barrier
    square, line = (Y, X, X ^ Y), (Z0 ^ Z1, Z1, Z0)

    near_lat, near_rope = swap(query_latent, CORE), swap(query_rope, CORE)
    far_lat, far_rope = swap(query_latent, Y), swap(query_rope, Y)
    keep, *send = attend(scale, True, info, (query_latent, near_lat), (query_rope, near_rope), caches)
    near = merge_pairs(keep, [swap(v, CORE) for v in send], 2)
    far_lat, far_rope, near = tied((far_lat, far_rope, near))
    near_x = swap(near[1], X)
    far_lat, far_rope = (far_lat, swap(far_lat, CORE)), (far_rope, swap(far_rope, CORE))
    keep, *send = attend(scale, False, info, far_lat, far_rope, caches)
    keep, send, near_x = tied((keep, send, near_x))
    near = merge_pairs(near[0], [near_x], 2)
    near_y = swap(near[1], Y)
    far = merge_pairs(keep, [swap(v, CORE) for v in send], len(square) + 1)
    far_xy, far_x, far_y = swap(far[3], X ^ Y), swap(far[2], X), swap(far[1], Y)
    parts = merge_plane((near[0], far_y, far_xy), (near_y, far[0], far_x))
    w_uv, w_o = load(parts[0], w_uv, w_o)
    parts = [parts[0], *(swap(v, mask) for v, mask in zip(parts[:0:-1], line))]
    keep, send = project(parts, w_uv, w_o)

    pieces = sums([keep, swap(send, CORE)], True)
    share, = sums([pieces[0], *(swap(v, mask) for v, mask in zip(pieces[:0:-1], square[::-1]))], False)
    share, = sums([share, *(swap(share, mask) for mask in line[::-1])], False)
    shares = [share, *(swap(share, mask) for mask in square)]
    shares = [v for pair in zip(shares, [swap(v, CORE) for v in shares]) for v in pair]
    attended, keep, send, residual = experts(
        shares, hidden, norm_gain.reshape(1, -1), expert_ids.T, gate_weights.T, w_gate, w_up, w_down)

    total = core_sum(keep, swap(send, CORE))
    total = lax.all_to_all(total, AXES[:3], split_axis=0, concat_axis=0, tiled=True)
    updated = (residual + jnp.sum(total.astype(F32), axis=0)).astype(BF)
    return (attended, updated)


def solution(mesh):
    if mesh.shape["ctx"] == SHAPE[0] * SHAPE[1] and mesh.shape["hx"] == SHAPE[2] * SHAPE[3]:
        chosen, names = local, AXES
        mesh = jax.sharding.Mesh(mesh.devices.reshape(SHAPE), AXES)
    else:
        chosen, names = general_local, ("ctx", "hx")
    all_axes, hx = names, names[len(names) // 2:]
    in_specs = (
        P(None, hx, None),
        P(None, hx),
        P(None, all_axes, None),
        P(None, None, all_axes),
        P(None, all_axes, None),
        P(None, None, all_axes),
        P(),
        P(),
        P(None, all_axes),
        P(all_axes, None),
        P(),
        P(),
        P(all_axes, None),
        P(all_axes, None),
        P(all_axes, None),
        P(),
        P(),
    )
    out_specs = (P(), P(None, all_axes))
    return jax.shard_map(chosen, mesh=mesh, in_specs=in_specs, out_specs=out_specs, check_vma=False)
```

```python
from functools import partial
import math

import jax
import jax.numpy as jnp
from jax import lax
from jax.experimental import pallas as pl
from jax.experimental.pallas import tpu as pltpu
from jax.sharding import PartitionSpec as P

DL = 512
DR = 64
DN = 128
DV = 128
EFF = 2048
REQ = 4
BEAMS = 4
HYPS = 16


MSCALE = 1.0 + 0.1 * math.log(40.0)
NEG = -1e30


def merged(value, axis, join):
    pieces = jax.tree.map(lambda part: lax.all_gather(part, axis), value)
    head = jax.tree.map(lambda part: part[0], pieces)
    tail = jax.tree.map(lambda part: part[1:], pieces)
    subtotal, _ = lax.scan(lambda subtotal, section: (join(subtotal, section), None), head, tail)
    return subtotal


def merge_pair(first_set, second_set):
    max_a, sum_a, acc_a = first_set
    max_b, sum_b, acc_b = second_set
    new_max = jnp.maximum(max_a, max_b)
    factor_a = jnp.exp(max_a - new_max)
    factor_b = jnp.exp(max_b - new_max)
    return (
        new_max,
        sum_a * factor_a + sum_b * factor_b,
        acc_a * factor_a[..., None] + acc_b * factor_b[..., None],
    )


def request_stats(
    q_lat, q_rope, pre_lat, pre_rope, suf_lat, suf_rope, is_live, softmax_scale, with_prefix
):
    suf_scores = jnp.einsum("bhl,bsl->bhs", q_lat, suf_lat, preferred_element_type=jnp.float32)
    suf_scores = (
        suf_scores
        + jnp.einsum("bhr,brs->bhs", q_rope, suf_rope, preferred_element_type=jnp.float32)
    ) * softmax_scale
    row_max = jnp.max(suf_scores, axis=2)
    beam_count, head_count, lat_width = q_lat.shape
    flat_lat = q_lat.reshape(beam_count * head_count, lat_width)
    flat_rope = q_rope.reshape(beam_count * head_count, q_rope.shape[2])
    pre_scores = lax.dot_general(
        flat_lat, pre_lat, (((1,), (1,)), ((), ())), preferred_element_type=jnp.float32
    )
    pre_scores = pre_scores + jnp.dot(flat_rope, pre_rope, preferred_element_type=jnp.float32)
    pre_scores = jnp.where(is_live[None, :], pre_scores * softmax_scale, NEG).reshape(
        beam_count, head_count, -1
    )
    row_max = jnp.maximum(row_max, jnp.max(pre_scores, axis=2))
    suf_weights = jnp.exp(suf_scores - row_max[..., None]).astype(jnp.bfloat16)
    weight_sum = jnp.sum(suf_weights.astype(jnp.float32), axis=2)
    weighted = jnp.einsum("bhs,bsl->bhl", suf_weights, suf_lat, preferred_element_type=jnp.float32)
    pre_weights = jnp.exp(pre_scores - row_max[..., None]).astype(jnp.bfloat16)
    weight_sum = weight_sum + jnp.sum(pre_weights.astype(jnp.float32), axis=2)
    prefix_part = jnp.dot(
        pre_weights.reshape(beam_count * head_count, -1),
        pre_lat,
        preferred_element_type=jnp.float32,
    )
    weighted = weighted + prefix_part.reshape(beam_count, head_count, lat_width)
    return (row_max, weight_sum, weighted)


def general_local(
    query_latent,
    query_rope,
    cache_latent,
    cache_rope,
    suffix_latent,
    suffix_rope,
    lengths,
    parents,
    w_uv,
    w_o,
    hidden,
    norm_gain,
    w_gate,
    w_up,
    w_down,
    expert_ids,
    gate_weights,
):
    q_lat, q_rope = (
        lax.all_gather(query_latent, "hx", axis=1, tiled=True),
        lax.all_gather(query_rope, "hx", axis=1, tiled=True),
    )
    head_count = q_lat.shape[1]
    q_rope = q_rope.reshape(HYPS, head_count, DR)
    softmax_scale = MSCALE * MSCALE / math.sqrt(DN + DR)
    n_hx = lax.axis_size("hx")
    linear = lax.axis_index("ctx") * n_hx + lax.axis_index("hx")
    ctx_block = cache_latent.shape[1]
    offsets = linear * ctx_block + jnp.arange(ctx_block, dtype=jnp.int32)
    suf_lat = jnp.take(suffix_latent, parents, axis=0)
    suf_rope = jnp.take(suffix_rope, parents, axis=0)
    maxima = []
    totals_list = []
    sums_list = []
    for request in range(REQ):
        hyp_rows = slice(request * BEAMS, (request + 1) * BEAMS)
        is_live = offsets < lengths[request]
        bound_stats = partial(
            request_stats,
            q_lat[hyp_rows],
            q_rope[hyp_rows],
            cache_latent[request],
            cache_rope[request],
            suf_lat[hyp_rows],
            suf_rope[hyp_rows],
            is_live,
            softmax_scale,
        )
        request_sums = bound_stats(True)
        maxima.append(request_sums[0])
        totals_list.append(request_sums[1])
        sums_list.append(request_sums[2])
    row_max = jnp.concatenate(maxima, axis=0)
    weight_sum = jnp.concatenate(totals_list, axis=0)
    weighted = jnp.concatenate(sums_list, axis=0)
    part_max, part_sum, part_acc = (
        lax.all_to_all(row_max[None], "ctx", split_axis=2, concat_axis=0, tiled=True),
        lax.all_to_all(weight_sum[None], "ctx", split_axis=2, concat_axis=0, tiled=True),
        lax.all_to_all(weighted[None], "ctx", split_axis=2, concat_axis=0, tiled=True),
    )
    group_max = jnp.max(part_max, axis=0)
    factor = jnp.exp(part_max - group_max[None])
    group_sum = jnp.sum(part_sum * factor, axis=0)
    group_acc = jnp.sum(part_acc * factor[..., None], axis=0)
    group_max, group_sum, group_acc = merged((group_max, group_sum, group_acc), "hx", merge_pair)
    attention = (group_acc / group_sum[..., None]).astype(jnp.bfloat16)
    columns = w_uv.shape[1]
    head_span = max(1, columns // DV)
    first_head = lax.axis_index("hx") * columns // DV
    chosen = lax.dynamic_slice_in_dim(attention, first_head, head_span, 1)
    value_map = w_uv.reshape(DL, head_span, columns // head_span)
    values = jnp.einsum("bnl,lnc->bnc", chosen, value_map, preferred_element_type=jnp.float32)
    values = values.astype(jnp.bfloat16).reshape(HYPS, columns)
    partial_out = jnp.dot(values, w_o, preferred_element_type=jnp.float32)
    attended = lax.psum(partial_out, ("ctx", "hx")).astype(jnp.bfloat16)
    residual = hidden.astype(jnp.float32) + attended.astype(jnp.float32)
    mean_square = jnp.mean(residual * residual, axis=1, keepdims=True)
    normed = (residual * lax.rsqrt(mean_square + 1e-06) * norm_gain).astype(jnp.bfloat16)
    unit_count = w_gate.shape[0]
    expert_here = linear * unit_count // EFF
    routed = jnp.sum(gate_weights * (expert_ids == expert_here).astype(jnp.float32), axis=1)
    gate_out = lax.dot_general(
        normed, w_gate, (((1,), (1,)), ((), ())), preferred_element_type=jnp.float32
    )
    up_out = lax.dot_general(
        normed, w_up, (((1,), (1,)), ((), ())), preferred_element_type=jnp.float32
    )
    activated = (jax.nn.silu(gate_out) * up_out * routed[:, None]).astype(jnp.bfloat16)
    expert_terms = jnp.dot(activated, w_down, preferred_element_type=jnp.float32)
    moe_share = lax.psum_scatter(expert_terms, ("ctx", "hx"), scatter_dimension=1, tiled=True)
    share_width = moe_share.shape[1]
    residual_share = lax.dynamic_slice_in_dim(residual, linear * share_width, share_width, 1)
    updated = (residual_share + moe_share).astype(jnp.bfloat16)
    return (attended, updated)


BF = jnp.bfloat16
F32 = jnp.float32
AXES = ("z", "x", "y", "core")
SHAPE = (4, 2, 2, 2)
CORE, Y, X, Z0, Z1 = 1, 2, 4, 8, 16
HEADS_DEV = 4
UNITS = 512
STAT = 8
LANES = 128
PARENTS = REQ
AHEAD = 2
LOG2E = math.log2(math.e)
VMEM = pl.BlockSpec(memory_space=pltpu.VMEM)
SMEM = pl.BlockSpec(memory_space=pltpu.SMEM)
HBM = pl.BlockSpec(memory_space=pltpu.HBM)
NT = (((1,), (1,)), ((), ()))
EXCHANGE = pl.CostEstimate(flops=0, bytes_accessed=12 << 20, transcendentals=0)


def swap(value, mask):
    return lax.ppermute(value, AXES, [(i, i ^ mask) for i in range(math.prod(SHAPE))])


def in_hbm(value):
    return pltpu.with_memory_space_constraint(value, pltpu.HBM)


def bits(linear):
    return [linear >> k & 1 for k in range(5)]


def column(lane_row):
    n = lane_row.shape[1]
    at = lax.broadcasted_iota(jnp.int32, (n, n), 0)
    to = lax.broadcasted_iota(jnp.int32, (n, n), 1)
    return jnp.sum(jnp.where(at == to, lane_row, 0.0), axis=1, keepdims=True)


def stat_rows(lse):
    parts = []
    for _ in range(3):
        part = lse.astype(BF).astype(F32)
        parts.append(part)
        lse = lse - part
    return parts


def write_stat(out, body, parts, stat):
    stat[...] = jnp.zeros_like(stat)
    for i, part in enumerate(parts):
        stat[0:1, i * LANES:i * LANES + part.shape[1]] = part
    out[body:] = stat[...].astype(BF)


def read_stat(block, n):
    block = block.astype(F32)
    return (block[:1, :n] + block[:1, LANES:LANES + n]) + block[:1, 2 * LANES:2 * LANES + n]


def joined(lses):
    top = lses[0]
    for lse in lses[1:]:
        top = jnp.maximum(top, lse)
    weights = [jnp.exp(lse - top) for lse in lses]
    total = sum(weights[1:], weights[0])
    return [w / total for w in weights], top + jnp.log(total)


def attend_kernel(scale, fetch, info, ql0, ql1, qr0, qr1, cl_hbm, cr_hbm, sl_hbm, sr_hbm, keep, send0, send1,
                  spread, qbuf, rbuf, pbuf, wide, lse_buf, stat, cl, cr, sl, sr, own_q, own_r, sems):
    linear = lax.axis_index(AXES)
    core, y, x, z0, _ = bits(linear)
    heads = ql1.shape[1]
    rows = 2 * heads
    total_rows = BEAMS * rows
    targets = keep.shape[0]
    body = keep.shape[1] - STAT
    small = body // (2 * REQ)
    query_copies = []
    if fetch:
        query_copies = [pltpu.make_async_copy(qr0, own_r, sems.at[4, 0]),
                        pltpu.make_async_copy(ql0, own_q, sems.at[4, 1])]
        for copy in query_copies:
            copy.start()
    copies = []
    for r in range(REQ):
        beams = pl.ds(r * BEAMS, BEAMS)
        group = [
            pltpu.make_async_copy(cl_hbm.at[r], cl.at[r], sems.at[0, r]),
            pltpu.make_async_copy(cr_hbm.at[r], cr.at[r], sems.at[1, r]),
            pltpu.make_async_copy(sl_hbm.at[beams], sl.at[beams], sems.at[2, r]),
            pltpu.make_async_copy(sr_hbm.at[beams], sr.at[beams], sems.at[3, r]),
        ]
        copies.append(group)
        if r < AHEAD:
            for copy in group:
                copy.start()
    first_q, first_r = (own_q, own_r) if fetch else (ql0, qr0)

    down = lax.broadcasted_iota(jnp.int32, (total_rows, 1), 0)
    along = lax.broadcasted_iota(jnp.int32, (1, total_rows), 1)

    def source_of(row):
        bit = lambda k: (row >> k) & 1
        beam, head = (row >> 2) & 3, row & 3
        target = (bit(6) ^ x) * 4 + (bit(5) ^ y) * 2 + (bit(7) ^ core)
        return beam * rows + (bit(4) ^ core ^ z0) * heads + target * HEADS_DEV + head

    spread[...] = jnp.where(source_of(down) == along, 1.0, 0.0).astype(BF)
    moves = source_of(along) == down
    messages = [keep.at[t] for t in range(targets)]
    messages += [send.at[t] for send in (send0, send1) for t in range(targets // 2)]
    lse_buf[...] = jnp.zeros_like(lse_buf)
    for copy in query_copies:
        copy.wait()
    wide[0] = first_r[...].astype(F32)
    wide[1] = qr1[...].astype(F32)
    per_group = LANES // DR
    block = 8
    row8 = lax.broadcasted_iota(jnp.int32, (block, LANES), 0)
    own_lanes = lax.broadcasted_iota(jnp.int32, (block, LANES), 1) // DR == row8 % per_group
    for r in range(REQ):
        for j in range(BEAMS):
            for piece, q in enumerate((first_q, ql1)):
                part = slice(j * rows + piece * heads, j * rows + (piece + 1) * heads)
                b = r * BEAMS + j
                qbuf[r, part] = q[b]
                unfolded = []
                for top in range(0, heads, block):
                    rows8 = jnp.zeros((block, LANES), F32)
                    for g in range(block // per_group):
                        at = (top // per_group + g) * LANES
                        rows8 = jnp.where(row8 // per_group == g, wide[piece, b:b + 1, at:at + LANES], rows8)
                    unfolded.append(jnp.where(own_lanes, rows8, 0.0))
                rbuf[r, part] = jnp.concatenate(unfolded, axis=0).astype(BF)

    def scores(r):
        for copy in copies[r]:
            copy.wait()
        if r + AHEAD < REQ:
            for copy in copies[r + AHEAD]:
                copy.start()
        keys = cl[r]
        ctx_block = keys.shape[0]
        pre = lax.dot_general(qbuf[r], keys, NT, preferred_element_type=F32)
        pre = pre + jnp.dot(rbuf[r], jnp.concatenate([cr[r]] * per_group, axis=0), preferred_element_type=F32)
        position = linear * ctx_block + lax.broadcasted_iota(jnp.int32, (1, ctx_block), 1)
        pre = jnp.where(position < info[r], pre, NEG)
        own = [info[PARENTS + r * BEAMS + j] for j in range(BEAMS)]
        suf = []
        suf_keys = []
        for j in range(0, BEAMS, 2):
            part = slice(j * rows, (j + 2) * rows)
            pair_keys = jnp.concatenate([sl[own[j]], sl[own[j + 1]]], axis=0)
            pair_rope = jnp.concatenate([sr[own[j]], sr[own[j + 1]]], axis=1)
            s = lax.dot_general(qbuf[r, part], pair_keys, NT, preferred_element_type=F32)
            s = s + jnp.dot(rbuf[r, part], jnp.concatenate([pair_rope] * per_group, axis=0),
                            preferred_element_type=F32)
            n = s.shape[1] // 2
            suf += [s[:rows, :n], s[rows:, n:]]
            suf_keys.append(pair_keys)
        return pre, jnp.concatenate(suf, axis=0), suf_keys

    def finish(r, pre, suf, suf_keys):
        top = jnp.maximum(jnp.max(pre, axis=1, keepdims=True), jnp.max(suf, axis=1, keepdims=True))
        pre_w = jnp.exp2((pre - top) * (scale * LOG2E))
        suf_w = jnp.exp2((suf - top) * (scale * LOG2E))
        total = jnp.sum(pre_w, axis=1, keepdims=True) + jnp.sum(suf_w, axis=1, keepdims=True)
        pre_w, suf_w = pre_w.astype(BF), suf_w.astype(BF)
        acc = jnp.dot(pre_w, cl[r], preferred_element_type=F32)
        inv = 1.0 / total
        for j in range(0, BEAMS, 2):
            part = slice(j * rows, (j + 2) * rows)
            first, second = suf_w[j * rows:(j + 1) * rows], suf_w[(j + 1) * rows:(j + 2) * rows]
            none = jnp.zeros_like(first)
            spread_w = jnp.concatenate([jnp.concatenate([first, none], axis=1),
                                        jnp.concatenate([none, second], axis=1)], axis=0)
            a = acc[part] + jnp.dot(spread_w, suf_keys[j // 2], preferred_element_type=F32)
            pbuf[r, part] = (a * inv[part]).astype(BF)
        moved = jnp.dot(spread[...], pbuf[r], preferred_element_type=F32).astype(BF)
        lse = scale * top + jnp.log(total)
        lane_lse = jnp.sum(jnp.where(moves, lse, 0.0), axis=0, keepdims=True)
        for n, message in enumerate(messages):
            for zz in range(2):
                at = (2 * n + zz) * small
                to = (zz * REQ + r) * small
                message[to:to + small] = moved[at:at + small]
                lse_buf[n:n + 1, to:to + small] = lane_lse[:, at:at + small]

    now = scores(0)
    for r in range(REQ):
        later = scores(r + 1) if r + 1 < REQ else None
        finish(r, *now)
        now = later
    parts = stat_rows(lse_buf[...])
    for n, message in enumerate(messages):
        write_stat(message, body, [p[n:n + 1] for p in parts], stat)


def attend(scale, fetch, info, q_lat, q_rope, caches):
    heads, width = q_lat[0].shape[1:]
    total_rows = BEAMS * 2 * heads
    targets = SHAPE[1] * SHAPE[2]
    body = REQ * total_rows // (2 * targets)
    message = lambda n: jax.ShapeDtypeStruct((n, body + STAT, width), BF)
    keys = caches[0].shape[1] + caches[2].shape[1]
    own = [v.shape if fetch else (16, LANES) for v in (q_lat[0], q_rope[0])]
    first = [in_hbm(v) if fetch else v for v in (q_lat[0], q_rope[0])]
    spec = HBM if fetch else VMEM
    return pl.pallas_call(
        partial(attend_kernel, scale, fetch),
        in_specs=[SMEM, spec, VMEM, spec, VMEM] + [HBM] * 4,
        out_specs=[VMEM] * 3,
        out_shape=[message(targets), message(targets // 2), message(targets // 2)],
        scratch_shapes=[
            pltpu.VMEM((total_rows, total_rows), BF),
            pltpu.VMEM((REQ, total_rows, width), BF),
            pltpu.VMEM((REQ, total_rows, LANES), BF),
            pltpu.VMEM((REQ, total_rows, width), BF),
            pltpu.VMEM((2, *q_rope[0].shape), F32),
            pltpu.VMEM((2 * targets, body), F32),
            pltpu.VMEM((STAT, width), F32),
        ] + [pltpu.VMEM(c.shape, BF) for c in caches]
        + [pltpu.VMEM(shape, BF) for shape in own] + [pltpu.SemaphoreType.DMA((5, REQ))],
        compiler_params=pltpu.CompilerParams(vmem_limit_bytes=14 << 20),
        cost_estimate=pl.CostEstimate(
            flops=REQ * 2 * total_rows * keys * (2 * width + DR), bytes_accessed=8 << 20,
            transcendentals=REQ * total_rows * keys),
        name="attend",
    )(info, first[0], q_lat[1], first[1], q_rope[1], *(in_hbm(c) for c in caches))


def pair_kernel(count, a, *refs):
    got, outs, stat = refs[:count], refs[count:-1], refs[-1]
    targets, rows, _ = a.shape
    body = rows - STAT
    for t in range(targets):
        ours, theirs = a.at[t], got[t // (targets // count)].at[t % (targets // count)]
        out = outs[t // (targets // len(outs))].at[t % (targets // len(outs))]
        weights, lse = joined([read_stat(v[body:], body) for v in (ours, theirs)])
        out[:body] = (ours[:body].astype(F32) * column(weights[0])
                      + theirs[:body].astype(F32) * column(weights[1])).astype(BF)
        write_stat(out, body, stat_rows(lse), stat)


def merge_pairs(a, got, parts):
    return pl.pallas_call(
        partial(pair_kernel, len(got)),
        in_specs=[VMEM] * (1 + len(got)),
        out_specs=[VMEM] * parts,
        out_shape=[jax.ShapeDtypeStruct((a.shape[0] // parts, *a.shape[1:]), BF)] * parts,
        scratch_shapes=[pltpu.VMEM((STAT, a.shape[2]), F32)],
        compiler_params=pltpu.CompilerParams(vmem_limit_bytes=4 << 20),
        cost_estimate=pl.CostEstimate(flops=4 * a.size, bytes_accessed=6 * a.size, transcendentals=0),
        name="merge_pairs",
    )(a, *got)


def plane_kernel(count, *refs):
    groups = refs[:count], refs[count:2 * count]
    outs, (stat, held) = refs[2 * count:-2], refs[-2:]
    body = refs[0].shape[1] - STAT
    small = body // 2
    _, y, _, _, z1 = bits(lax.axis_index(AXES))
    for other, sources in enumerate(groups):
        weights, lse = joined([read_stat(ref[0, body:], body) for ref in sources])
        parts = stat_rows(lse)
        columns = [column(w) for w in weights]
        for z0 in range(2):
            part = slice(z0 * small, (z0 + 1) * small)
            total = None
            for ref, w in zip(sources, columns):
                term = ref[0, part].astype(F32) * w[part]
                total = term if total is None else total + term
            held[2 * other + z0, :small] = total.astype(BF)
            write_stat(held.at[2 * other + z0], small, [p[:, part] for p in parts], stat)
    for d, out in enumerate(outs):
        out[...] = held[2 * ((d >> 1) ^ y ^ z1) + (d & 1)]


def merge_plane(same, other):
    _, rows, width = same[0].shape
    shape = ((rows - STAT) // 2 + STAT, width)
    return pl.pallas_call(
        partial(plane_kernel, len(same)),
        in_specs=[VMEM] * 2 * len(same),
        out_specs=[VMEM] * SHAPE[0],
        out_shape=[jax.ShapeDtypeStruct(shape, BF)] * SHAPE[0],
        scratch_shapes=[pltpu.VMEM((STAT, width), F32), pltpu.VMEM((SHAPE[0], *shape), BF)],
        compiler_params=pltpu.CompilerParams(vmem_limit_bytes=4 << 20),
        cost_estimate=pl.CostEstimate(flops=16 * rows * width, bytes_accessed=24 * rows * width, transcendentals=0),
        name="merge_plane",
    )(*same, *other)


def sum_kernel(count, *refs):
    ins, outs = refs[:count], refs[count:]
    for i, out in enumerate(outs):
        terms = [(ref[...] if len(outs) == 1 else ref[i]).astype(F32) for ref in ins]
        while len(terms) > 1:
            terms = [a + b for a, b in zip(terms[::2], terms[1::2])]
        out[...] = terms[0].astype(BF)


def sums(arrays, split):
    count, shape = len(arrays), arrays[0].shape
    outs = [shape[1:]] * shape[0] if split else [shape]
    return pl.pallas_call(
        partial(sum_kernel, count),
        in_specs=[VMEM] * count,
        out_specs=[VMEM] * len(outs),
        out_shape=[jax.ShapeDtypeStruct(out, BF) for out in outs],
        compiler_params=pltpu.CompilerParams(vmem_limit_bytes=4 << 20),
        cost_estimate=EXCHANGE,
        name="sums",
    )(*arrays)


def project_kernel(p0, p1, p2, p3, w_uv, w_o, keep, send):
    parts = (p0, p1, p2, p3)
    rows, _ = p0.shape
    body = rows - STAT
    weights, _ = joined([read_stat(p[body:], body) for p in parts])
    total = None
    for p, w in zip(parts, weights):
        term = p[:body].astype(F32) * column(w)
        total = term if total is None else total + term
    full = jnp.dot(total.astype(BF), w_uv[...], preferred_element_type=F32)
    rows, columns = full.shape
    row = lax.broadcasted_iota(jnp.int32, (rows, columns), 0)
    lane = lax.broadcasted_iota(jnp.int32, (rows, columns), 1)
    own = jnp.where((row & (HEADS_DEV - 1)) == lane // DV, full, 0.0).astype(BF)
    pick_hyp = lax.broadcasted_iota(jnp.int32, (HYPS, rows), 0)
    pick_row = lax.broadcasted_iota(jnp.int32, (HYPS, rows), 1)
    pick = jnp.where(pick_row // HEADS_DEV == pick_hyp, 1.0, 0.0).astype(BF)
    values = jnp.dot(pick, own, preferred_element_type=F32).astype(BF)
    width = keep.shape[2]
    plane = lax.axis_index(AXES) & 7
    for there, out in enumerate((keep, send)):
        for t in range(out.shape[0]):
            at = pl.multiple_of((plane ^ (2 * t + there)) * width, LANES)
            piece = jnp.dot(values, w_o[:, pl.ds(at, width)], preferred_element_type=F32)
            out[t] = piece.astype(BF)


def project(parts, w_uv, w_o):
    squares = SHAPE[1] * SHAPE[2]
    out = jax.ShapeDtypeStruct((squares, HYPS, w_o.shape[1] // (2 * squares)), BF)
    return pl.pallas_call(
        project_kernel,
        in_specs=[VMEM] * 6,
        out_specs=[VMEM] * 2,
        out_shape=[out] * 2,
        compiler_params=pltpu.CompilerParams(vmem_limit_bytes=4 << 20),
        cost_estimate=pl.CostEstimate(flops=2 * HYPS * w_o.size, bytes_accessed=2 * w_o.size, transcendentals=0),
        name="project",
    )(*parts, w_uv, w_o)


def core_sum_kernel(a, b, out):
    chip = lax.axis_index(AXES) >> 1
    square, depth = chip & 3, chip >> 2
    for t in range(a.shape[0]):
        for z in range(a.shape[1]):
            out[(depth ^ z) * a.shape[0] + (square ^ t)] = (a[t, z].astype(F32) + b[t, z].astype(F32)).astype(BF)


def core_sum(a, b):
    squares, depth, *tail = a.shape
    return pl.pallas_call(
        core_sum_kernel,
        in_specs=[VMEM] * 2,
        out_specs=VMEM,
        out_shape=jax.ShapeDtypeStruct((squares * depth, *tail), BF),
        compiler_params=pltpu.CompilerParams(vmem_limit_bytes=4 << 20),
        cost_estimate=EXCHANGE,
        name="core_sum",
    )(a, b)


def load_kernel(count, *refs):
    sources, dests, sems = refs[:count], refs[count + 1:-1], refs[-1]
    copies = [pltpu.make_async_copy(sources[i], dests[i], sems.at[i]) for i in range(count)]
    for copy in copies:
        copy.start()
    for copy in copies:
        copy.wait()


def load(after, *arrays):
    count = len(arrays)
    return pl.pallas_call(
        partial(load_kernel, count),
        in_specs=[HBM] * count + [pl.BlockSpec(memory_space=pl.ANY)],
        out_specs=[VMEM] * count,
        out_shape=[pltpu.VMEM(a.shape, a.dtype) for a in arrays],
        scratch_shapes=[pltpu.SemaphoreType.DMA((count,))],
        compiler_params=pltpu.CompilerParams(vmem_limit_bytes=1 << 20),
        cost_estimate=pl.CostEstimate(
            flops=0, bytes_accessed=sum(2 * a.size for a in arrays), transcendentals=0),
        name="load",
    )(*(in_hbm(a) for a in arrays), after)


def experts_kernel(*refs):
    shares, (hidden, gain, ids, gates, w_gate, w_up, down_hbm) = refs[:8], refs[8:15]
    attended, keep, send, residual, x_buf, acc, x_held, w_down, sems = refs[15:]
    units = w_gate.shape[0]
    chunks = units // UNITS
    parts = [slice(k * UNITS, (k + 1) * UNITS) for k in range(chunks)]
    downs = [pltpu.make_async_copy(down_hbm.at[pl.ds(k * UNITS, UNITS)], w_down.at[pl.ds(k * UNITS, UNITS)],
                                   sems.at[k]) for k in range(chunks)]
    for copy in downs:
        copy.start()
    linear = lax.axis_index(AXES)
    plane, depth = linear & 7, linear >> 3
    share = shares[0].shape[1]
    for d, ref in enumerate(shares):
        at = pl.multiple_of((plane ^ d) * share, LANES)
        x_buf[:, pl.ds(at, share)] = ref[...].astype(F32)
        attended[:, pl.ds(at, share)] = ref[...]
    x = x_buf[...] + hidden[...].astype(F32)
    mean_square = jnp.mean(x * x, axis=1, keepdims=True)
    normed = (x * lax.rsqrt(mean_square + 1e-06) * gain[...]).astype(BF)
    expert = linear * units // EFF
    routed = column(jnp.sum(jnp.where(ids[...] == expert, gates[...], 0.0), axis=0, keepdims=True))
    count, _, width = x_held.shape
    for d in range(count):
        x_held[d] = x[:, d * width:(d + 1) * width]
    residual[...] = x_held[linear]
    gate = [lax.dot_general(normed, w_gate[part], NT, preferred_element_type=F32) for part in parts]
    gate = [g / (1.0 + jnp.exp(-g)) * routed for g in gate]
    act = []
    for k, part in enumerate(parts):
        up = lax.dot_general(normed, w_up[part], NT, preferred_element_type=F32)
        act.append((gate[k] * up).astype(BF))
    for k, part in enumerate(parts):
        downs[k].wait()
        term = jnp.dot(act[k], w_down[part], preferred_element_type=F32)
        if k == 0:
            acc[...] = term
        else:
            acc[...] += term
    core = linear & CORE
    for d in range(0, count, 2):
        pair = [acc[:, (d + i) * width:(d + i + 1) * width].astype(BF) for i in range(2)]
        at = ((d >> 1) ^ (linear >> 1)) & 3, depth ^ (d >> 3)
        keep[at] = jnp.where(core == 1, pair[1], pair[0])
        send[at] = jnp.where(core == 1, pair[0], pair[1])


def experts(shares, hidden, gain, ids, gates, w_gate, w_up, w_down):
    units, width = w_gate.shape
    count = math.prod(SHAPE)
    small = width // count
    terms = jax.ShapeDtypeStruct((SHAPE[1] * SHAPE[2], SHAPE[0], HYPS, small), BF)
    return pl.pallas_call(
        experts_kernel,
        in_specs=[VMEM] * 14 + [HBM],
        out_specs=[VMEM] * 4,
        out_shape=[
            jax.ShapeDtypeStruct((HYPS, width), BF), terms, terms,
            jax.ShapeDtypeStruct((HYPS, small), F32),
        ],
        scratch_shapes=[pltpu.VMEM((HYPS, width), F32)] * 2 + [
            pltpu.VMEM((count, HYPS, small), F32),
            pltpu.VMEM((units, width), BF),
            pltpu.SemaphoreType.DMA((units // UNITS,)),
        ],
        compiler_params=pltpu.CompilerParams(vmem_limit_bytes=18 << 20),
        cost_estimate=pl.CostEstimate(flops=6 * HYPS * units * width, bytes_accessed=6 * units * width,
                                      transcendentals=HYPS * units),
        name="experts",
    )(*shares, hidden, gain, ids, gates, w_gate, w_up, in_hbm(w_down))


def local(
    query_latent,
    query_rope,
    cache_latent,
    cache_rope,
    suffix_latent,
    suffix_rope,
    lengths,
    parents,
    w_uv,
    w_o,
    hidden,
    norm_gain,
    w_gate,
    w_up,
    w_down,
    expert_ids,
    gate_weights,
):
    scale = MSCALE * MSCALE / math.sqrt(DN + DR)
    info = jnp.concatenate([lengths, parents])
    caches = (cache_latent, cache_rope, suffix_latent, suffix_rope)
    tied = lax.optimization_barrier
    square, line = (Y, X, X ^ Y), (Z0 ^ Z1, Z1, Z0)

    near_lat, near_rope = swap(query_latent, CORE), swap(query_rope, CORE)
    far_lat, far_rope = swap(query_latent, Y), swap(query_rope, Y)
    keep, *send = attend(scale, True, info, (query_latent, near_lat), (query_rope, near_rope), caches)
    near = merge_pairs(keep, [swap(v, CORE) for v in send], 2)
    far_lat, far_rope, near = tied((far_lat, far_rope, near))
    near_x = swap(near[1], X)
    far_lat, far_rope = (far_lat, swap(far_lat, CORE)), (far_rope, swap(far_rope, CORE))
    keep, *send = attend(scale, False, info, far_lat, far_rope, caches)
    keep, send, near_x = tied((keep, send, near_x))
    near = merge_pairs(near[0], [near_x], 2)
    near_y = swap(near[1], Y)
    far = merge_pairs(keep, [swap(v, CORE) for v in send], len(square) + 1)
    far_xy, far_x, far_y = swap(far[3], X ^ Y), swap(far[2], X), swap(far[1], Y)
    parts = merge_plane((near[0], far_y, far_xy), (near_y, far[0], far_x))
    w_uv, w_o = load(parts[0], w_uv, w_o)
    parts = [parts[0], *(swap(v, mask) for v, mask in zip(parts[:0:-1], line))]
    keep, send = project(parts, w_uv, w_o)

    pieces = sums([keep, swap(send, CORE)], True)
    share, = sums([pieces[0], *(swap(v, mask) for v, mask in zip(pieces[:0:-1], square[::-1]))], False)
    share, = sums([share, *(swap(share, mask) for mask in line[::-1])], False)
    shares = [share, *(swap(share, mask) for mask in square)]
    shares = [v for pair in zip(shares, [swap(v, CORE) for v in shares]) for v in pair]
    attended, keep, send, residual = experts(
        shares, hidden, norm_gain.reshape(1, -1), expert_ids.T, gate_weights.T, w_gate, w_up, w_down)

    total = core_sum(keep, swap(send, CORE))
    total = lax.all_to_all(total, AXES[:3], split_axis=0, concat_axis=0, tiled=True)
    updated = (residual + jnp.sum(total.astype(F32), axis=0)).astype(BF)
    return (attended, updated)


def solution(mesh):
    if mesh.shape["ctx"] == SHAPE[0] * SHAPE[1] and mesh.shape["hx"] == SHAPE[2] * SHAPE[3]:
        chosen, names = local, AXES
        mesh = jax.sharding.Mesh(mesh.devices.reshape(SHAPE), AXES)
    else:
        chosen, names = general_local, ("ctx", "hx")
    all_axes, hx = names, names[len(names) // 2:]
    in_specs = (
        P(None, hx, None),
        P(None, hx),
        P(None, all_axes, None),
        P(None, None, all_axes),
        P(None, all_axes, None),
        P(None, None, all_axes),
        P(),
        P(),
        P(None, all_axes),
        P(all_axes, None),
        P(),
        P(),
        P(all_axes, None),
        P(all_axes, None),
        P(all_axes, None),
        P(),
        P(),
    )
    out_specs = (P(), P(None, all_axes))
    return jax.shard_map(chosen, mesh=mesh, in_specs=in_specs, out_specs=out_specs, check_vma=False)
```

```python
from functools import partial
import math

import jax
import jax.numpy as jnp
from jax import lax
from jax.experimental import pallas as pl
from jax.experimental.pallas import tpu as pltpu
from jax.sharding import PartitionSpec as P

DL = 512
DR = 64
DN = 128
DV = 128
EFF = 2048
REQ = 4
BEAMS = 4
HYPS = 16


MSCALE = 1.0 + 0.1 * math.log(40.0)
NEG = -1e30


def merged(value, axis, join):
    pieces = jax.tree.map(lambda part: lax.all_gather(part, axis), value)
    head = jax.tree.map(lambda part: part[0], pieces)
    tail = jax.tree.map(lambda part: part[1:], pieces)
    subtotal, _ = lax.scan(lambda subtotal, section: (join(subtotal, section), None), head, tail)
    return subtotal


def merge_pair(first_set, second_set):
    max_a, sum_a, acc_a = first_set
    max_b, sum_b, acc_b = second_set
    new_max = jnp.maximum(max_a, max_b)
    factor_a = jnp.exp(max_a - new_max)
    factor_b = jnp.exp(max_b - new_max)
    return (
        new_max,
        sum_a * factor_a + sum_b * factor_b,
        acc_a * factor_a[..., None] + acc_b * factor_b[..., None],
    )


def request_stats(
    q_lat, q_rope, pre_lat, pre_rope, suf_lat, suf_rope, is_live, softmax_scale, with_prefix
):
    suf_scores = jnp.einsum("bhl,bsl->bhs", q_lat, suf_lat, preferred_element_type=jnp.float32)
    suf_scores = (
        suf_scores
        + jnp.einsum("bhr,brs->bhs", q_rope, suf_rope, preferred_element_type=jnp.float32)
    ) * softmax_scale
    row_max = jnp.max(suf_scores, axis=2)
    beam_count, head_count, lat_width = q_lat.shape
    flat_lat = q_lat.reshape(beam_count * head_count, lat_width)
    flat_rope = q_rope.reshape(beam_count * head_count, q_rope.shape[2])
    pre_scores = lax.dot_general(
        flat_lat, pre_lat, (((1,), (1,)), ((), ())), preferred_element_type=jnp.float32
    )
    pre_scores = pre_scores + jnp.dot(flat_rope, pre_rope, preferred_element_type=jnp.float32)
    pre_scores = jnp.where(is_live[None, :], pre_scores * softmax_scale, NEG).reshape(
        beam_count, head_count, -1
    )
    row_max = jnp.maximum(row_max, jnp.max(pre_scores, axis=2))
    suf_weights = jnp.exp(suf_scores - row_max[..., None]).astype(jnp.bfloat16)
    weight_sum = jnp.sum(suf_weights.astype(jnp.float32), axis=2)
    weighted = jnp.einsum("bhs,bsl->bhl", suf_weights, suf_lat, preferred_element_type=jnp.float32)
    pre_weights = jnp.exp(pre_scores - row_max[..., None]).astype(jnp.bfloat16)
    weight_sum = weight_sum + jnp.sum(pre_weights.astype(jnp.float32), axis=2)
    prefix_part = jnp.dot(
        pre_weights.reshape(beam_count * head_count, -1),
        pre_lat,
        preferred_element_type=jnp.float32,
    )
    weighted = weighted + prefix_part.reshape(beam_count, head_count, lat_width)
    return (row_max, weight_sum, weighted)


def general_local(
    query_latent,
    query_rope,
    cache_latent,
    cache_rope,
    suffix_latent,
    suffix_rope,
    lengths,
    parents,
    w_uv,
    w_o,
    hidden,
    norm_gain,
    w_gate,
    w_up,
    w_down,
    expert_ids,
    gate_weights,
):
    q_lat, q_rope = (
        lax.all_gather(query_latent, "hx", axis=1, tiled=True),
        lax.all_gather(query_rope, "hx", axis=1, tiled=True),
    )
    head_count = q_lat.shape[1]
    q_rope = q_rope.reshape(HYPS, head_count, DR)
    softmax_scale = MSCALE * MSCALE / math.sqrt(DN + DR)
    n_hx = lax.axis_size("hx")
    linear = lax.axis_index("ctx") * n_hx + lax.axis_index("hx")
    ctx_block = cache_latent.shape[1]
    offsets = linear * ctx_block + jnp.arange(ctx_block, dtype=jnp.int32)
    suf_lat = jnp.take(suffix_latent, parents, axis=0)
    suf_rope = jnp.take(suffix_rope, parents, axis=0)
    maxima = []
    totals_list = []
    sums_list = []
    for request in range(REQ):
        hyp_rows = slice(request * BEAMS, (request + 1) * BEAMS)
        is_live = offsets < lengths[request]
        bound_stats = partial(
            request_stats,
            q_lat[hyp_rows],
            q_rope[hyp_rows],
            cache_latent[request],
            cache_rope[request],
            suf_lat[hyp_rows],
            suf_rope[hyp_rows],
            is_live,
            softmax_scale,
        )
        request_sums = bound_stats(True)
        maxima.append(request_sums[0])
        totals_list.append(request_sums[1])
        sums_list.append(request_sums[2])
    row_max = jnp.concatenate(maxima, axis=0)
    weight_sum = jnp.concatenate(totals_list, axis=0)
    weighted = jnp.concatenate(sums_list, axis=0)
    part_max, part_sum, part_acc = (
        lax.all_to_all(row_max[None], "ctx", split_axis=2, concat_axis=0, tiled=True),
        lax.all_to_all(weight_sum[None], "ctx", split_axis=2, concat_axis=0, tiled=True),
        lax.all_to_all(weighted[None], "ctx", split_axis=2, concat_axis=0, tiled=True),
    )
    group_max = jnp.max(part_max, axis=0)
    factor = jnp.exp(part_max - group_max[None])
    group_sum = jnp.sum(part_sum * factor, axis=0)
    group_acc = jnp.sum(part_acc * factor[..., None], axis=0)
    group_max, group_sum, group_acc = merged((group_max, group_sum, group_acc), "hx", merge_pair)
    attention = (group_acc / group_sum[..., None]).astype(jnp.bfloat16)
    columns = w_uv.shape[1]
    head_span = max(1, columns // DV)
    first_head = lax.axis_index("hx") * columns // DV
    chosen = lax.dynamic_slice_in_dim(attention, first_head, head_span, 1)
    value_map = w_uv.reshape(DL, head_span, columns // head_span)
    values = jnp.einsum("bnl,lnc->bnc", chosen, value_map, preferred_element_type=jnp.float32)
    values = values.astype(jnp.bfloat16).reshape(HYPS, columns)
    partial_out = jnp.dot(values, w_o, preferred_element_type=jnp.float32)
    attended = lax.psum(partial_out, ("ctx", "hx")).astype(jnp.bfloat16)
    residual = hidden.astype(jnp.float32) + attended.astype(jnp.float32)
    mean_square = jnp.mean(residual * residual, axis=1, keepdims=True)
    normed = (residual * lax.rsqrt(mean_square + 1e-06) * norm_gain).astype(jnp.bfloat16)
    unit_count = w_gate.shape[0]
    expert_here = linear * unit_count // EFF
    routed = jnp.sum(gate_weights * (expert_ids == expert_here).astype(jnp.float32), axis=1)
    gate_out = lax.dot_general(
        normed, w_gate, (((1,), (1,)), ((), ())), preferred_element_type=jnp.float32
    )
    up_out = lax.dot_general(
        normed, w_up, (((1,), (1,)), ((), ())), preferred_element_type=jnp.float32
    )
    activated = (jax.nn.silu(gate_out) * up_out * routed[:, None]).astype(jnp.bfloat16)
    expert_terms = jnp.dot(activated, w_down, preferred_element_type=jnp.float32)
    moe_share = lax.psum_scatter(expert_terms, ("ctx", "hx"), scatter_dimension=1, tiled=True)
    share_width = moe_share.shape[1]
    residual_share = lax.dynamic_slice_in_dim(residual, linear * share_width, share_width, 1)
    updated = (residual_share + moe_share).astype(jnp.bfloat16)
    return (attended, updated)


BF = jnp.bfloat16
F32 = jnp.float32
AXES = ("z", "x", "y", "core")
SHAPE = (4, 2, 2, 2)
CORE, Y, X, Z0, Z1 = 1, 2, 4, 8, 16
HEADS_DEV = 4
UNITS = 256
DOT_UNITS = 128
STAT = 8
LANES = 128
PARENTS = REQ
AHEAD = 2
LOG2E = math.log2(math.e)
VMEM = pl.BlockSpec(memory_space=pltpu.VMEM)
SMEM = pl.BlockSpec(memory_space=pltpu.SMEM)
HBM = pl.BlockSpec(memory_space=pltpu.HBM)
NT = (((1,), (1,)), ((), ()))
EXCHANGE = pl.CostEstimate(flops=0, bytes_accessed=12 << 20, transcendentals=0)


def swap(value, mask):
    return lax.ppermute(value, AXES, [(i, i ^ mask) for i in range(math.prod(SHAPE))])


def in_hbm(value):
    return pltpu.with_memory_space_constraint(value, pltpu.HBM)


def bits(linear):
    return [linear >> k & 1 for k in range(5)]


def column(lane_row):
    n = lane_row.shape[1]
    at = lax.broadcasted_iota(jnp.int32, (n, n), 0)
    to = lax.broadcasted_iota(jnp.int32, (n, n), 1)
    return jnp.sum(jnp.where(at == to, lane_row, 0.0), axis=1, keepdims=True)


def stat_rows(lse):
    parts = []
    for _ in range(3):
        part = lse.astype(BF).astype(F32)
        parts.append(part)
        lse = lse - part
    return parts


def write_stat(out, body, parts, stat):
    stat[...] = jnp.zeros_like(stat)
    for i, part in enumerate(parts):
        stat[0:1, i * LANES:i * LANES + part.shape[1]] = part
    out[body:] = stat[...].astype(BF)


def read_stat(block, n):
    block = block.astype(F32)
    return (block[:1, :n] + block[:1, LANES:LANES + n]) + block[:1, 2 * LANES:2 * LANES + n]


def joined(lses):
    top = lses[0]
    for lse in lses[1:]:
        top = jnp.maximum(top, lse)
    weights = [jnp.exp(lse - top) for lse in lses]
    total = sum(weights[1:], weights[0])
    return [w / total for w in weights], top + jnp.log(total)


def attend_kernel(scale, fetch, info, ql0, ql1, qr0, qr1, cl_hbm, cr_hbm, sl_hbm, sr_hbm, keep, send0, send1,
                  spread, qbuf, rbuf, pbuf, wide, lse_buf, stat, cl, cr, sl, sr, own_q, own_r, sems):
    linear = lax.axis_index(AXES)
    core, y, x, z0, _ = bits(linear)
    heads = ql1.shape[1]
    rows = 2 * heads
    total_rows = BEAMS * rows
    targets = keep.shape[0]
    body = keep.shape[1] - STAT
    small = body // (2 * REQ)
    query_copies = []
    if fetch:
        query_copies = [pltpu.make_async_copy(qr0, own_r, sems.at[4, 0]),
                        pltpu.make_async_copy(ql0, own_q, sems.at[4, 1])]
        for copy in query_copies:
            copy.start()
    copies = []
    for r in range(REQ):
        beams = pl.ds(r * BEAMS, BEAMS)
        group = [
            pltpu.make_async_copy(cl_hbm.at[r], cl.at[r], sems.at[0, r]),
            pltpu.make_async_copy(cr_hbm.at[r], cr.at[r], sems.at[1, r]),
            pltpu.make_async_copy(sl_hbm.at[beams], sl.at[beams], sems.at[2, r]),
            pltpu.make_async_copy(sr_hbm.at[beams], sr.at[beams], sems.at[3, r]),
        ]
        copies.append(group)
        if r < AHEAD:
            for copy in group:
                copy.start()
    first_q, first_r = (own_q, own_r) if fetch else (ql0, qr0)

    down = lax.broadcasted_iota(jnp.int32, (total_rows, 1), 0)
    along = lax.broadcasted_iota(jnp.int32, (1, total_rows), 1)

    def source_of(row):
        bit = lambda k: (row >> k) & 1
        beam, head = (row >> 2) & 3, row & 3
        target = (bit(6) ^ x) * 4 + (bit(5) ^ y) * 2 + (bit(7) ^ core)
        return beam * rows + (bit(4) ^ core ^ z0) * heads + target * HEADS_DEV + head

    spread[...] = jnp.where(source_of(down) == along, 1.0, 0.0).astype(BF)
    moves = source_of(along) == down
    messages = [keep.at[t] for t in range(targets)]
    messages += [send.at[t] for send in (send0, send1) for t in range(targets // 2)]
    lse_buf[...] = jnp.zeros_like(lse_buf)
    for copy in query_copies:
        copy.wait()
    wide[0] = first_r[...].astype(F32)
    wide[1] = qr1[...].astype(F32)
    per_group = LANES // DR
    block = 8
    row8 = lax.broadcasted_iota(jnp.int32, (block, LANES), 0)
    own_lanes = lax.broadcasted_iota(jnp.int32, (block, LANES), 1) // DR == row8 % per_group
    for r in range(REQ):
        for j in range(BEAMS):
            for piece, q in enumerate((first_q, ql1)):
                part = slice(j * rows + piece * heads, j * rows + (piece + 1) * heads)
                b = r * BEAMS + j
                qbuf[r, part] = q[b]
                unfolded = []
                for top in range(0, heads, block):
                    rows8 = jnp.zeros((block, LANES), F32)
                    for g in range(block // per_group):
                        at = (top // per_group + g) * LANES
                        rows8 = jnp.where(row8 // per_group == g, wide[piece, b:b + 1, at:at + LANES], rows8)
                    unfolded.append(jnp.where(own_lanes, rows8, 0.0))
                rbuf[r, part] = jnp.concatenate(unfolded, axis=0).astype(BF)

    def scores(r):
        for copy in copies[r]:
            copy.wait()
        if r + AHEAD < REQ:
            for copy in copies[r + AHEAD]:
                copy.start()
        keys = cl[r]
        ctx_block = keys.shape[0]
        pre = lax.dot_general(qbuf[r], keys, NT, preferred_element_type=F32)
        pre = pre + jnp.dot(rbuf[r], jnp.concatenate([cr[r]] * per_group, axis=0), preferred_element_type=F32)
        position = linear * ctx_block + lax.broadcasted_iota(jnp.int32, (1, ctx_block), 1)
        pre = jnp.where(position < info[r], pre, NEG)
        own = [info[PARENTS + r * BEAMS + j] for j in range(BEAMS)]
        suf = []
        suf_keys = []
        for j in range(0, BEAMS, 2):
            part = slice(j * rows, (j + 2) * rows)
            pair_keys = jnp.concatenate([sl[own[j]], sl[own[j + 1]]], axis=0)
            pair_rope = jnp.concatenate([sr[own[j]], sr[own[j + 1]]], axis=1)
            s = lax.dot_general(qbuf[r, part], pair_keys, NT, preferred_element_type=F32)
            s = s + jnp.dot(rbuf[r, part], jnp.concatenate([pair_rope] * per_group, axis=0),
                            preferred_element_type=F32)
            n = s.shape[1] // 2
            suf += [s[:rows, :n], s[rows:, n:]]
            suf_keys.append(pair_keys)
        return pre, jnp.concatenate(suf, axis=0), suf_keys

    def finish(r, pre, suf, suf_keys):
        top = jnp.maximum(jnp.max(pre, axis=1, keepdims=True), jnp.max(suf, axis=1, keepdims=True))
        pre_w = jnp.exp2((pre - top) * (scale * LOG2E))
        suf_w = jnp.exp2((suf - top) * (scale * LOG2E))
        total = jnp.sum(pre_w, axis=1, keepdims=True) + jnp.sum(suf_w, axis=1, keepdims=True)
        pre_w, suf_w = pre_w.astype(BF), suf_w.astype(BF)
        acc = jnp.dot(pre_w, cl[r], preferred_element_type=F32)
        inv = 1.0 / total
        for j in range(0, BEAMS, 2):
            part = slice(j * rows, (j + 2) * rows)
            first, second = suf_w[j * rows:(j + 1) * rows], suf_w[(j + 1) * rows:(j + 2) * rows]
            none = jnp.zeros_like(first)
            spread_w = jnp.concatenate([jnp.concatenate([first, none], axis=1),
                                        jnp.concatenate([none, second], axis=1)], axis=0)
            a = acc[part] + jnp.dot(spread_w, suf_keys[j // 2], preferred_element_type=F32)
            pbuf[r, part] = (a * inv[part]).astype(BF)
        moved = jnp.dot(spread[...], pbuf[r], preferred_element_type=F32).astype(BF)
        lse = scale * top + jnp.log(total)
        lane_lse = jnp.sum(jnp.where(moves, lse, 0.0), axis=0, keepdims=True)
        for n, message in enumerate(messages):
            for zz in range(2):
                at = (2 * n + zz) * small
                to = (zz * REQ + r) * small
                message[to:to + small] = moved[at:at + small]
                lse_buf[n:n + 1, to:to + small] = lane_lse[:, at:at + small]

    now = scores(0)
    for r in range(REQ):
        later = scores(r + 1) if r + 1 < REQ else None
        finish(r, *now)
        now = later
    parts = stat_rows(lse_buf[...])
    for n, message in enumerate(messages):
        write_stat(message, body, [p[n:n + 1] for p in parts], stat)


def attend(scale, fetch, info, q_lat, q_rope, caches):
    heads, width = q_lat[0].shape[1:]
    total_rows = BEAMS * 2 * heads
    targets = SHAPE[1] * SHAPE[2]
    body = REQ * total_rows // (2 * targets)
    message = lambda n: jax.ShapeDtypeStruct((n, body + STAT, width), BF)
    keys = caches[0].shape[1] + caches[2].shape[1]
    own = [v.shape if fetch else (16, LANES) for v in (q_lat[0], q_rope[0])]
    first = [in_hbm(v) if fetch else v for v in (q_lat[0], q_rope[0])]
    spec = HBM if fetch else VMEM
    return pl.pallas_call(
        partial(attend_kernel, scale, fetch),
        in_specs=[SMEM, spec, VMEM, spec, VMEM] + [HBM] * 4,
        out_specs=[VMEM] * 3,
        out_shape=[message(targets), message(targets // 2), message(targets // 2)],
        scratch_shapes=[
            pltpu.VMEM((total_rows, total_rows), BF),
            pltpu.VMEM((REQ, total_rows, width), BF),
            pltpu.VMEM((REQ, total_rows, LANES), BF),
            pltpu.VMEM((REQ, total_rows, width), BF),
            pltpu.VMEM((2, *q_rope[0].shape), F32),
            pltpu.VMEM((2 * targets, body), F32),
            pltpu.VMEM((STAT, width), F32),
        ] + [pltpu.VMEM(c.shape, BF) for c in caches]
        + [pltpu.VMEM(shape, BF) for shape in own] + [pltpu.SemaphoreType.DMA((5, REQ))],
        compiler_params=pltpu.CompilerParams(vmem_limit_bytes=14 << 20),
        cost_estimate=pl.CostEstimate(
            flops=REQ * 2 * total_rows * keys * (2 * width + DR), bytes_accessed=8 << 20,
            transcendentals=REQ * total_rows * keys),
        name="attend",
    )(info, first[0], q_lat[1], first[1], q_rope[1], *(in_hbm(c) for c in caches))


def pair_kernel(count, a, *refs):
    got, outs, stat = refs[:count], refs[count:-1], refs[-1]
    targets, rows, _ = a.shape
    body = rows - STAT
    for t in range(targets):
        ours, theirs = a.at[t], got[t // (targets // count)].at[t % (targets // count)]
        out = outs[t // (targets // len(outs))].at[t % (targets // len(outs))]
        weights, lse = joined([read_stat(v[body:], body) for v in (ours, theirs)])
        out[:body] = (ours[:body].astype(F32) * column(weights[0])
                      + theirs[:body].astype(F32) * column(weights[1])).astype(BF)
        write_stat(out, body, stat_rows(lse), stat)


def merge_pairs(a, got, parts):
    return pl.pallas_call(
        partial(pair_kernel, len(got)),
        in_specs=[VMEM] * (1 + len(got)),
        out_specs=[VMEM] * parts,
        out_shape=[jax.ShapeDtypeStruct((a.shape[0] // parts, *a.shape[1:]), BF)] * parts,
        scratch_shapes=[pltpu.VMEM((STAT, a.shape[2]), F32)],
        compiler_params=pltpu.CompilerParams(vmem_limit_bytes=4 << 20),
        cost_estimate=pl.CostEstimate(flops=4 * a.size, bytes_accessed=6 * a.size, transcendentals=0),
        name="merge_pairs",
    )(a, *got)


def plane_kernel(count, *refs):
    groups = refs[:count], refs[count:2 * count]
    outs, (stat, held) = refs[2 * count:-2], refs[-2:]
    body = refs[0].shape[1] - STAT
    small = body // 2
    _, y, _, _, z1 = bits(lax.axis_index(AXES))
    for other, sources in enumerate(groups):
        weights, lse = joined([read_stat(ref[0, body:], body) for ref in sources])
        parts = stat_rows(lse)
        columns = [column(w) for w in weights]
        for z0 in range(2):
            part = slice(z0 * small, (z0 + 1) * small)
            total = None
            for ref, w in zip(sources, columns):
                term = ref[0, part].astype(F32) * w[part]
                total = term if total is None else total + term
            held[2 * other + z0, :small] = total.astype(BF)
            write_stat(held.at[2 * other + z0], small, [p[:, part] for p in parts], stat)
    for d, out in enumerate(outs):
        out[...] = held[2 * ((d >> 1) ^ y ^ z1) + (d & 1)]


def merge_plane(same, other):
    _, rows, width = same[0].shape
    shape = ((rows - STAT) // 2 + STAT, width)
    return pl.pallas_call(
        partial(plane_kernel, len(same)),
        in_specs=[VMEM] * 2 * len(same),
        out_specs=[VMEM] * SHAPE[0],
        out_shape=[jax.ShapeDtypeStruct(shape, BF)] * SHAPE[0],
        scratch_shapes=[pltpu.VMEM((STAT, width), F32), pltpu.VMEM((SHAPE[0], *shape), BF)],
        compiler_params=pltpu.CompilerParams(vmem_limit_bytes=4 << 20),
        cost_estimate=pl.CostEstimate(flops=16 * rows * width, bytes_accessed=24 * rows * width, transcendentals=0),
        name="merge_plane",
    )(*same, *other)


def sum_kernel(count, *refs):
    ins, outs = refs[:count], refs[count:]
    for i, out in enumerate(outs):
        terms = [(ref[...] if len(outs) == 1 else ref[i]).astype(F32) for ref in ins]
        while len(terms) > 1:
            terms = [a + b for a, b in zip(terms[::2], terms[1::2])]
        out[...] = terms[0].astype(BF)


def sums(arrays, split):
    count, shape = len(arrays), arrays[0].shape
    outs = [shape[1:]] * shape[0] if split else [shape]
    return pl.pallas_call(
        partial(sum_kernel, count),
        in_specs=[VMEM] * count,
        out_specs=[VMEM] * len(outs),
        out_shape=[jax.ShapeDtypeStruct(out, BF) for out in outs],
        compiler_params=pltpu.CompilerParams(vmem_limit_bytes=4 << 20),
        cost_estimate=EXCHANGE,
        name="sums",
    )(*arrays)


def project_kernel(p0, p1, p2, p3, w_uv, w_o, keep, send):
    parts = (p0, p1, p2, p3)
    rows, _ = p0.shape
    body = rows - STAT
    weights, _ = joined([read_stat(p[body:], body) for p in parts])
    total = None
    for p, w in zip(parts, weights):
        term = p[:body].astype(F32) * column(w)
        total = term if total is None else total + term
    full = jnp.dot(total.astype(BF), w_uv[...], preferred_element_type=F32)
    rows, columns = full.shape
    row = lax.broadcasted_iota(jnp.int32, (rows, columns), 0)
    lane = lax.broadcasted_iota(jnp.int32, (rows, columns), 1)
    own = jnp.where((row & (HEADS_DEV - 1)) == lane // DV, full, 0.0).astype(BF)
    pick_hyp = lax.broadcasted_iota(jnp.int32, (HYPS, rows), 0)
    pick_row = lax.broadcasted_iota(jnp.int32, (HYPS, rows), 1)
    pick = jnp.where(pick_row // HEADS_DEV == pick_hyp, 1.0, 0.0).astype(BF)
    values = jnp.dot(pick, own, preferred_element_type=F32).astype(BF)
    width = keep.shape[2]
    plane = lax.axis_index(AXES) & 7
    for there, out in enumerate((keep, send)):
        for t in range(out.shape[0]):
            at = pl.multiple_of((plane ^ (2 * t + there)) * width, LANES)
            piece = jnp.dot(values, w_o[:, pl.ds(at, width)], preferred_element_type=F32)
            out[t] = piece.astype(BF)


def project(parts, w_uv, w_o):
    squares = SHAPE[1] * SHAPE[2]
    out = jax.ShapeDtypeStruct((squares, HYPS, w_o.shape[1] // (2 * squares)), BF)
    return pl.pallas_call(
        project_kernel,
        in_specs=[VMEM] * 6,
        out_specs=[VMEM] * 2,
        out_shape=[out] * 2,
        compiler_params=pltpu.CompilerParams(vmem_limit_bytes=4 << 20),
        cost_estimate=pl.CostEstimate(flops=2 * HYPS * w_o.size, bytes_accessed=2 * w_o.size, transcendentals=0),
        name="project",
    )(*parts, w_uv, w_o)


def core_sum_kernel(a, b, out):
    chip = lax.axis_index(AXES) >> 1
    square, depth = chip & 3, chip >> 2
    for t in range(a.shape[0]):
        for z in range(a.shape[1]):
            out[(depth ^ z) * a.shape[0] + (square ^ t)] = (a[t, z].astype(F32) + b[t, z].astype(F32)).astype(BF)


def core_sum(a, b):
    squares, depth, *tail = a.shape
    return pl.pallas_call(
        core_sum_kernel,
        in_specs=[VMEM] * 2,
        out_specs=VMEM,
        out_shape=jax.ShapeDtypeStruct((squares * depth, *tail), BF),
        compiler_params=pltpu.CompilerParams(vmem_limit_bytes=4 << 20),
        cost_estimate=EXCHANGE,
        name="core_sum",
    )(a, b)


def load_kernel(count, *refs):
    sources, dests, sems = refs[:count], refs[count + 1:-1], refs[-1]
    copies = [pltpu.make_async_copy(sources[i], dests[i], sems.at[i]) for i in range(count)]
    for copy in copies:
        copy.start()
    for copy in copies:
        copy.wait()


def load(after, *arrays):
    count = len(arrays)
    return pl.pallas_call(
        partial(load_kernel, count),
        in_specs=[HBM] * count + [pl.BlockSpec(memory_space=pl.ANY)],
        out_specs=[VMEM] * count,
        out_shape=[pltpu.VMEM(a.shape, a.dtype) for a in arrays],
        scratch_shapes=[pltpu.SemaphoreType.DMA((count,))],
        compiler_params=pltpu.CompilerParams(vmem_limit_bytes=1 << 20),
        cost_estimate=pl.CostEstimate(
            flops=0, bytes_accessed=sum(2 * a.size for a in arrays), transcendentals=0),
        name="load",
    )(*(in_hbm(a) for a in arrays), after)


def experts_kernel(*refs):
    shares, (hidden, gain, ids, gates, w_gate, w_up, down_hbm) = refs[:8], refs[8:15]
    attended, keep, send, residual, x_buf, acc, x_held, w_down, sems = refs[15:]
    units = w_gate.shape[0]
    chunks = units // UNITS
    parts = [slice(k * UNITS, (k + 1) * UNITS) for k in range(chunks)]
    downs = [pltpu.make_async_copy(down_hbm.at[pl.ds(k * UNITS, UNITS)], w_down.at[pl.ds(k * UNITS, UNITS)],
                                   sems.at[k]) for k in range(chunks)]
    for copy in downs:
        copy.start()
    linear = lax.axis_index(AXES)
    plane, depth = linear & 7, linear >> 3
    share = shares[0].shape[1]
    for d, ref in enumerate(shares):
        at = pl.multiple_of((plane ^ d) * share, LANES)
        x_buf[:, pl.ds(at, share)] = ref[...].astype(F32)
        attended[:, pl.ds(at, share)] = ref[...]
    x = x_buf[...] + hidden[...].astype(F32)
    mean_square = jnp.mean(x * x, axis=1, keepdims=True)
    normed = (x * lax.rsqrt(mean_square + 1e-06) * gain[...]).astype(BF)
    expert = linear * units // EFF
    routed = column(jnp.sum(jnp.where(ids[...] == expert, gates[...], 0.0), axis=0, keepdims=True))
    count, _, width = x_held.shape
    for d in range(count):
        x_held[d] = x[:, d * width:(d + 1) * width]
    residual[...] = x_held[linear]
    dots = [slice(u, u + DOT_UNITS) for u in range(0, units, DOT_UNITS)]
    gate = [lax.dot_general(normed, w_gate[part], NT, preferred_element_type=F32) for part in dots]
    gate = [g / (1.0 + jnp.exp(-g)) * routed for g in gate]
    act = []
    for g, part in zip(gate, dots):
        up = lax.dot_general(normed, w_up[part], NT, preferred_element_type=F32)
        act.append((g * up).astype(BF))
    act = jnp.concatenate(act, axis=1)
    for k, part in enumerate(parts):
        downs[k].wait()
        term = jnp.dot(act[:, part], w_down[part], preferred_element_type=F32)
        if k == 0:
            acc[...] = term
        else:
            acc[...] += term
    core = linear & CORE
    for d in range(0, count, 2):
        pair = [acc[:, (d + i) * width:(d + i + 1) * width].astype(BF) for i in range(2)]
        at = ((d >> 1) ^ (linear >> 1)) & 3, depth ^ (d >> 3)
        keep[at] = jnp.where(core == 1, pair[1], pair[0])
        send[at] = jnp.where(core == 1, pair[0], pair[1])


def experts(shares, hidden, gain, ids, gates, w_gate, w_up, w_down):
    units, width = w_gate.shape
    count = math.prod(SHAPE)
    small = width // count
    terms = jax.ShapeDtypeStruct((SHAPE[1] * SHAPE[2], SHAPE[0], HYPS, small), BF)
    return pl.pallas_call(
        experts_kernel,
        in_specs=[VMEM] * 14 + [HBM],
        out_specs=[VMEM] * 4,
        out_shape=[
            jax.ShapeDtypeStruct((HYPS, width), BF), terms, terms,
            jax.ShapeDtypeStruct((HYPS, small), F32),
        ],
        scratch_shapes=[pltpu.VMEM((HYPS, width), F32)] * 2 + [
            pltpu.VMEM((count, HYPS, small), F32),
            pltpu.VMEM((units, width), BF),
            pltpu.SemaphoreType.DMA((units // UNITS,)),
        ],
        compiler_params=pltpu.CompilerParams(vmem_limit_bytes=18 << 20),
        cost_estimate=pl.CostEstimate(flops=6 * HYPS * units * width, bytes_accessed=6 * units * width,
                                      transcendentals=HYPS * units),
        name="experts",
    )(*shares, hidden, gain, ids, gates, w_gate, w_up, in_hbm(w_down))


def local(
    query_latent,
    query_rope,
    cache_latent,
    cache_rope,
    suffix_latent,
    suffix_rope,
    lengths,
    parents,
    w_uv,
    w_o,
    hidden,
    norm_gain,
    w_gate,
    w_up,
    w_down,
    expert_ids,
    gate_weights,
):
    scale = MSCALE * MSCALE / math.sqrt(DN + DR)
    info = jnp.concatenate([lengths, parents])
    caches = (cache_latent, cache_rope, suffix_latent, suffix_rope)
    tied = lax.optimization_barrier
    square, line = (Y, X, X ^ Y), (Z0 ^ Z1, Z1, Z0)

    near_lat, near_rope = swap(query_latent, CORE), swap(query_rope, CORE)
    far_lat, far_rope = swap(query_latent, Y), swap(query_rope, Y)
    keep, *send = attend(scale, True, info, (query_latent, near_lat), (query_rope, near_rope), caches)
    near = merge_pairs(keep, [swap(v, CORE) for v in send], 2)
    far_lat, far_rope, near = tied((far_lat, far_rope, near))
    near_x = swap(near[1], X)
    far_lat, far_rope = (far_lat, swap(far_lat, CORE)), (far_rope, swap(far_rope, CORE))
    keep, *send = attend(scale, False, info, far_lat, far_rope, caches)
    keep, send, near_x = tied((keep, send, near_x))
    near = merge_pairs(near[0], [near_x], 2)
    near_y = swap(near[1], Y)
    far = merge_pairs(keep, [swap(v, CORE) for v in send], len(square) + 1)
    far_xy, far_x, far_y = swap(far[3], X ^ Y), swap(far[2], X), swap(far[1], Y)
    parts = merge_plane((near[0], far_y, far_xy), (near_y, far[0], far_x))
    w_uv, w_o = load(parts[0], w_uv, w_o)
    parts = [parts[0], *(swap(v, mask) for v, mask in zip(parts[:0:-1], line))]
    keep, send = project(parts, w_uv, w_o)

    pieces = sums([keep, swap(send, CORE)], True)
    share, = sums([pieces[0], *(swap(v, mask) for v, mask in zip(pieces[:0:-1], square[::-1]))], False)
    share, = sums([share, *(swap(share, mask) for mask in line[::-1])], False)
    shares = [share, *(swap(share, mask) for mask in square)]
    shares = [v for pair in zip(shares, [swap(v, CORE) for v in shares]) for v in pair]
    attended, keep, send, residual = experts(
        shares, hidden, norm_gain.reshape(1, -1), expert_ids.T, gate_weights.T, w_gate, w_up, w_down)

    total = core_sum(keep, swap(send, CORE))
    total = lax.all_to_all(total, AXES[:3], split_axis=0, concat_axis=0, tiled=True)
    updated = (residual + jnp.sum(total.astype(F32), axis=0)).astype(BF)
    return (attended, updated)


def solution(mesh):
    if mesh.shape["ctx"] == SHAPE[0] * SHAPE[1] and mesh.shape["hx"] == SHAPE[2] * SHAPE[3]:
        chosen, names = local, AXES
        mesh = jax.sharding.Mesh(mesh.devices.reshape(SHAPE), AXES)
    else:
        chosen, names = general_local, ("ctx", "hx")
    all_axes, hx = names, names[len(names) // 2:]
    in_specs = (
        P(None, hx, None),
        P(None, hx),
        P(None, all_axes, None),
        P(None, None, all_axes),
        P(None, all_axes, None),
        P(None, None, all_axes),
        P(),
        P(),
        P(None, all_axes),
        P(all_axes, None),
        P(),
        P(),
        P(all_axes, None),
        P(all_axes, None),
        P(all_axes, None),
        P(),
        P(),
    )
    out_specs = (P(), P(None, all_axes))
    return jax.shard_map(chosen, mesh=mesh, in_specs=in_specs, out_specs=out_specs, check_vma=False)
```
